32 devices in a mesh: dp: 8 (over z, x), seq: 4 (over y, core).
Axes of the slice: x: 2, y: 2, z: 4, core: 2. Of those that a mesh axis runs over, the one named last changes fastest.
Arguments:
- tokens: bfloat16 [16, 1024, 1024], P(None, 'seq', 'dp'), may hold values from -6 to 6
- cotangent: bfloat16 [16, 1024, 1024], P('dp', 'seq'), may hold values from -6 to 6
- seq_lengths: int32 [16, 4], replicated, may hold values from 0 to 1024, as said below
- deal_order: int32 [16], replicated, may hold values from 0 to 15, as said below
- in_gain: bfloat16 [1024], P('dp'), may hold values from 0.5 to 1.5
- in_proj: bfloat16 [1024, 4096], P('dp'), may hold values from -0.1875 to 0.1875
- dt_proj: bfloat16 [1024, 24], P('dp'), may hold values from -0.1875 to 0.1875
- dt_bias: float32 [24], replicated, may hold values from -7 to -3
- a_log: float32 [24], replicated, may hold values from 0 to 2.5
- d_skip: float32 [24], replicated, may hold values from 0.5 to 2
- ssm_out: bfloat16 [1536, 1024], P('dp'), may hold values from -0.15625 to 0.15625
- attn_out: bfloat16 [512, 1024], P('dp'), may hold values from -1 to 1
- ffn_gain: bfloat16 [1024], P('dp'), may hold values from 0.5 to 1.5
- gate_up: bfloat16 [1024, 4096], P('dp'), may hold values from -0.1875 to 0.1875
- down_proj: bfloat16 [2048, 1024], P('dp'), may hold values from -0.125 to 0.125
Outputs:
- output: bfloat16 [16, 1024, 1024], P('dp', 'seq')
- grad_tokens: bfloat16 [16, 1024, 1024], P(None, 'seq', 'dp')
- grad_in_gain: float32 [1024], P('dp')
- grad_in_proj: float32 [1024, 4096], P('dp')
- grad_dt_proj: float32 [1024, 24], P('dp')
- grad_dt_bias: float32 [24], replicated
- grad_a_log: float32 [24], replicated
- grad_d_skip: float32 [24], replicated
- grad_ssm_out: float32 [1536, 1024], P('dp')
- grad_attn_out: float32 [512, 1024], P('dp')
- grad_ffn_gain: float32 [1024], P('dp')
- grad_gate_up: float32 [1024, 4096], P('dp')
- grad_down_proj: float32 [2048, 1024], P('dp')
The draws below stay inside these ranges and needn't reach their ends.
Inputs may be any that keep to these rules, and one draw needn't show every extreme that they name: `seq_lengths`: row p lists the lengths of up to 4 sequences packed in order into given pack p; they sum to 1024; a zero is an unused entry; the first entry is at least 769, and some pack is one whole sequence. A permutation of the 16 packs; dealt slot j holds given pack deal_order[j]; the slots 2 * g to 2 * g + 1 belong to index g of dp.
All inputs are finite; a program needn't handle non-finite values.
Results may differ from the reference program's by a relative error of at most 0.018.
Values may be sent and summed in bfloat16 or wider, within the bound.
A program may use at most 256 MiB of HBM per device.

```python
import math
import jax
import jax.numpy as jnp
from jax import lax

D = 1024
FF = 2048
QUERY_HEADS = 8
KEY_VALUE_HEADS = 2
HEAD_WIDTH = 64
MH = 24
HP = 64
NS = 128
PACK_LEN = 1024
STRETCH = 256
QBLOCK = 512
PACKS = 16
DI = 1536
IN_COLS = 4096
N_SEQ = 4


def pack_lengths(key):
    key_whole, key_pick, key_first, key_low, key_high = jax.random.split(key, 5)
    whole_pack = jax.random.randint(key_whole, (PACKS,), 0, 2) == 1
    forced = jnp.arange(PACKS) == jax.random.randint(key_pick, (), 0, PACKS)
    whole_pack = whole_pack | forced
    drawn_first = jax.random.randint(key_first, (PACKS,), 3 * PACK_LEN // 4 + 1, PACK_LEN + 1)
    first_len = jnp.where(whole_pack, PACK_LEN, drawn_first)
    rest_len = PACK_LEN - first_len
    cut_one = jax.random.randint(key_low, (PACKS,), 0, rest_len + 1)
    cut_two = jax.random.randint(key_high, (PACKS,), 0, rest_len + 1)
    low_cut = jnp.minimum(cut_one, cut_two)
    high_cut = jnp.maximum(cut_one, cut_two)
    return jnp.stack([first_len, low_cut, high_cut - low_cut, rest_len - high_cut], axis=-1).astype(jnp.int32)


def draw_seq_lengths(key, part):
    return pack_lengths(key)


def draw_deal_order(key, part):
    lengths = pack_lengths(key)
    key = jax.random.fold_in(key, 5)
    pack_cost = jnp.sum(lengths * lengths, axis=-1)
    by_cost = jnp.argsort(pack_cost, stable=True).astype(jnp.int32)
    half_count = PACKS // 2
    heavy_packs = by_cost[half_count:][::-1]
    light_packs = by_cost[:half_count]
    placing = jax.random.permutation(key, half_count)
    dealing = jnp.zeros((PACKS,), jnp.int32)
    dealing = dealing.at[2 * placing].set(heavy_packs)
    dealing = dealing.at[2 * placing + 1].set(light_packs)
    return dealing


def shard_levels(own_key, dims, cuts, least, top_value):
    def one(dim, parts):
        draws = jax.random.uniform(jax.random.fold_in(jax.random.fold_in(own_key, 6), dim), (parts,), jnp.float32, least / len(cuts), top_value / len(cuts))
        return jnp.repeat(jnp.exp(draws), dims[dim] // parts).reshape((-1,) + (1,) * (len(dims) - dim - 1))

    level = one(*cuts[0])
    for cut in cuts[1:]:
        level = level * one(*cut)
    return level


def noise(stream_key, dims, scale, bound, cuts=(), kind=jnp.bfloat16):
    array = scale * jax.random.normal(stream_key, dims, jnp.float32)
    if cuts:
        array = array * shard_levels(stream_key, dims, cuts, -0.22, 0.18)
    return jnp.clip(array, -bound, bound).astype(kind)


def setup_inputs(seed: int = 0) -> dict:
    splits = jax.random.split(jax.random.key(seed), 16)
    tokens = noise(splits[0], (PACKS, PACK_LEN, D), 1.0, 6.0, ((1, 4), (2, 8)))
    cotangent = noise(splits[1], (PACKS, PACK_LEN, D), 1.0, 6.0, ((0, 8), (1, 4)))
    seq_lengths = draw_seq_lengths(jax.random.fold_in(splits[15], 71), 0)
    deal_order = draw_deal_order(jax.random.fold_in(splits[15], 71), 0)
    in_gain = jnp.clip(1.0 + 0.1 * jax.random.normal(splits[4], (D,), jnp.float32), 0.5, 1.5).astype(jnp.bfloat16)
    in_proj = noise(splits[5], (D, IN_COLS), D ** -0.5, 0.1875, ((0, 8),))
    dt_proj = noise(splits[6], (D, MH), D ** -0.5, 0.1875, ((0, 8),))
    dt_bias = jnp.clip(jax.random.uniform(splits[7], (MH,), jnp.float32, -7.0, -3.0), -7.0, -3.0)
    a_log = jnp.clip(jax.random.uniform(splits[8], (MH,), jnp.float32, 0.0, 2.5), 0.0, 2.5)
    d_skip = jnp.clip(jnp.exp(jax.random.uniform(splits[9], (MH,), jnp.float32, math.log(0.5), math.log(2.0))), 0.5, 2.0)
    ssm_out = noise(splits[10], (DI, D), DI ** -0.5, 0.15625, ((0, 8),))
    attn_out = noise(splits[11], (QUERY_HEADS * HEAD_WIDTH, D), (QUERY_HEADS * HEAD_WIDTH // 16) ** -0.5, 1.0, ((0, 8),))
    ffn_gain = jnp.clip(1.0 + 0.1 * jax.random.normal(splits[12], (D,), jnp.float32), 0.5, 1.5).astype(jnp.bfloat16)
    gate_up = noise(splits[13], (D, 2 * FF), D ** -0.5, 0.1875, ((0, 8),))
    down_proj = noise(splits[14], (FF, D), FF ** -0.5, 0.125, ((0, 8),))
    return {"tokens": tokens, "cotangent": cotangent, "seq_lengths": seq_lengths, "deal_order": deal_order, "in_gain": in_gain, "in_proj": in_proj, "dt_proj": dt_proj, "dt_bias": dt_bias, "a_log": a_log, "d_skip": d_skip, "ssm_out": ssm_out, "attn_out": attn_out, "ffn_gain": ffn_gain, "gate_up": gate_up, "down_proj": down_proj}


EPS = 1e-05
THETA = 100000000000.0
HIGH_PRECISION = lax.Precision.HIGHEST

@jax.custom_vjp
def low(v):
    return lax.optimization_barrier(v.astype(jnp.bfloat16)).astype(jnp.float32)

@jax.custom_vjp
def low_back(v):
    return v

def low_keep(v):
    return (low(v), None)

def low_pass(kept, grad):
    return (grad,)

def back_keep(v):
    return (v, None)

def back_low(kept, grad):
    return (low(grad),)
low.defvjp(low_keep, low_pass)
low_back.defvjp(back_keep, back_low)

def both_ways(value_rows):
    return low(low_back(value_rows))

def rms_scale(value_rows, gain):
    return value_rows * lax.rsqrt(lax.optimization_barrier(jnp.mean(value_rows * value_rows, axis=-1, keepdims=True)) + EPS) * gain

def segments(lengths, seq_len):
    seq_ends = jnp.cumsum(lengths, axis=-1)[..., :-1].astype(jnp.int32)
    places = jnp.arange(seq_len, dtype=jnp.int32)
    return lax.optimization_barrier(jnp.sum((places[None, :, None] >= seq_ends[:, None, :]).astype(jnp.int32), axis=-1)).astype(jnp.int32)

def rotate(value_rows, places):
    half_dim = value_rows.shape[-1] // 2
    frequency = THETA ** (-jnp.arange(half_dim, dtype=jnp.float32) * 2.0 / value_rows.shape[-1])
    angles = places.astype(jnp.float32)[:, None] * frequency[None, :]
    cosine = jnp.cos(angles)[None, :, None, :]
    sine_vals = jnp.sin(angles)[None, :, None, :]
    lower_half = value_rows[..., :half_dim]
    upper_half = value_rows[..., half_dim:]
    return jnp.concatenate([lower_half * cosine - upper_half * sine_vals, upper_half * cosine + lower_half * sine_vals], axis=-1)

def attention(queries, key_rows, value_rows, seg_ids):
    num_packs, seq_len, num_heads, head_width = queries.shape
    places = jnp.arange(seq_len, dtype=jnp.int32)
    queries = rotate(queries, places)
    key_rows = rotate(key_rows[:, :, None, :], places)[:, :, 0, :]
    blocks = seq_len // QBLOCK
    q_blocks = jnp.moveaxis(queries.reshape(num_packs, blocks, QBLOCK, num_heads, head_width), 1, 0)
    seg_blocks = jnp.moveaxis(seg_ids.reshape(num_packs, blocks, QBLOCK), 1, 0)
    place_blocks = places.reshape(blocks, QBLOCK)

    def one_block(inputs):
        query_block, seg_block, place_block = inputs
        score_matrix = jnp.einsum('rgce,rme->rcgm', query_block, key_rows, precision=HIGH_PRECISION) * head_width ** (-0.5)
        score_matrix = low_back(score_matrix)
        causal = (place_block[:, None] >= places[None, :])[None, None]
        same_seq = (seg_block[:, :, None] == seg_ids[:, None, :])[:, None]
        masked = jnp.where(causal & same_seq, score_matrix, -jnp.inf)
        row_top = lax.optimization_barrier(jnp.max(masked, axis=-1, keepdims=True))
        weights = jnp.exp(masked - row_top)
        group_shares = low(weights / lax.optimization_barrier(jnp.sum(weights, axis=-1, keepdims=True)))
        return jnp.einsum('jnft,jtm->jfnm', group_shares, value_rows, precision=HIGH_PRECISION)
    results = lax.map(jax.checkpoint(one_block), (q_blocks, seg_blocks, place_blocks))
    return jnp.moveaxis(results, 0, 1).reshape(num_packs, seq_len, num_heads * head_width)

def scan_heads(inputs_x, inputs_b, inputs_c, dt_raw, bias_dt, log_a, skip_d, seg_ids):
    num_packs, seq_len, num_heads, head_width = inputs_x.shape
    dt_vals = jax.nn.softplus(dt_raw + bias_dt)
    log_decay = -dt_vals * jnp.exp(log_a)
    scaled_x = inputs_x * dt_vals[..., None]
    blocks = seq_len // STRETCH

    def to_blocks(value_rows):
        return jnp.moveaxis(value_rows.reshape((num_packs, blocks, STRETCH) + value_rows.shape[2:]), 1, 0)
    tri_mask = jnp.arange(STRETCH)[:, None] >= jnp.arange(STRETCH)[None, :]

    def stretch_step(carry, inputs):
        carry_state, prev_seg = carry
        x_scaled, b_part, c_part, decay_log, seg_part = inputs
        cum_log = jnp.cumsum(decay_log, axis=1)
        same_seg = (seg_part[:, :, None] == seg_part[:, None, :]) & tri_mask[None]
        spread = jnp.exp(jnp.where(same_seg[..., None], cum_log[:, :, None, :] - cum_log[:, None, :, :], -jnp.inf))
        inner_prod = jnp.einsum('btn,bsn->bts', c_part, b_part, precision=HIGH_PRECISION)
        mixing = inner_prod[..., None] * spread
        local_y = jnp.einsum('btsm,bsmp->btmp', mixing, x_scaled, precision=HIGH_PRECISION)
        carried = (seg_part == prev_seg[:, None]).astype(jnp.float32)
        from_state = jnp.einsum('btn,bmpn->btmp', c_part, carry_state, precision=HIGH_PRECISION)
        local_y = local_y + from_state * (jnp.exp(cum_log) * carried[..., None])[..., None]
        last_seg = seg_part[:, -1].astype(jnp.int32)
        end_same = (seg_part == last_seg[:, None])[..., None]
        to_end = jnp.exp(jnp.where(end_same, cum_log[:, -1:, :] - cum_log, -jnp.inf))
        keep_state = jnp.exp(cum_log[:, -1, :]) * (last_seg == prev_seg).astype(jnp.float32)[:, None]
        weighted_x = to_end[..., None] * x_scaled
        carry_state = carry_state * keep_state[..., None, None] + jnp.einsum('bsmp,bsn->bmpn', weighted_x, b_part, precision=HIGH_PRECISION)
        return ((carry_state, last_seg), local_y)
    start_carry = (jnp.zeros((num_packs, num_heads, head_width, inputs_b.shape[-1]), inputs_x.dtype), jnp.full((num_packs,), -1, jnp.int32))
    ignored, outputs = lax.scan(jax.checkpoint(stretch_step), start_carry, (to_blocks(scaled_x), to_blocks(inputs_b), to_blocks(inputs_c), to_blocks(log_decay), to_blocks(seg_ids)))
    result = jnp.moveaxis(outputs, 0, 1).reshape(inputs_x.shape) + skip_d[:, None] * inputs_x
    return result.reshape(num_packs, seq_len, num_heads * head_width)

def matmul(left, right):
    return jnp.einsum('bld,df->blf', left, right, precision=HIGH_PRECISION)

def layer(params, residual, seg_ids):
    in_gain, in_proj, dt_proj, dt_bias, a_log, d_skip, ssm_out, attn_out, ffn_gain, gate_up, down_proj = params
    num_packs, seq_len = (residual.shape[0], residual.shape[1])
    inner_dim = MH * HP
    normed = both_ways(rms_scale(residual, in_gain))
    projected = both_ways(matmul(normed, in_proj))
    dt_raw = both_ways(matmul(normed, dt_proj))
    z_part = projected[..., :inner_dim]
    x_part = projected[..., inner_dim:2 * inner_dim]
    b_part = projected[..., 2 * inner_dim:2 * inner_dim + NS]
    c_part = projected[..., 2 * inner_dim + NS:2 * inner_dim + 2 * NS]
    q_start = 2 * inner_dim + 2 * NS
    key_offset = q_start + QUERY_HEADS * HEAD_WIDTH
    value_offset = key_offset + KEY_VALUE_HEADS * HEAD_WIDTH
    query_group = QUERY_HEADS // N_SEQ
    m_group = MH // N_SEQ
    attn_pieces = []
    ssm_pieces = []
    for group_number in range(N_SEQ):
        key_value_head = group_number * query_group // (QUERY_HEADS // KEY_VALUE_HEADS)
        queries = projected[..., q_start + group_number * query_group * HEAD_WIDTH:q_start + (group_number + 1) * query_group * HEAD_WIDTH]
        key_rows = low_back(projected[..., key_offset + key_value_head * HEAD_WIDTH:key_offset + (key_value_head + 1) * HEAD_WIDTH])
        value_rows = low_back(projected[..., value_offset + key_value_head * HEAD_WIDTH:value_offset + (key_value_head + 1) * HEAD_WIDTH])
        attn_pieces.append(attention(queries.reshape(num_packs, seq_len, query_group, HEAD_WIDTH), key_rows, value_rows, seg_ids))
        low_head = group_number * m_group
        high_head = low_head + m_group
        inputs_x = x_part[..., low_head * HP:high_head * HP].reshape(num_packs, seq_len, m_group, HP)
        ssm_pieces.append(scan_heads(inputs_x, low_back(b_part), low_back(c_part), dt_raw[..., low_head:high_head], dt_bias[low_head:high_head], a_log[low_head:high_head], d_skip[low_head:high_head], seg_ids))
    attn_vals = both_ways(jnp.concatenate(attn_pieces, axis=-1))
    ssm_vals = both_ways(jnp.concatenate(ssm_pieces, axis=-1))
    gated_vals = both_ways(ssm_vals * jax.nn.silu(z_part))
    branch = low_back(matmul(gated_vals, ssm_out) + matmul(attn_vals, attn_out))
    middle = residual + branch
    normed_two = both_ways(rms_scale(middle, ffn_gain))
    gate_vals = both_ways(matmul(normed_two, gate_up))
    acted_vals = both_ways(jax.nn.silu(gate_vals[..., :FF]) * gate_vals[..., FF:])
    return middle + low_back(matmul(acted_vals, down_proj))

def reference(tokens, cotangent, seq_lengths, deal_order, in_gain, in_proj, dt_proj, dt_bias, a_log, d_skip, ssm_out, attn_out, ffn_gain, gate_up, down_proj):
    params = tuple((weight.astype(jnp.float32) for weight in (in_gain, in_proj, dt_proj, dt_bias, a_log, d_skip, ssm_out, attn_out, ffn_gain, gate_up, down_proj)))
    dealt = tokens.astype(jnp.float32)[deal_order]
    seg_all = segments(seq_lengths[deal_order], PACK_LEN)
    x_batches = dealt.reshape(PACKS // 4, 4, PACK_LEN, D)
    cot_batches = cotangent.astype(jnp.float32).reshape(PACKS // 4, 4, PACK_LEN, D)
    seg_batches = seg_all.reshape(PACKS // 4, 4, PACK_LEN)

    def batch_step(grad_total, inputs):
        x_batch, cot_batch, seg_batch = inputs

        def forward(params_in, x_in):
            return layer(params_in, x_in, seg_batch)
        out_batch, back_fn = jax.vjp(forward, params, x_batch)
        grad_params, grad_x = back_fn(cot_batch)
        return (jax.tree.map(jnp.add, grad_total, grad_params), (out_batch, grad_x))
    zero_grads = jax.tree.map(jnp.zeros_like, params)
    grad_total, (outs_all, grads_all) = lax.scan(batch_step, zero_grads, (x_batches, cot_batches, seg_batches))
    output = outs_all.reshape(PACKS, PACK_LEN, D).astype(jnp.bfloat16)
    grad_dealt = grads_all.reshape(PACKS, PACK_LEN, D).astype(jnp.bfloat16)
    grad_tokens = grad_dealt[jnp.argsort(deal_order)]
    return (output, grad_tokens, grad_total[0], grad_total[1], grad_total[2], grad_total[3], grad_total[4], grad_total[5], grad_total[6], grad_total[7], grad_total[8], grad_total[9], grad_total[10])
```

```python
import functools

import jax
import jax.numpy as jnp
from jax import lax
from jax.experimental import pallas as pl
from jax.experimental.pallas import tpu as pltpu
from jax.sharding import PartitionSpec as P

FF = 2048
QUERY_HEADS = 8
KEY_VALUE_HEADS = 2
HEAD_WIDTH = 64
MH = 24
HP = 64
NS = 128
EPS = 1e-05
THETA = 100000000000.0
BF = jnp.bfloat16
F32 = jnp.float32
CORES = 2
CHIP_HEADS = MH // CORES
XW = CHIP_HEADS * HP
QW = QUERY_HEADS // CORES * HEAD_WIDTH
Z0, X0, Q0, KV0, B0, C0, T0 = 0, XW, 2 * XW, 2 * XW + QW, 2 * XW + QW + 128, 2 * XW + QW + 256, 2 * XW + QW + 384
COLS = T0 + 128
CHUNK = 256
QB = 256
FAR = -1e30
MIB = 1 << 20
MESH = pl.DeviceIdType.MESH
VM = pltpu.VMEM


def dot(a, b, dims=((1,), (0,)), precision=None):
    return lax.dot_general(a, b, (dims, ((), ())), precision=precision, preferred_element_type=F32)


def lanes(rows, width=128):
    return lax.broadcasted_iota(jnp.int32, (rows, width), 1)


def swap_halves(v):
    low = lanes(v.shape[0], v.shape[1]) % 64 < 32
    return jnp.where(low, pltpu.roll(v, v.shape[1] - 32, 1), pltpu.roll(v, 32, 1))


def turn(v, cosine, sine):
    return v * cosine + swap_halves(v) * sine


def turn_back(v, cosine, sine):
    return v * cosine - swap_halves(v) * sine


def widen(v, spread):
    v = jnp.where(lanes(v.shape[0]) < 64, v, 0.0)
    top = v.astype(BF)
    rest = (v - top.astype(F32)).astype(BF).astype(F32)
    both = top.astype(F32) + pltpu.roll(rest, 64, 1)
    return dot(both.astype(BF), spread)


def attn_masks(segc_ref, segr_ref, i, upto):
    rows = pl.ds(i * QB, QB)
    same = segc_ref[rows, 0:1] == segr_ref[0:1, 0:upto]
    t = lax.broadcasted_iota(jnp.int32, (QB, upto), 0) + i * QB
    u = lax.broadcasted_iota(jnp.int32, (QB, upto), 1)
    return jnp.where(same & (u <= t), 0.0, FAR)


def key_value_pairs(kv, cosine, sine):
    low = lanes(kv.shape[0]) < 64
    other = pltpu.roll(kv, 64, 1)
    kk = turn(jnp.where(low, kv, other), cosine, sine)
    vv = jnp.where(low, other, kv)
    return kk.astype(BF), vv.astype(BF)


def attention_forward(proj_ref, cos_ref, sin_ref, segc_ref, segr_ref, attn_ref, lse_ref):
    seq_len = proj_ref.shape[0]
    kk, vv = key_value_pairs(proj_ref[:, KV0 : KV0 + 128].astype(F32), cos_ref[...], sin_ref[...])
    low = lanes(QB) < 64
    for i in range(seq_len // QB):
        rows = slice(i * QB, (i + 1) * QB)
        upto = (i + 1) * QB
        mask = attn_masks(segc_ref, segr_ref, i, upto)
        tops = jnp.zeros((QB, 128), F32)
        for pair in range(QW // 128):
            q = proj_ref[rows, Q0 + 128 * pair : Q0 + 128 * (pair + 1)].astype(F32)
            q = turn(q, cos_ref[rows, :], sin_ref[rows, :]) * HEAD_WIDTH**-0.5
            outs = []
            for half in range(2):
                qh = jnp.where(low if half == 0 else ~low, q, 0.0).astype(BF)
                s = dot(qh, kk[:upto], ((1,), (1,))) + mask
                top = jnp.max(s, axis=1, keepdims=True)
                e = jnp.exp(s - top)
                total = jnp.sum(e, axis=1, keepdims=True)
                outs.append(dot(e.astype(BF), vv[:upto]) / total)
                tops = jnp.where(lanes(QB) == 2 * pair + half, top + jnp.log(total), tops)
            attn_ref[rows, 128 * pair : 128 * (pair + 1)] = jnp.where(low, outs[0], outs[1]).astype(BF)
        lse_ref[rows, :] = tops


def attention_backward(proj_ref, cos_ref, sin_ref, segc_ref, segr_ref, attn_ref, lse_ref, gattn_ref, gproj_ref, gkv):
    seq_len = proj_ref.shape[0]
    kk, vv = key_value_pairs(proj_ref[:, KV0 : KV0 + 128].astype(F32), cos_ref[...], sin_ref[...])
    low = lanes(QB) < 64
    gkv[...] = jnp.zeros_like(gkv)
    pick = (lax.broadcasted_iota(jnp.int32, (QW, 128), 0) // 64 == lanes(QW)).astype(BF)
    for i in range(seq_len // QB):
        rows = slice(i * QB, (i + 1) * QB)
        upto = (i + 1) * QB
        same = segc_ref[0:upto, 0:1] == segr_ref[0:1, rows]
        t = lanes(upto, QB) + i * QB
        u = lax.broadcasted_iota(jnp.int32, (upto, QB), 0)
        mask = jnp.where(same & (u <= t), 0.0, FAR)
        weighed = gattn_ref[rows, :].astype(F32) * attn_ref[rows, :].astype(F32)
        deltas = dot(weighed.astype(BF), pick).T
        tops = lse_ref[rows, :].T
        for pair in range(QW // 128):
            cosine, sine = cos_ref[rows, :], sin_ref[rows, :]
            q = proj_ref[rows, Q0 + 128 * pair : Q0 + 128 * (pair + 1)].astype(F32)
            q = turn(q, cosine, sine) * HEAD_WIDTH**-0.5
            g = gattn_ref[rows, 128 * pair : 128 * (pair + 1)]
            grads = []
            for half in range(2):
                head = 2 * pair + half
                mine = low if half == 0 else ~low
                qh = jnp.where(mine, q, 0.0).astype(BF)
                gh = jnp.where(mine, g, jnp.zeros_like(g))
                s = dot(kk[:upto], qh, ((1,), (1,))) + mask
                p = jnp.exp(s - tops[head : head + 1, :])
                gp = dot(vv[:upto], gh, ((1,), (1,)))
                gs = (p * (gp - deltas[head : head + 1, :])).astype(BF)
                gkv[0:upto, 0:128] += dot(gs, qh)
                gkv[0:upto, 128:256] += dot(p.astype(BF), gh)
                grads.append(dot(gs, kk[:upto], ((0,), (0,))))
            gq = jnp.where(low, grads[0], grads[1]) * HEAD_WIDTH**-0.5
            gproj_ref[rows, Q0 + 128 * pair : Q0 + 128 * (pair + 1)] = turn_back(gq, cosine, sine).astype(BF)
    gk = gkv[:, 0:128]
    gv = gkv[:, 128:256]
    gk = turn_back(gk + pltpu.roll(gk, 64, 1), cos_ref[...], sin_ref[...])
    gv = gv + pltpu.roll(gv, 64, 1)
    gproj_ref[:, KV0 : KV0 + 128] = jnp.where(lanes(seq_len) < 64, gk, gv).astype(BF)


def scan_pieces(j, proj_ref, segc_ref, segr_ref, par_ref):
    rows = pl.ds(pl.multiple_of(j * CHUNK, CHUNK), CHUNK)
    seg = segc_ref[rows, :]
    prev = segc_ref[pl.ds(jnp.maximum(j * CHUNK - 1, 0), 1), :]
    prev = jnp.where(j == 0, -1, prev)
    last = segc_ref[pl.ds(j * CHUNK + CHUNK - 1, 1), :]
    valid = lanes(CHUNK) < CHIP_HEADS
    raw = proj_ref[rows, T0 : T0 + 128].astype(F32) + par_ref[0:1, :]
    dt = jnp.where(valid, jnp.maximum(raw, 0.0) + jnp.log1p(jnp.exp(-jnp.abs(raw))), 0.0)
    decay = dt * par_ref[1:2, :]
    place = lax.broadcasted_iota(jnp.int32, (CHUNK, CHUNK), 0)
    under = (place >= lanes(CHUNK, CHUNK)).astype(F32)
    cum = dot(under, decay, precision=lax.Precision.HIGHEST)
    end = cum[CHUNK - 1 : CHUNK, :]
    from_start = jnp.where(seg == prev, jnp.exp(cum), 0.0)
    to_end = jnp.where(seg == last, jnp.exp(end - cum), 0.0)
    keep = jnp.where(last == prev, jnp.exp(end), 0.0)
    return rows, raw, dt, decay, cum, from_start, to_end, keep, under


def scan_forward(proj_ref, segc_ref, segr_ref, par_ref, spread_ref, wide_ref, gated_ref, y_ref, states_ref, state):
    spread = spread_ref[...]
    state[...] = jnp.zeros_like(state)

    def chunk(j, carry):
        rows, raw, dt, decay, cum, from_start, to_end, keep, under = scan_pieces(j, proj_ref, segc_ref, segr_ref, par_ref)
        place = lax.broadcasted_iota(jnp.int32, (CHUNK, CHUNK), 0)
        same = segc_ref[rows, 0:1] == segr_ref[0:1, rows]
        mask = jnp.where(same & (place >= lanes(CHUNK, CHUNK)), 0.0, FAR)
        cum_t = cum.T
        b = proj_ref[rows, B0 : B0 + 128]
        c = proj_ref[rows, C0 : C0 + 128]
        cb = dot(c, b, ((1,), (1,)))
        x = proj_ref[rows, X0 : X0 + XW].astype(F32)
        xdt = x * widen(dt, spread)
        xdt_low = xdt.astype(BF)
        old = state[...]
        states_ref[j] = old
        y_state = dot(c, old.astype(BF)) * widen(from_start, spread)
        low = lanes(CHUNK) < 64
        for pair in range(CHIP_HEADS // 2):
            cols = slice(128 * pair, 128 * (pair + 1))
            xp = xdt_low[:, cols]
            local = y_state[:, cols]
            for half in range(2):
                h = 2 * pair + half
                spread_h = jnp.exp(cum[:, h : h + 1] - cum_t[h : h + 1, :] + mask)
                mix = (cb * spread_h).astype(BF)
                xh = jnp.where(low if half == 0 else ~low, xp, jnp.zeros_like(xp))
                local = local + dot(mix, xh)
            y_ref[rows, cols] = local
            y = (local + x[:, cols] * wide_ref[0:1, cols]).astype(BF).astype(F32)
            z = proj_ref[rows, Z0 + 128 * pair : Z0 + 128 * (pair + 1)].astype(F32)
            gated_ref[rows, cols] = (y * (z / (1.0 + jnp.exp(-z)))).astype(BF)
        weighted = (xdt * widen(to_end, spread)).astype(BF)
        keep_wide = widen(jnp.broadcast_to(keep, (8, 128)), spread)[0:1, :]
        state[...] = old * keep_wide + dot(b, weighted, ((0,), (0,)))
        return carry

    lax.fori_loop(0, proj_ref.shape[0] // CHUNK, chunk, 0)


def scan_backward(proj_ref, segc_ref, segr_ref, par_ref, spread_ref, wide_ref, y_ref, states_ref, ggated_ref, gproj_ref, gpar_ref, gstate):
    spread = spread_ref[...]
    gstate[...] = jnp.zeros_like(gstate)
    gpar_ref[...] = jnp.zeros_like(gpar_ref)
    chunks = proj_ref.shape[0] // CHUNK

    def narrow(v):
        top = v.astype(BF)
        rest = (v - top.astype(F32)).astype(BF)
        return dot(top, spread, ((1,), (1,))) + dot(rest, spread, ((1,), (1,)))

    def chunk(step, carry):
        j = chunks - 1 - step
        rows, raw, dt, decay, cum, from_start, to_end, keep, under = scan_pieces(j, proj_ref, segc_ref, segr_ref, par_ref)
        place = lax.broadcasted_iota(jnp.int32, (CHUNK, CHUNK), 0)
        same = segc_ref[rows, 0:1] == segr_ref[0:1, rows]
        mask = jnp.where(same & (place <= lanes(CHUNK, CHUNK)), 0.0, FAR)
        cum_t = cum.T
        b = proj_ref[rows, B0 : B0 + 128]
        c = proj_ref[rows, C0 : C0 + 128]
        bc = dot(b, c, ((1,), (1,)))
        x = proj_ref[rows, X0 : X0 + XW].astype(F32)
        dt_wide = widen(dt, spread)
        xdt_low = (x * dt_wide).astype(BF)
        start_wide = widen(from_start, spread)
        end_wide = widen(to_end, spread)
        old = states_ref[j]
        gnew = gstate[...]
        z = proj_ref[rows, Z0 : Z0 + XW].astype(F32)
        gg = ggated_ref[rows, :].astype(F32)
        y_own = y_ref[rows, :]
        y = (y_own + x * wide_ref[0:1, :]).astype(BF).astype(F32)
        sig = 1.0 / (1.0 + jnp.exp(-z))
        gy_low = (gg * (z * sig)).astype(BF)
        gproj_ref[rows, Z0 : Z0 + XW] = (gg * y * (sig * (1.0 + z * (1.0 - sig)))).astype(BF)
        gy = gy_low.astype(F32)
        gx_state = end_wide * dot(b, gnew.astype(BF))
        gbc = jnp.zeros((CHUNK, CHUNK), F32)
        low = lanes(CHUNK) < 64
        gxdt = []
        for pair in range(CHIP_HEADS // 2):
            cols = slice(128 * pair, 128 * (pair + 1))
            xp, gp = xdt_low[:, cols], gy_low[:, cols]
            total = gx_state[:, cols]
            for half in range(2):
                h = 2 * pair + half
                mine = low if half == 0 else ~low
                spread_h = jnp.exp(cum_t[h : h + 1, :] - cum[:, h : h + 1] + mask)
                mix = (bc * spread_h).astype(BF)
                gh = jnp.where(mine, gp, jnp.zeros_like(gp))
                total = total + dot(mix, gh)
                gbc = gbc + dot(xp, gh, ((1,), (1,))) * spread_h
            gxdt.append(total)
        gxdt = jnp.concatenate(gxdt, axis=1)
        gstart = (gy * start_wide).astype(BF)
        weighted = (xdt_low.astype(F32) * end_wide).astype(BF)
        gbc_low = gbc.astype(BF)
        gnew_low, old_low = gnew.astype(BF), old.astype(BF)
        gproj_ref[rows, C0 : C0 + 128] = (dot(gbc_low, b, ((0,), (0,))) + dot(gstart, old_low, ((1,), (1,)))).astype(BF)
        gproj_ref[rows, B0 : B0 + 128] = (dot(gbc_low, c) + dot(weighted, gnew_low, ((1,), (1,)))).astype(BF)
        keep_wide = widen(jnp.broadcast_to(keep, (8, 128)), spread)[0:1, :]
        kept = jnp.sum(old * gnew, axis=0, keepdims=True) * keep_wide
        gstate[...] = gnew * keep_wide + dot(c, gstart, ((0,), (0,)))
        xdt_f = xdt_low.astype(F32)
        gcum = narrow(gy * y_own) - narrow(xdt_f * gxdt)
        at_end = jnp.sum(xdt_f * gx_state, axis=0, keepdims=True) + kept
        at_end = narrow(jnp.broadcast_to(at_end, (8, XW)))[0:1, :]
        gdecay = dot(under, gcum, ((0,), (0,)), precision=lax.Precision.HIGHEST) + at_end
        gdt = narrow(gxdt * x) + gdecay * par_ref[1:2, :]
        graw = gdt / (1.0 + jnp.exp(-raw))
        graw = jnp.where(lanes(CHUNK) < CHIP_HEADS, graw, 0.0)
        gproj_ref[rows, T0 : T0 + 128] = graw.astype(BF)
        gproj_ref[rows, X0 : X0 + XW] = (gxdt * dt_wide + gy * wide_ref[0:1, :]).astype(BF)
        gpar_ref[0:1, :] += jnp.sum(graw, axis=0, keepdims=True)
        gpar_ref[1:2, :] += jnp.sum(gdecay * decay, axis=0, keepdims=True)
        skip = jnp.sum(gy * x, axis=0, keepdims=True)
        gpar_ref[2:3, :] += narrow(jnp.broadcast_to(skip, (8, XW)))[0:1, :]
        return carry

    lax.fori_loop(0, chunks, chunk, 0)


def forward_kernel(proj, cosine, sine, segc, segr, par, spread, wide, gated, attn, lse, y, states, state):
    attention_forward(proj, cosine, sine, segc, segr, attn, lse)
    scan_forward(proj, segc, segr, par, spread, wide, gated, y, states, state)


def backward_kernel(proj, cosine, sine, segc, segr, par, spread, wide, attn, lse, y, states, ggated, gattn, gproj, gpar, gkv, gstate):
    attention_backward(proj, cosine, sine, segc, segr, attn, lse, gattn, gproj, gkv)
    scan_backward(proj, segc, segr, par, spread, wide, y, states, ggated, gproj, gpar, gstate)


def whole(n):
    return [pl.BlockSpec(memory_space=VM)] * n


def mixer_forward(proj, consts):
    seq_len = proj.shape[0]
    chunks = seq_len // CHUNK
    return pl.pallas_call(
        forward_kernel,
        name="mixer_forward",
        out_shape=(
            jax.ShapeDtypeStruct((seq_len, XW), BF),
            jax.ShapeDtypeStruct((seq_len, QW), BF),
            jax.ShapeDtypeStruct((seq_len, 128), F32),
            jax.ShapeDtypeStruct((seq_len, XW), F32),
            jax.ShapeDtypeStruct((chunks, NS, XW), F32),
        ),
        in_specs=whole(8),
        out_specs=tuple(whole(5)),
        scratch_shapes=[VM((NS, XW), F32)],
        compiler_params=pltpu.CompilerParams(vmem_limit_bytes=56 * MIB),
    )(proj, *consts)


def mixer_backward(proj, consts, attn, lse, y, states, ggated, gattn):
    seq_len = proj.shape[0]
    return pl.pallas_call(
        backward_kernel,
        name="mixer_backward",
        out_shape=(
            jax.ShapeDtypeStruct((seq_len, COLS), BF),
            jax.ShapeDtypeStruct((8, 128), F32),
        ),
        in_specs=whole(14),
        out_specs=tuple(whole(2)),
        scratch_shapes=[VM((seq_len, 256), F32), VM((NS, XW), F32)],
        compiler_params=pltpu.CompilerParams(vmem_limit_bytes=56 * MIB),
    )(proj, *consts, attn, lse, y, states, ggated, gattn)


def place():
    d, s = lax.axis_index("dp"), lax.axis_index("seq")
    return d // 2, d % 2, s // 2, s % 2


def device(z, x, y, c):
    return (2 * z + x, 2 * y + c)


def greet(peers):
    barrier = pltpu.get_barrier_semaphore()
    for peer in peers:
        pl.semaphore_signal(barrier, inc=1, device_id=peer, device_id_type=MESH)
    pl.semaphore_wait(barrier, len(peers))


def send(src, dst, sems, k, target):
    copy = pltpu.make_async_remote_copy(
        src_ref=src, dst_ref=dst, send_sem=sems[0].at[k], recv_sem=sems[1].at[k], device_id=target, device_id_type=MESH
    )
    copy.start()
    return copy


def landed(dst, sems, k, target):
    pltpu.make_async_remote_copy(
        src_ref=dst, dst_ref=dst, send_sem=sems[0].at[k], recv_sem=sems[1].at[k], device_id=target, device_id_type=MESH
    ).wait_recv()


ARRAY_SENDS = 13


class Gather:
    def __init__(self, src, dst, sems, base, local_sem):
        self.src, self.dst, self.sems, self.base = src, dst, sems, base
        self.local_sem = local_sem
        self.z, self.x, self.y, self.c = place()
        half = src.shape[0] // 2
        self.mine = pl.ds(self.y * half, half)
        self.other = pl.ds((1 - self.y) * half, half)
        self.sent = []
        self.xpeer = device(self.z, 1 - self.x, self.y, self.c)
        self.ypeer = device(self.z, self.x, 1 - self.y, self.c)

    def block(self, r, x, rows):
        return self.dst.at[2 * (self.z ^ r) + x, rows]

    def push(self, k, ref, target, dst=None):
        self.sent.append(send(ref, ref if dst is None else dst, self.sems, self.base + k, target))

    def start(self):
        own = 2 * self.z + self.x
        self.local = pltpu.make_async_copy(self.src, self.dst.at[own], self.local_sem)
        self.local.start()
        for r in (1, 2, 3):
            target = device(self.z ^ r, self.x, self.y, self.c)
            self.push(r - 1, self.src.at[self.mine], target, self.dst.at[own, self.mine])
        self.push(3, self.src, self.xpeer, self.dst.at[own])

    def forward(self, r):
        ref = self.block(r, self.x, self.mine)
        landed(ref, self.sems, self.base + r - 1, self.xpeer)
        self.push(3 + r, ref, self.xpeer)
        self.push(6 + r, ref, self.ypeer)

    def corner(self, r):
        if r == 1:
            ref = self.block(r, self.x, self.other)
            landed(ref, self.sems, self.base + 6 + r, self.ypeer)
            self.push(9 + r, ref, self.xpeer)
        else:
            ref = self.block(r, 1 - self.x, self.mine)
            landed(ref, self.sems, self.base + 3 + r, self.xpeer)
            self.push(9 + r, ref, self.ypeer)

    def finish(self):
        landed(self.dst.at[2 * self.z + 1 - self.x], self.sems, self.base + 3, self.xpeer)
        for r in (1, 2, 3):
            if r == 1:
                landed(self.block(r, 1 - self.x, self.mine), self.sems, self.base + 3 + r, self.xpeer)
            else:
                landed(self.block(r, self.x, self.other), self.sems, self.base + 6 + r, self.ypeer)
            landed(self.block(r, 1 - self.x, self.other), self.sems, self.base + 9 + r, self.ypeer)
        for copy in self.sent:
            copy.wait_send()
        self.local.wait()


def chip_peers():
    z, x, y, c = place()
    peers = [device(z ^ r, x, y, c) for r in (1, 2, 3)]
    peers += [device(z, 1 - x, y, c), device(z, x, 1 - y, c), device(z, x, y, 1 - c)]
    return peers


def start_kernel(dealt, cot, w, rows, weights, gcot, dsend, drecv, wsend, wrecv, local):
    z, x, y, c = place()
    own = 2 * z + x
    slot = 2 * y + c
    partner = device(z, x, y, 1 - c)
    ypeer = device(z, x, 1 - y, c)
    others = [(r, i, j) for r in range(4) for i in range(2) for j in range(2) if r or i or j]
    targets = [device(z ^ r, x ^ i, y ^ j, c) for r, i, j in others]
    greet(targets + [partner])
    sems = (dsend, drecv)
    gather = Gather(w, weights, (wsend, wrecv), 0, local.at[0])
    columns = lambda d: pl.ds(pl.multiple_of(d * 128, 128), 128)
    sent = []
    for k, (r, i, j) in enumerate(others):
        pack = 2 * (2 * (z ^ r) + (x ^ i)) + (y ^ j)
        sent.append(send(dealt.at[pack], rows.at[slot, :, columns(own)], sems, k, targets[k]))
    here = pltpu.make_async_copy(dealt.at[2 * own + y], rows.at[slot, :, columns(own)], local.at[1])
    here.start()
    gather.start()
    sent.append(send(cot.at[1 - y], gcot.at[slot], sems, 18, ypeer))
    sent.append(send(cot.at[y], gcot.at[slot], sems, 19, partner))
    mine = pltpu.make_async_copy(cot.at[y], gcot.at[slot], local.at[2])
    mine.start()
    for r in (1, 2, 3):
        gather.forward(r)
    here.wait()
    for same_y in (True, False):
        for k, (r, i, j) in enumerate(others):
            if (j == 0) == same_y:
                src = 2 * (z ^ r) + (x ^ i)
                landed(rows.at[2 * (y ^ j) + c, :, columns(src)], sems, k, targets[k])
        ref = rows.at[slot if same_y else 2 * (1 - y) + c]
        sent.append(send(ref, ref, sems, 15 if same_y else 16, partner))
    for r in (1, 2, 3):
        gather.corner(r)
    ref = gcot.at[2 * (1 - y) + c]
    landed(ref, sems, 18, ypeer)
    sent.append(send(ref, ref, sems, 17, partner))
    landed(rows.at[2 * y + 1 - c], sems, 15, partner)
    landed(rows.at[2 * (1 - y) + 1 - c], sems, 16, partner)
    landed(gcot.at[2 * (1 - y) + 1 - c], sems, 17, partner)
    landed(gcot.at[2 * y + 1 - c], sems, 19, partner)
    for copy in sent:
        copy.wait_send()
    gather.finish()
    mine.wait()


def any_specs(n):
    return [pl.BlockSpec(memory_space=pl.ANY)] * n


def start_transfers(dealt, cot, w):
    packs, span, width = dealt.shape
    return pl.pallas_call(
        start_kernel,
        name="deal_and_gather",
        out_shape=(
            jax.ShapeDtypeStruct((4, span, 8 * width), BF),
            jax.ShapeDtypeStruct((8,) + w.shape, BF),
            jax.ShapeDtypeStruct((4,) + cot.shape[1:], BF),
        ),
        in_specs=any_specs(3),
        out_specs=tuple(any_specs(3)),
        scratch_shapes=[
            pltpu.SemaphoreType.DMA((20,)),
            pltpu.SemaphoreType.DMA((20,)),
            pltpu.SemaphoreType.DMA((ARRAY_SENDS,)),
            pltpu.SemaphoreType.DMA((ARRAY_SENDS,)),
            pltpu.SemaphoreType.DMA((3,)),
        ],
        compiler_params=pltpu.CompilerParams(collective_id=0, has_side_effects=True),
    )(dealt, cot, w)


def gather_kernel(ssm, att, gu, dn, ssm_own, att_own, gu_all, dn_all, ssm_all, att_all, gsend, grecv, csend, crecv, local):
    z, x, y, c = place()
    partner = device(z, x, y, 1 - c)
    greet(chip_peers())
    sems = (gsend, grecv)
    pairs = ((ssm, ssm_all), (att, att_all), (gu, gu_all), (dn, dn_all))
    gathers = [Gather(a, b, sems, ARRAY_SENDS * i, local.at[i]) for i, (a, b) in enumerate(pairs)]
    for g in gathers:
        g.start()
    for g in gathers:
        for r in (1, 2, 3):
            g.forward(r)
    for g in gathers:
        for r in (1, 2, 3):
            g.corner(r)
    sent = []
    for i, (g, out) in enumerate(zip(gathers[:2], (ssm_own, att_own))):
        g.finish()
        half = g.src.shape[1]
        columns = lambda k: pl.ds(pl.multiple_of(k * half, 128), half)
        here = pltpu.make_async_copy(g.dst.at[pl.ds(4 * c, 4)], out.at[:, :, columns(c)], local.at[4 + i])
        here.start()
        sent.append(here)
        sent.append(send(g.dst.at[pl.ds(4 * (1 - c), 4)], out.at[:, :, columns(c)], (csend, crecv), i, partner))
    for g in gathers[2:]:
        g.finish()
    for i, out in enumerate((ssm_own, att_own)):
        half = out.shape[2] // 2
        landed(out.at[:, :, pl.ds(pl.multiple_of((1 - c) * half, 128), half)], (csend, crecv), i, partner)
        sent[2 * i].wait()
        sent[2 * i + 1].wait_send()


def gather_weights(ssm, att, gu, dn):
    total = 4 * ARRAY_SENDS
    outs = pl.pallas_call(
        gather_kernel,
        name="gather_weights",
        out_shape=(
            jax.ShapeDtypeStruct((4, ssm.shape[0], 2 * ssm.shape[1]), BF),
            jax.ShapeDtypeStruct((4, att.shape[0], 2 * att.shape[1]), BF),
            jax.ShapeDtypeStruct((8,) + gu.shape, BF),
            jax.ShapeDtypeStruct((8,) + dn.shape, BF),
            jax.ShapeDtypeStruct((8,) + ssm.shape, BF),
            jax.ShapeDtypeStruct((8,) + att.shape, BF),
        ),
        in_specs=any_specs(4),
        out_specs=tuple(any_specs(6)),
        scratch_shapes=[
            pltpu.SemaphoreType.DMA((total,)),
            pltpu.SemaphoreType.DMA((total,)),
            pltpu.SemaphoreType.DMA((2,)),
            pltpu.SemaphoreType.DMA((2,)),
            pltpu.SemaphoreType.DMA((6,)),
        ],
        compiler_params=pltpu.CompilerParams(collective_id=1, has_side_effects=True),
    )(ssm, att, gu, dn)
    return [v.reshape(-1, v.shape[-1]) for v in outs[:4]]


def pair_kernel(blocks, part, got, sems_out, sems_in):
    z, x, y, c = place()
    partner = device(z, x, y, 1 - c)
    greet([partner])
    sems = (sems_out, sems_in)
    if blocks:
        sent = [send(part.at[2 * k + 1 - c], got.at[k], sems, k, partner) for k in range(2)]
    else:
        sent = [send(part, got, sems, 0, partner)]
    for copy in sent:
        copy.wait()


def pair_swap(part):
    blocks = part.ndim == 3
    return pl.pallas_call(
        functools.partial(pair_kernel, blocks),
        name="pair_swap_rows" if blocks else "pair_swap",
        out_shape=jax.ShapeDtypeStruct(((2,) + part.shape[1:]) if blocks else part.shape, BF),
        in_specs=any_specs(1),
        out_specs=any_specs(1)[0],
        scratch_shapes=[pltpu.SemaphoreType.DMA((2,)), pltpu.SemaphoreType.DMA((2,))],
        compiler_params=pltpu.CompilerParams(collective_id=3 if blocks else 2, has_side_effects=True),
    )(part)


def columns_kernel(ssm, att, ssm_all, att_all, sems_out, sems_in, local):
    z, x, y, c = place()
    partner = device(z, x, y, 1 - c)
    greet([partner])
    copies = []
    for i, (src, dst) in enumerate(((ssm, ssm_all), (att, att_all))):
        half = src.shape[2] // 2
        columns = lambda k: src.at[:, :, pl.ds(pl.multiple_of(k * half, 128), half)]
        here = pltpu.make_async_copy(columns(c), dst.at[pl.ds(4 * c, 4)], local.at[i])
        here.start()
        copies += [here, send(columns(1 - c), dst.at[pl.ds(4 * c, 4)], (sems_out, sems_in), i, partner)]
    for i, dst in enumerate((ssm_all, att_all)):
        copies[2 * i].wait()
        copies[2 * i + 1].wait_send()
        landed(dst.at[pl.ds(4 * (1 - c), 4)], (sems_out, sems_in), i, partner)


def swap_columns(ssm, att):
    args = [v.reshape(4, -1, v.shape[-1]) for v in (ssm, att)]
    return pl.pallas_call(
        columns_kernel,
        name="swap_columns",
        out_shape=tuple(jax.ShapeDtypeStruct((8, v.shape[1], v.shape[2] // 2), BF) for v in args),
        in_specs=any_specs(2),
        out_specs=tuple(any_specs(2)),
        scratch_shapes=[pltpu.SemaphoreType.DMA((2,))] * 3,
        compiler_params=pltpu.CompilerParams(collective_id=5, has_side_effects=True),
    )(*args)


class Reduce:
    VIA_X = (0, 1)

    def __init__(self, part, out, far, near_x, near_y, deep, sems, base):
        self.part, self.out, self.far, self.near_x, self.near_y, self.deep = part, out, far, near_x, near_y, deep
        self.sems, self.base = sems, base
        self.z, self.x, self.y, self.c = place()
        half = part.shape[1] // 2
        self.mine = pl.ds(self.y * half, half)
        self.other = pl.ds((1 - self.y) * half, half)
        self.xpeer = device(self.z, 1 - self.x, self.y, self.c)
        self.ypeer = device(self.z, self.x, 1 - self.y, self.c)
        self.sent = []

    def piece(self, r, x, rows):
        return self.part.at[2 * (self.z ^ r) + x, rows]

    def push(self, k, src, dst, target):
        self.sent.append(send(src, dst, self.sems, self.base + k, target))

    def start(self):
        for r in (1, 2, 3, 0):
            far = self.piece(r, 1 - self.x, self.other)
            self.push(r, far, self.far.at[r], self.xpeer if r in self.VIA_X else self.ypeer)
        for r in (1, 2, 3, 0):
            if r in self.VIA_X:
                self.push(4 + r, self.piece(r, 1 - self.x, self.mine), self.near_x.at[r], self.xpeer)
            else:
                self.push(8 + r, self.piece(r, self.x, self.other), self.near_y.at[r], self.ypeer)

    def relay(self, r):
        landed(self.far.at[r], self.sems, self.base + r, self.xpeer)
        own = self.piece(r, self.x, self.other) if r in self.VIA_X else self.piece(r, 1 - self.x, self.mine)
        self.far[r] = (own[...].astype(F32) + self.far[r].astype(F32)).astype(BF)
        if r in self.VIA_X:
            self.push(8 + r, self.far.at[r], self.near_y.at[r], self.ypeer)
        else:
            self.push(4 + r, self.far.at[r], self.near_x.at[r], self.xpeer)

    def root(self, r):
        landed(self.near_x.at[r], self.sems, self.base + 4 + r, self.xpeer)
        landed(self.near_y.at[r], self.sems, self.base + 8 + r, self.ypeer)
        own = self.piece(r, self.x, self.mine)[...].astype(F32)
        total = own + (self.near_x[r].astype(F32) + self.near_y[r].astype(F32))
        self.near_x[r] = total.astype(BF)
        if r:
            target = device(self.z ^ r, self.x, self.y, self.c)
            self.push(11 + r, self.near_x.at[r], self.deep.at[r - 1], target)

    def total(self, partner):
        for r in (1, 2, 3):
            landed(self.deep.at[r - 1], self.sems, self.base + 11 + r, self.xpeer)
        total = self.near_x[0].astype(F32) + self.deep[0].astype(F32)
        total = total + (self.deep[1].astype(F32) + self.deep[2].astype(F32))
        self.out[self.c, self.mine] = total.astype(BF)
        ref = self.out.at[self.c, self.mine]
        self.push(15, ref, ref, self.ypeer)
        self.push(16, ref, ref, partner)

    def spread(self, partner):
        ref = self.out.at[self.c, self.other]
        landed(ref, self.sems, self.base + 15, self.ypeer)
        self.push(17, ref, ref, partner)

    def finish(self, partner):
        landed(self.out.at[1 - self.c, self.mine], self.sems, self.base + 16, partner)
        landed(self.out.at[1 - self.c, self.other], self.sems, self.base + 17, partner)
        for copy in self.sent:
            copy.wait_send()


REDUCE_SENDS = 18
N_REDUCED = 5


def reduce_kernel(*refs):
    parts, refs = refs[:N_REDUCED], refs[N_REDUCED:]
    out_rows, gx, refs = refs[0], refs[1], refs[2:]
    reduced, refs = refs[:N_REDUCED], refs[N_REDUCED:]
    output, returned, refs = refs[0], refs[1], refs[2:]
    buffers, refs = [refs[4 * i : 4 * i + 4] for i in range(N_REDUCED)], refs[4 * N_REDUCED :]
    rsend, rrecv, dsend, drecv, local = refs
    z, x, y, c = place()
    own = 2 * z + x
    slot = 2 * own + y
    partner = device(z, x, y, 1 - c)
    ypeer = device(z, x, 1 - y, c)
    others = [(r, i, j) for r in range(4) for i in range(2) for j in range(2) if r or i or j]
    targets = [device(z ^ r, x ^ i, y ^ j, c) for r, i, j in others]
    greet(targets + [partner])
    sums = [Reduce(p, o, *b, (rsend, rrecv), REDUCE_SENDS * k) for k, (p, o, b) in enumerate(zip(parts, reduced, buffers))]
    for s in sums:
        s.start()
    columns = lambda d: pl.ds(pl.multiple_of(d * 128, 128), 128)
    sems = (dsend, drecv)
    sent = [send(out_rows.at[1 - y], output.at[y], sems, 15, ypeer)]
    here = [
        pltpu.make_async_copy(out_rows.at[y], output.at[y], local.at[0]),
        pltpu.make_async_copy(gx.at[y, :, columns(own)], returned.at[slot], local.at[1]),
    ]
    for copy in here:
        copy.start()
    for k, (r, i, j) in enumerate(others):
        d = 2 * (z ^ r) + (x ^ i)
        sent.append(send(gx.at[y ^ j, :, columns(d)], returned.at[slot], sems, k, targets[k]))
    for s in sums:
        for r in (1, 2, 3, 0):
            s.relay(r)
    for s in sums:
        for r in (1, 2, 3, 0):
            s.root(r)
    for s in sums:
        s.total(partner)
    for s in sums:
        s.spread(partner)
    for s in sums:
        s.finish(partner)
    for k, (r, i, j) in enumerate(others):
        landed(returned.at[2 * (2 * (z ^ r) + (x ^ i)) + (y ^ j)], sems, k, targets[k])
    landed(output.at[1 - y], sems, 15, ypeer)
    for copy in sent:
        copy.wait_send()
    for copy in here:
        copy.wait()


def reduce_all(parts, out_rows, gx):
    outs = [jax.ShapeDtypeStruct((2,) + p.shape[1:], BF) for p in parts]
    outs += [jax.ShapeDtypeStruct(out_rows.shape, BF), jax.ShapeDtypeStruct((16, gx.shape[1], 128), BF)]
    scratch = []
    for p in parts:
        half = (p.shape[1] // 2, p.shape[2])
        scratch += [VM((4,) + half, BF)] * 3 + [VM((3,) + half, BF)]
    total = REDUCE_SENDS * len(parts)
    scratch += [pltpu.SemaphoreType.DMA((n,)) for n in (total, total, 16, 16, 2)]
    return pl.pallas_call(
        reduce_kernel,
        name="reduce_and_return",
        out_shape=tuple(outs),
        in_specs=whole(len(parts)) + any_specs(2),
        out_specs=tuple(whole(len(parts)) + any_specs(2)),
        scratch_shapes=scratch,
        compiler_params=pltpu.CompilerParams(collective_id=4, has_side_effects=True, vmem_limit_bytes=60 * MIB),
    )(*parts, out_rows, gx)


def plain_start(dealt, cot, w, y):
    arrived = lax.all_to_all(dealt, "dp", split_axis=0, concat_axis=2, tiled=True)
    rows = lax.all_gather(arrived, "seq", axis=1, tiled=True)
    cots = lax.all_gather(cot, "seq", axis=1, tiled=True)
    pick = lambda v: lax.dynamic_index_in_dim(v, y, 0, keepdims=False)
    return pick(rows), lax.all_gather(w, "dp", axis=0, tiled=True), pick(cots)


def plain_gather(ssm, att, gu, dn, c):
    every = [lax.all_gather(v, "dp", axis=0, tiled=True) for v in (ssm, att, gu, dn)]
    out = []
    for v in every[:2]:
        rows = v.shape[0] // 2
        mine = lax.all_gather(v, "seq", axis=1, tiled=True)[:, : 2 * v.shape[1]]
        out.append(lax.dynamic_slice_in_dim(mine, c * rows, rows))
    return out + every[2:]


def plain_pair(part):
    return lax.ppermute(part, "seq", [(0, 1), (1, 0), (2, 3), (3, 2)])


def plain_reduce(parts, out_rows, gx, y, c):
    reduced = []
    for p in parts:
        total = lax.psum_scatter(p.reshape(-1, p.shape[-1]), "dp", scatter_dimension=0, tiled=True)
        every = lax.all_gather(total, "seq", axis=0).astype(F32)
        reduced.append(jnp.stack([every[0] + every[2], every[1] + every[3]]))
    peer = lax.ppermute(out_rows, "seq", [(0, 2), (1, 3), (2, 0), (3, 1)])
    output = jnp.where(jnp.arange(2)[:, None, None] == y, out_rows, jnp.flip(peer, 0))
    whole_rows = lax.all_gather(gx, "seq", axis=0)
    slot = 2 * y + c
    by_pack = lax.dynamic_index_in_dim(whole_rows, c, 0, False), lax.dynamic_index_in_dim(whole_rows, c + 2, 0, False)
    both = jnp.stack([lax.dynamic_index_in_dim(v, y, 0, False) for v in by_pack])
    returned = lax.all_to_all(both, "dp", split_axis=2, concat_axis=0, tiled=True)
    return reduced, output, returned


def rms_parts(v):
    scale = lax.rsqrt(jnp.mean(v * v, axis=-1, keepdims=True) + EPS)
    return v * scale, scale


def rms_back(normed, scale, gain, grad):
    inner = grad * gain
    return scale * (inner - normed * jnp.mean(inner * normed, axis=-1, keepdims=True))


def silu(v):
    return v / (1.0 + jnp.exp(-v))


def low(v):
    return v.astype(BF)


def body(tokens, cot, seq_lengths, deal_order, in_gain, in_proj, dt_proj, dt_bias, a_log, d_skip, ssm_out, attn_out, ffn_gain, gate_up, down_proj):
    groups = lax.axis_size("dp")
    fast = groups == 8
    dp_index, seq_index = lax.axis_index("dp"), lax.axis_index("seq")
    y, c = seq_index // 2, seq_index % 2
    packs, span, width = cot.shape
    seq_len = span * lax.axis_size("seq")
    inner = MH * HP
    block = in_proj.shape[0]

    cut = lambda v, start, size: lax.dynamic_slice_in_dim(v, start, size, axis=1)
    q_start = 2 * inner + 2 * NS
    k_start = q_start + QUERY_HEADS * HEAD_WIDTH
    v_start = k_start + KEY_VALUE_HEADS * HEAD_WIDTH
    w_in = jnp.concatenate(
        [
            cut(in_proj, XW * c, XW),
            cut(in_proj, inner + XW * c, XW),
            cut(in_proj, q_start + QW * c, QW),
            cut(in_proj, k_start + HEAD_WIDTH * c, HEAD_WIDTH),
            cut(in_proj, v_start + HEAD_WIDTH * c, HEAD_WIDTH),
            in_proj[:, 2 * inner : q_start],
            cut(dt_proj, CHIP_HEADS * c, CHIP_HEADS),
            in_gain[:, None],
            ffn_gain[:, None],
            jnp.zeros((block, 128 - CHIP_HEADS - 2), BF),
        ],
        axis=1,
    )
    half_units = down_proj.shape[0] // 2
    w_gu = gate_up.reshape(block, 2, groups, 2, half_units)
    w_gu = lax.dynamic_index_in_dim(w_gu, c, 3, keepdims=False).reshape(block, FF)
    w_dn = lax.dynamic_slice_in_dim(down_proj, half_units * c, half_units, axis=0)
    w_ssm = cut(ssm_out, width // 2 * c, width // 2)
    w_att = cut(attn_out, width // 2 * c, width // 2)

    dealt = jnp.take(tokens, deal_order, axis=0)
    if fast:
        rows, w_in, cots = start_transfers(dealt, cot, w_in)
        rows, cots = rows.reshape(seq_len, width), cots.reshape(seq_len, width)
        w_in = w_in.reshape(width, COLS)
        w_ssm, w_att, w_gu, w_dn = gather_weights(w_ssm, w_att, w_gu, w_dn)
        pair = pair_swap
    else:
        rows, w_in, cots = plain_start(dealt, cot, w_in, y)
        w_ssm, w_att, w_gu, w_dn = plain_gather(w_ssm, w_att, w_gu, w_dn, c)
        pair = plain_pair

    pack = lax.dynamic_index_in_dim(deal_order, dp_index * packs + y, 0, keepdims=False)
    ends = jnp.cumsum(lax.dynamic_index_in_dim(seq_lengths, pack, 0, keepdims=False))[:-1]
    places = jnp.arange(seq_len, dtype=jnp.int32)
    seg = jnp.sum((places[:, None] >= ends[None, :]).astype(jnp.int32), axis=1)
    segc = jnp.broadcast_to(seg[:, None], (seq_len, 128))
    segr = jnp.broadcast_to(seg[None, :], (8, seq_len))
    half = HEAD_WIDTH // 2
    frequency = THETA ** (-jnp.arange(half, dtype=F32) * 2.0 / HEAD_WIDTH)
    angles = places.astype(F32)[:, None] * frequency[None, :]
    cosine = jnp.tile(jnp.cos(angles), (1, 4))
    sine = jnp.tile(jnp.concatenate([-jnp.sin(angles), jnp.sin(angles)], axis=1), (1, 2))
    own_heads = lambda v: lax.dynamic_slice_in_dim(v, CHIP_HEADS * c, CHIP_HEADS)
    par = jnp.zeros((8, 128), F32)
    par = par.at[0, :CHIP_HEADS].set(own_heads(dt_bias)).at[1, :CHIP_HEADS].set(-jnp.exp(own_heads(a_log)))
    wide = jnp.broadcast_to(jnp.repeat(own_heads(d_skip), HP)[None, :], (8, XW))
    head_of = jnp.arange(XW) // HP
    spread = (jnp.arange(128)[:, None] % 64 == head_of[None, :]).astype(BF)
    consts = (cosine, sine, segc, segr, par, spread, wide)

    x = rows.astype(F32)
    gain_in = w_in[:, T0 + CHIP_HEADS].astype(F32)[None, :]
    gain_ffn = w_in[:, T0 + CHIP_HEADS + 1].astype(F32)[None, :]
    unit_in, scale_in = rms_parts(x)
    normed = low(unit_in * gain_in)
    proj = low(dot(normed, w_in))
    gated, attn, lse, y_own, states = mixer_forward(proj, consts)
    part = low(dot(gated, w_ssm) + dot(attn, w_att))
    middle = x + (part.astype(F32) + pair(part).astype(F32))
    unit_ffn, scale_ffn = rms_parts(middle)
    normed_two = low(unit_ffn * gain_ffn)
    gu = low(dot(normed_two, w_gu)).astype(F32)
    gate, up = gu[:, : FF // 2], gu[:, FF // 2 :]
    act = low(silu(gate) * up)
    out_part = low(dot(act, w_dn)).reshape(4, span, width)
    by_core = lambda v: lax.dynamic_index_in_dim(v.reshape(2, 2, span, width), c, 1, keepdims=False)
    swap_rows = (lambda v: pair(v)) if fast else (lambda v: by_core(plain_pair(v)))
    out_rows = low(by_core(middle) + (by_core(out_part).astype(F32) + swap_rows(out_part).astype(F32)))

    g_act = low(dot(cots, w_dn, ((1,), (1,)))).astype(F32)
    grad_dn = low(dot(act, cots, ((0,), (0,))))
    sig = 1.0 / (1.0 + jnp.exp(-gate))
    g_gu = low(jnp.concatenate([g_act * up * (sig * (1.0 + gate * (1.0 - sig))), g_act * (gate * sig)], axis=1))
    grad_gu = low(dot(normed_two, g_gu, ((0,), (0,))))
    part = low(dot(g_gu, w_gu, ((1,), (1,))))
    g_two = low(part.astype(F32) + pair(part).astype(F32)).astype(F32)
    g_mid = cots.astype(F32) + rms_back(unit_ffn, scale_ffn, gain_ffn, g_two)
    grad_gain_ffn = 0.5 * jnp.sum(g_two * unit_ffn, axis=0)
    g_branch = low(g_mid)
    g_gated = low(dot(g_branch, w_ssm, ((1,), (1,))))
    g_attn = low(dot(g_branch, w_att, ((1,), (1,))))
    grad_ssm = low(dot(gated, g_branch, ((0,), (0,))))
    grad_att = low(dot(attn, g_branch, ((0,), (0,))))
    g_proj, g_par = mixer_backward(proj, consts, attn, lse, y_own, states, g_gated, g_attn)
    grad_in = dot(normed, g_proj, ((0,), (0,)))
    part = low(dot(g_proj, w_in, ((1,), (1,)))).reshape(4, span, width)
    g_h1 = low(by_core(part).astype(F32) + swap_rows(part).astype(F32)).astype(F32)
    g_x = by_core(g_mid) + rms_back(by_core(unit_in), by_core(jnp.broadcast_to(scale_in, x.shape)), gain_in, g_h1)
    g_x = low(g_x)
    grad_gain_in = jnp.sum(g_h1 * by_core(unit_in), axis=(0, 1))
    head_grads = jnp.tile(jnp.pad(g_par[:3, :CHIP_HEADS].T, ((0, block - CHIP_HEADS), (0, 0))), (groups, 1))
    extra = jnp.concatenate([grad_gain_in[:, None], grad_gain_ffn[:, None], head_grads], axis=1)
    grad_in = low(lax.dynamic_update_slice(grad_in, extra, (0, T0 + CHIP_HEADS)))

    by_block = lambda v: v.reshape(groups, -1, v.shape[-1])
    if fast:
        parts = (by_block(grad_in), by_block(grad_gu), by_block(grad_dn))
        parts += tuple(by_block(v) for v in swap_columns(grad_ssm, grad_att))
        *reduced, output, returned = reduce_all(parts, out_rows, g_x)
        reduced = [v.astype(F32) for v in reduced]
    else:
        parts = [by_block(grad_in), by_block(grad_gu), by_block(grad_dn)]
        for v in (grad_ssm, grad_att):
            both = jnp.stack([v, plain_pair(v)])
            both = jnp.where(c == 0, both, both[::-1]).reshape(-1, width)
            parts.append(by_block(cut(both, width // 2 * c, width // 2)))
        reduced, output, returned = plain_reduce(parts, out_rows, g_x, y, c)
    r_in, r_gu, r_dn, r_ssm, r_att = reduced
    both = lambda start, size: [r_in[0, :, start : start + size], r_in[1, :, start : start + size]]
    grad_in_proj = jnp.concatenate(
        both(Z0, XW)
        + both(X0, XW)
        + [r_in[0, :, B0:T0] + r_in[1, :, B0:T0]]
        + both(Q0, QW)
        + both(KV0, HEAD_WIDTH)
        + both(KV0 + HEAD_WIDTH, HEAD_WIDTH),
        axis=1,
    )
    grad_dt_proj = jnp.concatenate(both(T0, CHIP_HEADS), axis=1)
    tail = r_in[:, :, T0 + CHIP_HEADS : T0 + CHIP_HEADS + 5]
    gains = tail[0, :, :2] + tail[1, :, :2]
    heads = tail[:, :CHIP_HEADS, 2:5].reshape(MH, 3)
    grad_gate_up = jnp.stack(
        [r_gu[k].reshape(block, 2, groups, half_units) for k in range(2)], axis=3
    ).reshape(block, 2 * FF)
    side = lambda v: jnp.concatenate([v[0], v[1]], axis=1)
    return (
        output,
        jnp.take(returned, jnp.argsort(deal_order), axis=0),
        gains[:, 0],
        grad_in_proj,
        grad_dt_proj,
        heads[:, 0],
        heads[:, 1],
        heads[:, 2],
        side(r_ssm),
        side(r_att),
        gains[:, 1],
        grad_gate_up,
        r_dn.reshape(-1, width),
    )


def solution(mesh):
    return jax.shard_map(
        body,
        mesh=mesh,
        in_specs=(
            P(None, "seq", "dp"),
            P("dp", "seq", None),
            P(),
            P(),
            P("dp"),
            P("dp", None),
            P("dp", None),
            P(),
            P(),
            P(),
            P("dp", None),
            P("dp", None),
            P("dp"),
            P("dp", None),
            P("dp", None),
        ),
        out_specs=(
            P("dp", "seq", None),
            P(None, "seq", "dp"),
            P("dp"),
            P("dp", None),
            P("dp", None),
            P(),
            P(),
            P(),
            P("dp", None),
            P("dp", None),
            P("dp"),
            P("dp", None),
            P("dp", None),
        ),
        check_vma=False,
    )
```

```python
import functools

import jax
import jax.numpy as jnp
from jax import lax
from jax.experimental import pallas as pl
from jax.experimental.pallas import tpu as pltpu
from jax.sharding import PartitionSpec as P

FF = 2048
QUERY_HEADS = 8
KEY_VALUE_HEADS = 2
HEAD_WIDTH = 64
MH = 24
HP = 64
NS = 128
EPS = 1e-05
THETA = 100000000000.0
BF = jnp.bfloat16
F32 = jnp.float32
CORES = 2
CHIP_HEADS = MH // CORES
XW = CHIP_HEADS * HP
QW = QUERY_HEADS // CORES * HEAD_WIDTH
Z0, X0, Q0, KV0, B0, C0, T0 = 0, XW, 2 * XW, 2 * XW + QW, 2 * XW + QW + 128, 2 * XW + QW + 256, 2 * XW + QW + 384
COLS = T0 + 128
CHUNK = 256
QB = 256
FAR = -1e30
MIB = 1 << 20
MESH = pl.DeviceIdType.MESH
VM = pltpu.VMEM


def dot(a, b, dims=((1,), (0,)), precision=None):
    return lax.dot_general(a, b, (dims, ((), ())), precision=precision, preferred_element_type=F32)


def lanes(rows, width=128):
    return lax.broadcasted_iota(jnp.int32, (rows, width), 1)


def swap_halves(v):
    low = lanes(v.shape[0], v.shape[1]) % 64 < 32
    return jnp.where(low, pltpu.roll(v, v.shape[1] - 32, 1), pltpu.roll(v, 32, 1))


def turn(v, cosine, sine):
    return v * cosine + swap_halves(v) * sine


def turn_back(v, cosine, sine):
    return v * cosine - swap_halves(v) * sine


def widen(v, spread):
    v = jnp.where(lanes(v.shape[0]) < 64, v, 0.0)
    top = v.astype(BF)
    rest = (v - top.astype(F32)).astype(BF).astype(F32)
    both = top.astype(F32) + pltpu.roll(rest, 64, 1)
    return dot(both.astype(BF), spread)


def attn_masks(segc_ref, segr_ref, i, upto):
    rows = pl.ds(i * QB, QB)
    same = segc_ref[rows, 0:1] == segr_ref[0:1, 0:upto]
    t = lax.broadcasted_iota(jnp.int32, (QB, upto), 0) + i * QB
    u = lax.broadcasted_iota(jnp.int32, (QB, upto), 1)
    return jnp.where(same & (u <= t), 0.0, FAR)


def key_value_pairs(kv, cosine, sine):
    low = lanes(kv.shape[0]) < 64
    other = pltpu.roll(kv, 64, 1)
    kk = turn(jnp.where(low, kv, other), cosine, sine)
    vv = jnp.where(low, other, kv)
    return kk.astype(BF), vv.astype(BF)


def attention_forward(proj_ref, cos_ref, sin_ref, segc_ref, segr_ref, attn_ref, lse_ref, tick):
    seq_len = proj_ref.shape[0]
    kk, vv = key_value_pairs(proj_ref[:, KV0 : KV0 + 128].astype(F32), cos_ref[...], sin_ref[...])
    low = lanes(QB) < 64
    for i in range(seq_len // QB):
        rows = slice(i * QB, (i + 1) * QB)
        upto = (i + 1) * QB
        mask = attn_masks(segc_ref, segr_ref, i, upto)
        tops = jnp.zeros((QB, 128), F32)
        for pair in range(QW // 128):
            q = proj_ref[rows, Q0 + 128 * pair : Q0 + 128 * (pair + 1)].astype(F32)
            q = turn(q, cos_ref[rows, :], sin_ref[rows, :]) * HEAD_WIDTH**-0.5
            outs = []
            for half in range(2):
                qh = jnp.where(low if half == 0 else ~low, q, 0.0).astype(BF)
                s = dot(qh, kk[:upto], ((1,), (1,))) + mask
                top = jnp.max(s, axis=1, keepdims=True)
                e = jnp.exp(s - top)
                total = jnp.sum(e, axis=1, keepdims=True)
                outs.append(dot(e.astype(BF), vv[:upto]) / total)
                tops = jnp.where(lanes(QB) == 2 * pair + half, top + jnp.log(total), tops)
                tick()
            attn_ref[rows, 128 * pair : 128 * (pair + 1)] = jnp.where(low, outs[0], outs[1]).astype(BF)
        lse_ref[rows, :] = tops


def attention_backward(proj_ref, cos_ref, sin_ref, segc_ref, segr_ref, attn_ref, lse_ref, gattn_ref, gproj_ref, gkv, tick):
    seq_len = proj_ref.shape[0]
    kk, vv = key_value_pairs(proj_ref[:, KV0 : KV0 + 128].astype(F32), cos_ref[...], sin_ref[...])
    low = lanes(QB) < 64
    gkv[...] = jnp.zeros_like(gkv)
    pick = (lax.broadcasted_iota(jnp.int32, (QW, 128), 0) // 64 == lanes(QW)).astype(BF)
    for i in range(seq_len // QB):
        rows = slice(i * QB, (i + 1) * QB)
        upto = (i + 1) * QB
        same = segc_ref[0:upto, 0:1] == segr_ref[0:1, rows]
        t = lanes(upto, QB) + i * QB
        u = lax.broadcasted_iota(jnp.int32, (upto, QB), 0)
        mask = jnp.where(same & (u <= t), 0.0, FAR)
        weighed = gattn_ref[rows, :].astype(F32) * attn_ref[rows, :].astype(F32)
        deltas = dot(weighed.astype(BF), pick).T
        tops = lse_ref[rows, :].T
        for pair in range(QW // 128):
            cosine, sine = cos_ref[rows, :], sin_ref[rows, :]
            q = proj_ref[rows, Q0 + 128 * pair : Q0 + 128 * (pair + 1)].astype(F32)
            q = turn(q, cosine, sine) * HEAD_WIDTH**-0.5
            g = gattn_ref[rows, 128 * pair : 128 * (pair + 1)]
            grads = []
            for half in range(2):
                head = 2 * pair + half
                mine = low if half == 0 else ~low
                qh = jnp.where(mine, q, 0.0).astype(BF)
                gh = jnp.where(mine, g, jnp.zeros_like(g))
                s = dot(kk[:upto], qh, ((1,), (1,))) + mask
                p = jnp.exp(s - tops[head : head + 1, :])
                gp = dot(vv[:upto], gh, ((1,), (1,)))
                gs = (p * (gp - deltas[head : head + 1, :])).astype(BF)
                gkv[0:upto, 0:128] += dot(gs, qh)
                gkv[0:upto, 128:256] += dot(p.astype(BF), gh)
                grads.append(dot(gs, kk[:upto], ((0,), (0,))))
                tick()
            gq = jnp.where(low, grads[0], grads[1]) * HEAD_WIDTH**-0.5
            gproj_ref[rows, Q0 + 128 * pair : Q0 + 128 * (pair + 1)] = turn_back(gq, cosine, sine).astype(BF)
    gk = gkv[:, 0:128]
    gv = gkv[:, 128:256]
    gk = turn_back(gk + pltpu.roll(gk, 64, 1), cos_ref[...], sin_ref[...])
    gv = gv + pltpu.roll(gv, 64, 1)
    gproj_ref[:, KV0 : KV0 + 128] = jnp.where(lanes(seq_len) < 64, gk, gv).astype(BF)


def scan_pieces(j, proj_ref, segc_ref, segr_ref, par_ref):
    rows = pl.ds(j * CHUNK, CHUNK)
    seg = segc_ref[rows, :]
    prev = segc_ref[pl.ds(j * CHUNK - 1, 1), :] if j else jnp.full((1, 128), -1, jnp.int32)
    last = segc_ref[pl.ds(j * CHUNK + CHUNK - 1, 1), :]
    valid = lanes(CHUNK) < CHIP_HEADS
    raw = proj_ref[rows, T0 : T0 + 128].astype(F32) + par_ref[0:1, :]
    dt = jnp.where(valid, jnp.maximum(raw, 0.0) + jnp.log1p(jnp.exp(-jnp.abs(raw))), 0.0)
    decay = dt * par_ref[1:2, :]
    place = lax.broadcasted_iota(jnp.int32, (CHUNK, CHUNK), 0)
    under = (place >= lanes(CHUNK, CHUNK)).astype(F32)
    cum = dot(under, decay, precision=lax.Precision.HIGHEST)
    end = cum[CHUNK - 1 : CHUNK, :]
    from_start = jnp.where(seg == prev, jnp.exp(cum), 0.0)
    to_end = jnp.where(seg == last, jnp.exp(end - cum), 0.0)
    keep = jnp.where(last == prev, jnp.exp(end), 0.0)
    return rows, raw, dt, decay, cum, from_start, to_end, keep, under


def scan_forward(proj_ref, segc_ref, segr_ref, par_ref, spread_ref, wide_ref, gated_ref, y_ref, states_ref, state, tick):
    spread = spread_ref[...]
    state[...] = jnp.zeros_like(state)

    for j in range(proj_ref.shape[0] // CHUNK):
        rows, raw, dt, decay, cum, from_start, to_end, keep, under = scan_pieces(j, proj_ref, segc_ref, segr_ref, par_ref)
        place = lax.broadcasted_iota(jnp.int32, (CHUNK, CHUNK), 0)
        same = segc_ref[rows, 0:1] == segr_ref[0:1, rows]
        mask = jnp.where(same & (place >= lanes(CHUNK, CHUNK)), 0.0, FAR)
        cum_t = cum.T
        b = proj_ref[rows, B0 : B0 + 128]
        c = proj_ref[rows, C0 : C0 + 128]
        cb = dot(c, b, ((1,), (1,)))
        x = proj_ref[rows, X0 : X0 + XW].astype(F32)
        xdt = x * widen(dt, spread)
        xdt_low = xdt.astype(BF)
        old = state[...]
        states_ref[j] = old
        y_state = dot(c, old.astype(BF)) * widen(from_start, spread)
        low = lanes(CHUNK) < 64
        for pair in range(CHIP_HEADS // 2):
            cols = slice(128 * pair, 128 * (pair + 1))
            xp = xdt_low[:, cols]
            local = y_state[:, cols]
            for half in range(2):
                h = 2 * pair + half
                spread_h = jnp.exp(cum[:, h : h + 1] - cum_t[h : h + 1, :] + mask)
                mix = (cb * spread_h).astype(BF)
                xh = jnp.where(low if half == 0 else ~low, xp, jnp.zeros_like(xp))
                local = local + dot(mix, xh)
            y_ref[rows, cols] = local
            y = (local + x[:, cols] * wide_ref[0:1, cols]).astype(BF).astype(F32)
            z = proj_ref[rows, Z0 + 128 * pair : Z0 + 128 * (pair + 1)].astype(F32)
            gated_ref[rows, cols] = (y * (z / (1.0 + jnp.exp(-z)))).astype(BF)
            tick()
        weighted = (xdt * widen(to_end, spread)).astype(BF)
        keep_wide = widen(jnp.broadcast_to(keep, (8, 128)), spread)[0:1, :]
        state[...] = old * keep_wide + dot(b, weighted, ((0,), (0,)))


def scan_backward(proj_ref, segc_ref, segr_ref, par_ref, spread_ref, wide_ref, y_ref, states_ref, ggated_ref, gproj_ref, gpar_ref, gstate, tick):
    spread = spread_ref[...]
    gstate[...] = jnp.zeros_like(gstate)
    gpar_ref[...] = jnp.zeros_like(gpar_ref)
    chunks = proj_ref.shape[0] // CHUNK

    def narrow(v):
        top = v.astype(BF)
        rest = (v - top.astype(F32)).astype(BF)
        return dot(top, spread, ((1,), (1,))) + dot(rest, spread, ((1,), (1,)))

    for j in reversed(range(chunks)):
        rows, raw, dt, decay, cum, from_start, to_end, keep, under = scan_pieces(j, proj_ref, segc_ref, segr_ref, par_ref)
        place = lax.broadcasted_iota(jnp.int32, (CHUNK, CHUNK), 0)
        same = segc_ref[rows, 0:1] == segr_ref[0:1, rows]
        mask = jnp.where(same & (place <= lanes(CHUNK, CHUNK)), 0.0, FAR)
        cum_t = cum.T
        b = proj_ref[rows, B0 : B0 + 128]
        c = proj_ref[rows, C0 : C0 + 128]
        bc = dot(b, c, ((1,), (1,)))
        x = proj_ref[rows, X0 : X0 + XW].astype(F32)
        dt_wide = widen(dt, spread)
        xdt_low = (x * dt_wide).astype(BF)
        start_wide = widen(from_start, spread)
        end_wide = widen(to_end, spread)
        old = states_ref[j]
        gnew = gstate[...]
        z = proj_ref[rows, Z0 : Z0 + XW].astype(F32)
        gg = ggated_ref[rows, :].astype(F32)
        y_own = y_ref[rows, :]
        y = (y_own + x * wide_ref[0:1, :]).astype(BF).astype(F32)
        sig = 1.0 / (1.0 + jnp.exp(-z))
        gy_low = (gg * (z * sig)).astype(BF)
        gproj_ref[rows, Z0 : Z0 + XW] = (gg * y * (sig * (1.0 + z * (1.0 - sig)))).astype(BF)
        gy = gy_low.astype(F32)
        gx_state = end_wide * dot(b, gnew.astype(BF))
        gbc = jnp.zeros((CHUNK, CHUNK), F32)
        low = lanes(CHUNK) < 64
        gxdt = []
        for pair in range(CHIP_HEADS // 2):
            cols = slice(128 * pair, 128 * (pair + 1))
            xp, gp = xdt_low[:, cols], gy_low[:, cols]
            total = gx_state[:, cols]
            for half in range(2):
                h = 2 * pair + half
                mine = low if half == 0 else ~low
                spread_h = jnp.exp(cum_t[h : h + 1, :] - cum[:, h : h + 1] + mask)
                mix = (bc * spread_h).astype(BF)
                gh = jnp.where(mine, gp, jnp.zeros_like(gp))
                total = total + dot(mix, gh)
                gbc = gbc + dot(xp, gh, ((1,), (1,))) * spread_h
            gxdt.append(total)
            tick()
        gxdt = jnp.concatenate(gxdt, axis=1)
        gstart = (gy * start_wide).astype(BF)
        weighted = (xdt_low.astype(F32) * end_wide).astype(BF)
        gbc_low = gbc.astype(BF)
        gnew_low, old_low = gnew.astype(BF), old.astype(BF)
        gproj_ref[rows, C0 : C0 + 128] = (dot(gbc_low, b, ((0,), (0,))) + dot(gstart, old_low, ((1,), (1,)))).astype(BF)
        gproj_ref[rows, B0 : B0 + 128] = (dot(gbc_low, c) + dot(weighted, gnew_low, ((1,), (1,)))).astype(BF)
        keep_wide = widen(jnp.broadcast_to(keep, (8, 128)), spread)[0:1, :]
        kept = jnp.sum(old * gnew, axis=0, keepdims=True) * keep_wide
        gstate[...] = gnew * keep_wide + dot(c, gstart, ((0,), (0,)))
        xdt_f = xdt_low.astype(F32)
        gcum = narrow(gy * y_own) - narrow(xdt_f * gxdt)
        at_end = jnp.sum(xdt_f * gx_state, axis=0, keepdims=True) + kept
        at_end = narrow(jnp.broadcast_to(at_end, (8, XW)))[0:1, :]
        gdecay = dot(under, gcum, ((0,), (0,)), precision=lax.Precision.HIGHEST) + at_end
        gdt = narrow(gxdt * x) + gdecay * par_ref[1:2, :]
        graw = gdt / (1.0 + jnp.exp(-raw))
        graw = jnp.where(lanes(CHUNK) < CHIP_HEADS, graw, 0.0)
        gproj_ref[rows, T0 : T0 + 128] = graw.astype(BF)
        gproj_ref[rows, X0 : X0 + XW] = (gxdt * dt_wide + gy * wide_ref[0:1, :]).astype(BF)
        gpar_ref[0:1, :] += jnp.sum(graw, axis=0, keepdims=True)
        gpar_ref[1:2, :] += jnp.sum(gdecay * decay, axis=0, keepdims=True)
        skip = jnp.sum(gy * x, axis=0, keepdims=True)
        gpar_ref[2:3, :] += narrow(jnp.broadcast_to(skip, (8, XW)))[0:1, :]


class Ticker:
    def __init__(self, steps, ticks):
        self.steps, self.ticks, self.calls, self.done = steps, ticks, 0, 0

    def __call__(self):
        self.calls += 1
        while self.done < len(self.steps) and self.done * self.ticks < self.calls * len(self.steps):
            self.steps[self.done]()
            self.done += 1

    def drain(self):
        while self.done < len(self.steps):
            self.steps[self.done]()
            self.done += 1


def whole(n):
    return [pl.BlockSpec(memory_space=VM)] * n


def place():
    d, s = lax.axis_index("dp"), lax.axis_index("seq")
    return d // 2, d % 2, s // 2, s % 2


def device(z, x, y, c):
    return (2 * z + x, 2 * y + c)


def greet(peers):
    barrier = pltpu.get_barrier_semaphore()
    for peer in peers:
        pl.semaphore_signal(barrier, inc=1, device_id=peer, device_id_type=MESH)
    pl.semaphore_wait(barrier, len(peers))


def send(src, dst, sems, k, target):
    copy = pltpu.make_async_remote_copy(
        src_ref=src, dst_ref=dst, send_sem=sems[0].at[k], recv_sem=sems[1].at[k], device_id=target, device_id_type=MESH
    )
    copy.start()
    return copy


def landed(dst, sems, k, target):
    pltpu.make_async_remote_copy(
        src_ref=dst, dst_ref=dst, send_sem=sems[0].at[k], recv_sem=sems[1].at[k], device_id=target, device_id_type=MESH
    ).wait_recv()


ARRAY_SENDS = 13
CORNER_X = 3


class Gather:
    def __init__(self, src, dst, sems, base, local_sem):
        self.src, self.dst, self.sems, self.base = src, dst, sems, base
        self.local_sem = local_sem
        self.z, self.x, self.y, self.c = place()
        half = src.shape[0] // 2
        self.mine = pl.ds(self.y * half, half)
        self.other = pl.ds((1 - self.y) * half, half)
        self.sent = []
        self.xpeer = device(self.z, 1 - self.x, self.y, self.c)
        self.ypeer = device(self.z, self.x, 1 - self.y, self.c)

    def block(self, r, x, rows):
        return self.dst.at[2 * (self.z ^ r) + x, rows]

    def push(self, k, ref, target, dst=None):
        self.sent.append(send(ref, ref if dst is None else dst, self.sems, self.base + k, target))

    def start(self):
        own = 2 * self.z + self.x
        self.local = pltpu.make_async_copy(self.src, self.dst.at[own], self.local_sem)
        self.local.start()
        for r in (1, 2, 3):
            target = device(self.z ^ r, self.x, self.y, self.c)
            self.push(r - 1, self.src.at[self.mine], target, self.dst.at[own, self.mine])
        self.push(3, self.src, self.xpeer, self.dst.at[own])

    def cross(self):
        landed(self.block(0, 1 - self.x, slice(None)), self.sems, self.base + 3, self.xpeer)
        self.push(4, self.block(0, 1 - self.x, self.mine), device(self.z ^ 1, self.x, self.y, self.c))

    def forward(self, r):
        ref = self.block(r, self.x, self.mine)
        landed(ref, self.sems, self.base + r - 1, self.xpeer)
        self.push(6 + r, ref, self.ypeer)
        if r > 1:
            self.push(3 + r, ref, self.xpeer)

    def corner(self, r):
        if r == CORNER_X:
            ref = self.block(r, self.x, self.other)
            landed(ref, self.sems, self.base + 6 + r, self.ypeer)
            self.push(9 + r, ref, self.xpeer)
        else:
            ref = self.block(r, 1 - self.x, self.mine)
            landed(ref, self.sems, self.base + 3 + r, self.xpeer)
            self.push(9 + r, ref, self.ypeer)

    def arrive(self):
        for r in (1, 2, 3):
            if r == CORNER_X:
                landed(self.block(r, 1 - self.x, self.mine), self.sems, self.base + 3 + r, self.xpeer)
            else:
                landed(self.block(r, self.x, self.other), self.sems, self.base + 6 + r, self.ypeer)
            landed(self.block(r, 1 - self.x, self.other), self.sems, self.base + 9 + r, self.ypeer)
        self.local.wait()

    def finish(self):
        for copy in self.sent:
            copy.wait_send()


def gather_steps(gathers):
    def one(g):
        return [
            lambda: g.forward(1),
            g.cross,
            lambda: g.forward(2),
            lambda: g.forward(3),
        ]

    def corners(g):
        return [lambda r=r: g.corner(r) for r in (2, 3, 1)]

    steps = []
    count = len(gathers)
    for k in range(count + 1):
        if k + 1 < count:
            steps.append(gathers[k + 1].start)
        ahead = one(gathers[k]) if k < count else []
        behind = corners(gathers[k - 1]) if k else []
        steps += ahead[:2] + behind[:1] + ahead[2:3] + behind[1:2] + ahead[3:] + behind[2:]
    return steps


def reduce_steps(sums, partner):
    def early(s):
        return [
            lambda: s.relay(1),
            lambda: s.relay(2),
            lambda: s.root(1),
            lambda: s.relay(3),
            s.cross,
            lambda: s.relay(0),
        ]

    def late(s):
        return [lambda r=r: s.root(r) for r in (2, 3, 0)]

    steps = []
    for k in range(len(sums) + 3):
        if k < len(sums):
            if k + 1 < len(sums):
                steps.append(sums[k + 1].start)
            steps += early(sums[k])
        if 0 <= k - 1 < len(sums):
            steps += late(sums[k - 1])
        if 0 <= k - 2 < len(sums):
            steps.append(lambda s=sums[k - 2]: s.total(partner))
        if 0 <= k - 3 < len(sums):
            steps.append(lambda s=sums[k - 3]: s.spread(partner))
    return steps


def chip_peers():
    z, x, y, c = place()
    peers = [device(z ^ r, x, y, c) for r in (1, 2, 3)]
    peers += [device(z, 1 - x, y, c), device(z, x, 1 - y, c), device(z, x, y, 1 - c)]
    return peers


def start_kernel(dealt, w, rows, weights, dsend, drecv, wsend, wrecv, local):
    z, x, y, c = place()
    own = 2 * z + x
    slot = 2 * y + c
    partner = device(z, x, y, 1 - c)
    others = [(r, i, j) for r in range(4) for i in range(2) for j in range(2) if r or i or j]
    targets = [device(z ^ r, x ^ i, y ^ j, c) for r, i, j in others]
    greet(targets + [partner])
    sems = (dsend, drecv)
    gather = Gather(w, weights, (wsend, wrecv), 0, local.at[0])
    columns = lambda d: pl.ds(pl.multiple_of(d * 128, 128), 128)
    sent = []
    gather.start()
    for k, (r, i, j) in enumerate(others):
        pack = 2 * (2 * (z ^ r) + (x ^ i)) + (y ^ j)
        sent.append(send(dealt.at[pack], rows.at[slot, :, columns(own)], sems, k, targets[k]))
    here = pltpu.make_async_copy(dealt.at[2 * own + y], rows.at[slot, :, columns(own)], local.at[1])
    here.start()
    gather.forward(1)
    gather.cross()
    gather.forward(2)
    gather.forward(3)
    here.wait()
    for same_y in (True, False):
        for k, (r, i, j) in enumerate(others):
            if (j == 0) == same_y:
                src = 2 * (z ^ r) + (x ^ i)
                landed(rows.at[2 * (y ^ j) + c, :, columns(src)], sems, k, targets[k])
        ref = rows.at[slot if same_y else 2 * (1 - y) + c]
        sent.append(send(ref, ref, sems, 15 if same_y else 16, partner))
    for r in (1, 2, 3):
        gather.corner(r)
    landed(rows.at[2 * y + 1 - c], sems, 15, partner)
    landed(rows.at[2 * (1 - y) + 1 - c], sems, 16, partner)
    gather.arrive()
    for copy in sent:
        copy.wait_send()
    gather.finish()


def any_specs(n):
    return [pl.BlockSpec(memory_space=pl.ANY)] * n


def start_transfers(dealt, w):
    packs, span, width = dealt.shape
    return pl.pallas_call(
        start_kernel,
        name="deal_and_gather",
        out_shape=(
            jax.ShapeDtypeStruct((4, span, 8 * width), BF),
            jax.ShapeDtypeStruct((8,) + w.shape, BF),
        ),
        in_specs=whole(2),
        out_specs=tuple(any_specs(2)),
        scratch_shapes=[
            pltpu.SemaphoreType.DMA((17,)),
            pltpu.SemaphoreType.DMA((17,)),
            pltpu.SemaphoreType.DMA((ARRAY_SENDS,)),
            pltpu.SemaphoreType.DMA((ARRAY_SENDS,)),
            pltpu.SemaphoreType.DMA((2,)),
        ],
        compiler_params=pltpu.CompilerParams(collective_id=0, has_side_effects=True),
    )(dealt, w)


class Cotangents:
    def __init__(self, src, dst, sems, local_sem):
        self.src, self.dst, self.sems, self.local_sem = src, dst, sems, local_sem
        self.z, self.x, self.y, self.c = place()
        self.slot = 2 * self.y + self.c
        self.partner = device(self.z, self.x, self.y, 1 - self.c)
        self.ypeer = device(self.z, self.x, 1 - self.y, self.c)

    def start(self):
        src, dst = self.src, self.dst
        self.sent = [
            send(src.at[1 - self.y], dst.at[self.slot], self.sems, 0, self.ypeer),
            send(src.at[self.y], dst.at[self.slot], self.sems, 1, self.partner),
        ]
        self.local = pltpu.make_async_copy(src.at[self.y], dst.at[self.slot], self.local_sem)
        self.local.start()

    def forward(self):
        ref = self.dst.at[2 * (1 - self.y) + self.c]
        landed(ref, self.sems, 0, self.ypeer)
        self.sent.append(send(ref, ref, self.sems, 2, self.partner))

    def arrive(self):
        landed(self.dst.at[2 * self.y + 1 - self.c], self.sems, 1, self.partner)
        landed(self.dst.at[2 * (1 - self.y) + 1 - self.c], self.sems, 2, self.partner)
        self.local.wait()

    def finish(self):
        for copy in self.sent:
            copy.wait_send()


class Halves:
    def __init__(self, gather, dst, sems, base, local_sem):
        self.gather, self.dst, self.sems, self.base, self.local_sem = gather, dst, sems, base, local_sem
        z, x, y, self.c = place()
        self.partner = device(z, x, y, 1 - self.c)

    def columns(self, k):
        half = self.gather.src.shape[1]
        return self.dst.at[:, :, pl.ds(pl.multiple_of(k * half, 128), half)]

    def start(self):
        src, c = self.gather.dst, self.c
        self.gather.arrive()
        self.local = pltpu.make_async_copy(src.at[pl.ds(4 * c, 4)], self.columns(c), self.local_sem)
        self.local.start()
        self.sent = send(src.at[pl.ds(4 * (1 - c), 4)], self.columns(c), self.sems, self.base, self.partner)

    def arrive(self):
        landed(self.columns(1 - self.c), self.sems, self.base, self.partner)
        self.local.wait()
        self.sent.wait_send()


def forward_kernel(*refs):
    proj, cosine, sine, segc, segr, par, spread, wide, cot, *refs = refs
    ssm, att, gu, dn, *refs = refs
    gated, attn, lse, y_own, states, gcot, ssm_own, att_own, gu_all, dn_all, *refs = refs
    state, ssm_all, att_all, gsend, grecv, csend, crecv, local = refs
    greet(chip_peers())
    sems = (gsend, grecv)
    pairs = ((ssm, ssm_all), (att, att_all), (gu, gu_all), (dn, dn_all))
    gathers = [Gather(a, b, sems, ARRAY_SENDS * i, local.at[i]) for i, (a, b) in enumerate(pairs)]
    cots = Cotangents(cot, gcot, (csend, crecv), local.at[6])
    halves = [Halves(g, out, (csend, crecv), 3 + i, local.at[4 + i]) for i, (g, out) in enumerate(zip(gathers, (ssm_own, att_own)))]
    gathers[0].start()
    cots.start()
    ticker = Ticker(gather_steps(gathers) + [cots.forward], 40)
    attention_forward(proj, cosine, sine, segc, segr, attn, lse, ticker)
    scan_forward(proj, segc, segr, par, spread, wide, gated, y_own, states, state, ticker)
    ticker.drain()
    for h in halves:
        h.start()
    for g in gathers[2:]:
        g.arrive()
    cots.arrive()
    for h in halves:
        h.arrive()
    for g in gathers:
        g.finish()
    cots.finish()


def forward_and_gather(proj, consts, cot, shards):
    seq_len = proj.shape[0]
    chunks = seq_len // CHUNK
    total = 4 * ARRAY_SENDS
    ssm, att, gu, dn = shards
    outs = pl.pallas_call(
        forward_kernel,
        name="mixer_forward_and_gather",
        out_shape=(
            jax.ShapeDtypeStruct((seq_len, XW), BF),
            jax.ShapeDtypeStruct((seq_len, QW), BF),
            jax.ShapeDtypeStruct((seq_len, 128), F32),
            jax.ShapeDtypeStruct((seq_len, XW), F32),
            jax.ShapeDtypeStruct((chunks, NS, XW), F32),
            jax.ShapeDtypeStruct((4,) + cot.shape[1:], BF),
            jax.ShapeDtypeStruct((4, ssm.shape[0], 2 * ssm.shape[1]), BF),
            jax.ShapeDtypeStruct((4, att.shape[0], 2 * att.shape[1]), BF),
            jax.ShapeDtypeStruct((8,) + gu.shape, BF),
            jax.ShapeDtypeStruct((8,) + dn.shape, BF),
        ),
        in_specs=whole(13),
        out_specs=tuple(whole(5) + any_specs(5)),
        scratch_shapes=[
            VM((NS, XW), F32),
            VM((8,) + ssm.shape, BF),
            VM((8,) + att.shape, BF),
            pltpu.SemaphoreType.DMA((total,)),
            pltpu.SemaphoreType.DMA((total,)),
            pltpu.SemaphoreType.DMA((5,)),
            pltpu.SemaphoreType.DMA((5,)),
            pltpu.SemaphoreType.DMA((7,)),
        ],
        compiler_params=pltpu.CompilerParams(collective_id=1, has_side_effects=True, vmem_limit_bytes=56 * MIB),
    )(proj, *consts, cot, ssm, att, gu, dn)
    return outs[:5], outs[5].reshape(seq_len, -1), [v.reshape(-1, v.shape[-1]) for v in outs[6:]]


def plain_forward_kernel(proj, cosine, sine, segc, segr, par, spread, wide, gated, attn, lse, y_own, states, state):
    tick = Ticker([], 1)
    attention_forward(proj, cosine, sine, segc, segr, attn, lse, tick)
    scan_forward(proj, segc, segr, par, spread, wide, gated, y_own, states, state, tick)


def mixer_forward(proj, consts):
    seq_len = proj.shape[0]
    return pl.pallas_call(
        plain_forward_kernel,
        name="mixer_forward",
        out_shape=(
            jax.ShapeDtypeStruct((seq_len, XW), BF),
            jax.ShapeDtypeStruct((seq_len, QW), BF),
            jax.ShapeDtypeStruct((seq_len, 128), F32),
            jax.ShapeDtypeStruct((seq_len, XW), F32),
            jax.ShapeDtypeStruct((seq_len // CHUNK, NS, XW), F32),
        ),
        in_specs=whole(8),
        out_specs=tuple(whole(5)),
        scratch_shapes=[VM((NS, XW), F32)],
        compiler_params=pltpu.CompilerParams(vmem_limit_bytes=56 * MIB),
    )(proj, *consts)


def pair_kernel(blocks, part, got, sems_out, sems_in):
    z, x, y, c = place()
    partner = device(z, x, y, 1 - c)
    greet([partner])
    sems = (sems_out, sems_in)
    if blocks:
        sent = [send(part.at[2 * k + 1 - c], got.at[k], sems, k, partner) for k in range(2)]
    else:
        sent = [send(part, got, sems, 0, partner)]
    for copy in sent:
        copy.wait()


def pair_swap(part):
    blocks = part.ndim == 3
    return pl.pallas_call(
        functools.partial(pair_kernel, blocks),
        name="pair_swap_rows" if blocks else "pair_swap",
        out_shape=jax.ShapeDtypeStruct(((2,) + part.shape[1:]) if blocks else part.shape, BF),
        in_specs=any_specs(1),
        out_specs=any_specs(1)[0],
        scratch_shapes=[pltpu.SemaphoreType.DMA((2,)), pltpu.SemaphoreType.DMA((2,))],
        compiler_params=pltpu.CompilerParams(collective_id=3 if blocks else 2, has_side_effects=True),
    )(part)


def columns_kernel(ssm, att, ssm_all, att_all, sems_out, sems_in, local):
    z, x, y, c = place()
    partner = device(z, x, y, 1 - c)
    greet([partner])
    copies = []
    for i, (src, dst) in enumerate(((ssm, ssm_all), (att, att_all))):
        half = src.shape[2] // 2
        columns = lambda k: src.at[:, :, pl.ds(pl.multiple_of(k * half, 128), half)]
        here = pltpu.make_async_copy(columns(c), dst.at[pl.ds(4 * c, 4)], local.at[i])
        here.start()
        copies += [here, send(columns(1 - c), dst.at[pl.ds(4 * c, 4)], (sems_out, sems_in), i, partner)]
    for i, dst in enumerate((ssm_all, att_all)):
        copies[2 * i].wait()
        copies[2 * i + 1].wait_send()
        landed(dst.at[pl.ds(4 * (1 - c), 4)], (sems_out, sems_in), i, partner)


def swap_columns(ssm, att):
    args = [v.reshape(4, -1, v.shape[-1]) for v in (ssm, att)]
    return pl.pallas_call(
        columns_kernel,
        name="swap_columns",
        out_shape=tuple(jax.ShapeDtypeStruct((8, v.shape[1], v.shape[2] // 2), BF) for v in args),
        in_specs=whole(2),
        out_specs=tuple(any_specs(2)),
        scratch_shapes=[pltpu.SemaphoreType.DMA((2,))] * 3,
        compiler_params=pltpu.CompilerParams(collective_id=5, has_side_effects=True),
    )(*args)


class Reduce:
    def __init__(self, part, out, far, near_x, near_y, deep, sems, base):
        self.part, self.out, self.far, self.near_x, self.near_y, self.deep = part, out, far, near_x, near_y, deep
        self.sems, self.base = sems, base
        self.z, self.x, self.y, self.c = place()
        half = part.shape[1] // 2
        self.mine = pl.ds(self.y * half, half)
        self.other = pl.ds((1 - self.y) * half, half)
        self.xpeer = device(self.z, 1 - self.x, self.y, self.c)
        self.ypeer = device(self.z, self.x, 1 - self.y, self.c)
        self.sent = []

    def piece(self, r, x, rows):
        return self.part.at[2 * (self.z ^ r) + x, rows]

    def push(self, k, src, dst, target):
        self.sent.append(send(src, dst, self.sems, self.base + k, target))

    def start(self):
        for r in (1, 2, 3, 0):
            far = self.piece(r, 1 - self.x, self.other)
            self.push(r, far, self.far.at[r], self.ypeer if r == 1 else self.xpeer)
        self.push(9, self.piece(1, self.x, self.other), self.near_y.at[1], self.ypeer)
        for r in (2, 3):
            self.push(4 + r, self.piece(r, 1 - self.x, self.mine), self.near_x.at[r], self.xpeer)

    def relay(self, r):
        landed(self.far.at[r], self.sems, self.base + r, self.xpeer)
        own = self.piece(r, 1 - self.x, self.mine) if r == 1 else self.piece(r, self.x, self.other)
        self.far[r] = (own[...].astype(F32) + self.far[r].astype(F32)).astype(BF)
        if r == 1:
            self.push(5, self.far.at[1], self.near_x.at[1], device(self.z ^ 1, self.x, self.y, self.c))
        else:
            self.push(8 + r, self.far.at[r], self.near_y.at[r], self.ypeer)

    def cross(self):
        landed(self.near_x.at[1], self.sems, self.base + 5, self.xpeer)
        own = self.piece(0, 1 - self.x, self.mine)[...].astype(F32)
        self.near_x[1] = (own + self.near_x[1].astype(F32)).astype(BF)
        self.push(4, self.near_x.at[1], self.near_x.at[0], self.xpeer)

    def root(self, r):
        landed(self.near_y.at[r], self.sems, self.base + 8 + r, self.ypeer)
        total = self.piece(r, self.x, self.mine)[...].astype(F32) + self.near_y[r].astype(F32)
        if r != 1:
            landed(self.near_x.at[r], self.sems, self.base + 4 + r, self.xpeer)
            total = total + self.near_x[r].astype(F32)
        self.near_y[r] = total.astype(BF)
        if r:
            target = device(self.z ^ r, self.x, self.y, self.c)
            self.push(11 + r, self.near_y.at[r], self.deep.at[r - 1], target)

    def total(self, partner):
        for r in (1, 2, 3):
            landed(self.deep.at[r - 1], self.sems, self.base + 11 + r, self.xpeer)
        total = self.near_y[0].astype(F32) + self.deep[0].astype(F32)
        total = total + (self.deep[1].astype(F32) + self.deep[2].astype(F32))
        self.out[self.c, self.mine] = total.astype(BF)
        ref = self.out.at[self.c, self.mine]
        self.push(15, ref, ref, self.ypeer)
        self.push(16, ref, ref, partner)

    def spread(self, partner):
        ref = self.out.at[self.c, self.other]
        landed(ref, self.sems, self.base + 15, self.ypeer)
        self.push(17, ref, ref, partner)

    def finish(self, partner):
        landed(self.out.at[1 - self.c, self.mine], self.sems, self.base + 16, partner)
        landed(self.out.at[1 - self.c, self.other], self.sems, self.base + 17, partner)
        for copy in self.sent:
            copy.wait_send()


REDUCE_SENDS = 18


def reduce_buffers(parts):
    scratch = []
    for p in parts:
        half = (p.shape[1] // 2, p.shape[2])
        scratch += [VM((4,) + half, BF)] * 3 + [VM((3,) + half, BF)]
    total = REDUCE_SENDS * len(parts)
    return scratch + [pltpu.SemaphoreType.DMA((total,))] * 2


def backward_kernel(*refs):
    proj, cosine, sine, segc, segr, par, spread, wide, attn, lse, y_own, states, ggated, gattn, *refs = refs
    parts, out_rows, (gproj, gpar), reduced, output, refs = refs[:4], refs[4], refs[5:7], refs[7:11], refs[11], refs[12:]
    gkv, gstate, *refs = refs
    buffers, (rsend, rrecv, osend, orecv, local) = [refs[4 * i : 4 * i + 4] for i in range(4)], refs[16:]
    z, x, y, c = place()
    partner = device(z, x, y, 1 - c)
    ypeer = device(z, x, 1 - y, c)
    greet(chip_peers())
    sums = [Reduce(p, o, *b, (rsend, rrecv), REDUCE_SENDS * k) for k, (p, o, b) in enumerate(zip(parts, reduced, buffers))]
    sums[0].start()
    sent = send(out_rows.at[1 - y], output.at[y], (osend, orecv), 0, ypeer)
    here = pltpu.make_async_copy(out_rows.at[y], output.at[y], local.at[0])
    here.start()
    ticker = Ticker(reduce_steps(sums, partner), 40)
    attention_backward(proj, cosine, sine, segc, segr, attn, lse, gattn, gproj, gkv, ticker)
    scan_backward(proj, segc, segr, par, spread, wide, y_own, states, ggated, gproj, gpar, gstate, ticker)
    ticker.drain()
    for s in sums:
        s.finish(partner)
    landed(output.at[1 - y], (osend, orecv), 0, ypeer)
    sent.wait_send()
    here.wait()


def backward_and_reduce(proj, consts, saved, ggated, gattn, parts, out_rows):
    seq_len = proj.shape[0]
    outs = [jax.ShapeDtypeStruct((seq_len, COLS), BF), jax.ShapeDtypeStruct((8, 128), F32)]
    outs += [jax.ShapeDtypeStruct((2,) + p.shape[1:], BF) for p in parts]
    outs += [jax.ShapeDtypeStruct(out_rows.shape, BF)]
    scratch = [VM((seq_len, 256), F32), VM((NS, XW), F32)] + reduce_buffers(parts)
    scratch += [pltpu.SemaphoreType.DMA((1,))] * 3
    return pl.pallas_call(
        backward_kernel,
        name="mixer_backward_and_reduce",
        out_shape=tuple(outs),
        in_specs=whole(14 + len(parts) + 1),
        out_specs=tuple(whole(2 + len(parts)) + any_specs(1)),
        scratch_shapes=scratch,
        compiler_params=pltpu.CompilerParams(collective_id=6, has_side_effects=True, vmem_limit_bytes=62 * MIB),
    )(proj, *consts, *saved, ggated, gattn, *parts, out_rows)


def plain_backward_kernel(proj, cosine, sine, segc, segr, par, spread, wide, attn, lse, y_own, states, ggated, gattn, gproj, gpar, gkv, gstate):
    tick = Ticker([], 1)
    attention_backward(proj, cosine, sine, segc, segr, attn, lse, gattn, gproj, gkv, tick)
    scan_backward(proj, segc, segr, par, spread, wide, y_own, states, ggated, gproj, gpar, gstate, tick)


def mixer_backward(proj, consts, saved, ggated, gattn):
    seq_len = proj.shape[0]
    return pl.pallas_call(
        plain_backward_kernel,
        name="mixer_backward",
        out_shape=(
            jax.ShapeDtypeStruct((seq_len, COLS), BF),
            jax.ShapeDtypeStruct((8, 128), F32),
        ),
        in_specs=whole(14),
        out_specs=tuple(whole(2)),
        scratch_shapes=[VM((seq_len, 256), F32), VM((NS, XW), F32)],
        compiler_params=pltpu.CompilerParams(vmem_limit_bytes=56 * MIB),
    )(proj, *consts, *saved, ggated, gattn)


def end_kernel(part, gx, reduced, returned, far, near_x, near_y, deep, rsend, rrecv, dsend, drecv, local):
    z, x, y, c = place()
    own = 2 * z + x
    slot = 2 * own + y
    partner = device(z, x, y, 1 - c)
    others = [(r, i, j) for r in range(4) for i in range(2) for j in range(2) if r or i or j]
    targets = [device(z ^ r, x ^ i, y ^ j, c) for r, i, j in others]
    greet(targets + [partner])
    sums = [Reduce(part, reduced, far, near_x, near_y, deep, (rsend, rrecv), 0)]
    sums[0].start()
    columns = lambda d: pl.ds(pl.multiple_of(d * 128, 128), 128)
    sems = (dsend, drecv)
    here = pltpu.make_async_copy(gx.at[y, :, columns(own)], returned.at[slot], local.at[0])
    here.start()
    sent = []
    for k, (r, i, j) in enumerate(others):
        d = 2 * (z ^ r) + (x ^ i)
        sent.append(send(gx.at[y ^ j, :, columns(d)], returned.at[slot], sems, k, targets[k]))
    for step in reduce_steps(sums, partner):
        step()
    for s in sums:
        s.finish(partner)
    for k, (r, i, j) in enumerate(others):
        landed(returned.at[2 * (2 * (z ^ r) + (x ^ i)) + (y ^ j)], sems, k, targets[k])
    for copy in sent:
        copy.wait_send()
    here.wait()


def end_transfers(part, gx):
    return pl.pallas_call(
        end_kernel,
        name="reduce_and_return",
        out_shape=(
            jax.ShapeDtypeStruct((2,) + part.shape[1:], BF),
            jax.ShapeDtypeStruct((16, gx.shape[1], 128), BF),
        ),
        in_specs=whole(2),
        out_specs=tuple(whole(1) + any_specs(1)),
        scratch_shapes=reduce_buffers([part]) + [pltpu.SemaphoreType.DMA((n,)) for n in (15, 15, 1)],
        compiler_params=pltpu.CompilerParams(collective_id=4, has_side_effects=True, vmem_limit_bytes=60 * MIB),
    )(part, gx)


def plain_start(dealt, cot, w, y):
    arrived = lax.all_to_all(dealt, "dp", split_axis=0, concat_axis=2, tiled=True)
    rows = lax.all_gather(arrived, "seq", axis=1, tiled=True)
    cots = lax.all_gather(cot, "seq", axis=1, tiled=True)
    pick = lambda v: lax.dynamic_index_in_dim(v, y, 0, keepdims=False)
    return pick(rows), lax.all_gather(w, "dp", axis=0, tiled=True), pick(cots)


def plain_gather(ssm, att, gu, dn, c):
    every = [lax.all_gather(v, "dp", axis=0, tiled=True) for v in (ssm, att, gu, dn)]
    out = []
    for v in every[:2]:
        rows = v.shape[0] // 2
        mine = lax.all_gather(v, "seq", axis=1, tiled=True)[:, : 2 * v.shape[1]]
        out.append(lax.dynamic_slice_in_dim(mine, c * rows, rows))
    return out + every[2:]


def plain_pair(part):
    return lax.ppermute(part, "seq", [(0, 1), (1, 0), (2, 3), (3, 2)])


def plain_reduce(parts, out_rows, gx, y, c):
    reduced = []
    for p in parts:
        total = lax.psum_scatter(p.reshape(-1, p.shape[-1]), "dp", scatter_dimension=0, tiled=True)
        every = lax.all_gather(total, "seq", axis=0).astype(F32)
        reduced.append(jnp.stack([every[0] + every[2], every[1] + every[3]]))
    peer = lax.ppermute(out_rows, "seq", [(0, 2), (1, 3), (2, 0), (3, 1)])
    output = jnp.where(jnp.arange(2)[:, None, None] == y, out_rows, jnp.flip(peer, 0))
    whole_rows = lax.all_gather(gx, "seq", axis=0)
    slot = 2 * y + c
    by_pack = lax.dynamic_index_in_dim(whole_rows, c, 0, False), lax.dynamic_index_in_dim(whole_rows, c + 2, 0, False)
    both = jnp.stack([lax.dynamic_index_in_dim(v, y, 0, False) for v in by_pack])
    returned = lax.all_to_all(both, "dp", split_axis=2, concat_axis=0, tiled=True)
    return reduced, output, returned


def rms_parts(v):
    scale = lax.rsqrt(jnp.mean(v * v, axis=-1, keepdims=True) + EPS)
    return v * scale, scale


def rms_back(normed, scale, gain, grad):
    inner = grad * gain
    return scale * (inner - normed * jnp.mean(inner * normed, axis=-1, keepdims=True))


def silu(v):
    return v / (1.0 + jnp.exp(-v))


def low(v):
    return v.astype(BF)


def body(tokens, cot, seq_lengths, deal_order, in_gain, in_proj, dt_proj, dt_bias, a_log, d_skip, ssm_out, attn_out, ffn_gain, gate_up, down_proj):
    groups = lax.axis_size("dp")
    fast = groups == 8
    dp_index, seq_index = lax.axis_index("dp"), lax.axis_index("seq")
    y, c = seq_index // 2, seq_index % 2
    packs, span, width = cot.shape
    seq_len = span * lax.axis_size("seq")
    inner = MH * HP
    block = in_proj.shape[0]

    cut = lambda v, start, size: lax.dynamic_slice_in_dim(v, start, size, axis=1)
    q_start = 2 * inner + 2 * NS
    k_start = q_start + QUERY_HEADS * HEAD_WIDTH
    v_start = k_start + KEY_VALUE_HEADS * HEAD_WIDTH
    w_in = jnp.concatenate(
        [
            cut(in_proj, XW * c, XW),
            cut(in_proj, inner + XW * c, XW),
            cut(in_proj, q_start + QW * c, QW),
            cut(in_proj, k_start + HEAD_WIDTH * c, HEAD_WIDTH),
            cut(in_proj, v_start + HEAD_WIDTH * c, HEAD_WIDTH),
            in_proj[:, 2 * inner : q_start],
            cut(dt_proj, CHIP_HEADS * c, CHIP_HEADS),
            in_gain[:, None],
            ffn_gain[:, None],
            jnp.zeros((block, 128 - CHIP_HEADS - 2), BF),
        ],
        axis=1,
    )
    half_units = down_proj.shape[0] // 2
    w_gu = gate_up.reshape(block, 2, groups, 2, half_units)
    w_gu = lax.dynamic_index_in_dim(w_gu, c, 3, keepdims=False).reshape(block, FF)
    w_dn = lax.dynamic_slice_in_dim(down_proj, half_units * c, half_units, axis=0)
    w_ssm = cut(ssm_out, width // 2 * c, width // 2)
    w_att = cut(attn_out, width // 2 * c, width // 2)

    dealt = jnp.take(tokens, deal_order, axis=0)
    if fast:
        rows, w_in = start_transfers(dealt, w_in)
        rows, w_in = rows.reshape(seq_len, width), w_in.reshape(width, COLS)
        pair = pair_swap
    else:
        rows, w_in, cots = plain_start(dealt, cot, w_in, y)
        w_ssm, w_att, w_gu, w_dn = plain_gather(w_ssm, w_att, w_gu, w_dn, c)
        pair = plain_pair

    pack = lax.dynamic_index_in_dim(deal_order, dp_index * packs + y, 0, keepdims=False)
    ends = jnp.cumsum(lax.dynamic_index_in_dim(seq_lengths, pack, 0, keepdims=False))[:-1]
    places = jnp.arange(seq_len, dtype=jnp.int32)
    seg = jnp.sum((places[:, None] >= ends[None, :]).astype(jnp.int32), axis=1)
    segc = jnp.broadcast_to(seg[:, None], (seq_len, 128))
    segr = jnp.broadcast_to(seg[None, :], (8, seq_len))
    half = HEAD_WIDTH // 2
    frequency = THETA ** (-jnp.arange(half, dtype=F32) * 2.0 / HEAD_WIDTH)
    angles = places.astype(F32)[:, None] * frequency[None, :]
    cosine = jnp.tile(jnp.cos(angles), (1, 4))
    sine = jnp.tile(jnp.concatenate([-jnp.sin(angles), jnp.sin(angles)], axis=1), (1, 2))
    own_heads = lambda v: lax.dynamic_slice_in_dim(v, CHIP_HEADS * c, CHIP_HEADS)
    par = jnp.zeros((8, 128), F32)
    par = par.at[0, :CHIP_HEADS].set(own_heads(dt_bias)).at[1, :CHIP_HEADS].set(-jnp.exp(own_heads(a_log)))
    wide = jnp.broadcast_to(jnp.repeat(own_heads(d_skip), HP)[None, :], (8, XW))
    head_of = jnp.arange(XW) // HP
    spread = (jnp.arange(128)[:, None] % 64 == head_of[None, :]).astype(BF)
    consts = (cosine, sine, segc, segr, par, spread, wide)

    x = rows.astype(F32)
    gain_in = w_in[:, T0 + CHIP_HEADS].astype(F32)[None, :]
    gain_ffn = w_in[:, T0 + CHIP_HEADS + 1].astype(F32)[None, :]
    unit_in, scale_in = rms_parts(x)
    normed = low(unit_in * gain_in)
    proj = low(dot(normed, w_in))
    if fast:
        (gated, *saved), cots, weights = forward_and_gather(proj, consts, cot, (w_ssm, w_att, w_gu, w_dn))
        w_ssm, w_att, w_gu, w_dn = weights
    else:
        gated, *saved = mixer_forward(proj, consts)
    attn = saved[0]
    part = low(dot(gated, w_ssm) + dot(attn, w_att))
    middle = x + (part.astype(F32) + pair(part).astype(F32))
    unit_ffn, scale_ffn = rms_parts(middle)
    normed_two = low(unit_ffn * gain_ffn)
    gu = low(dot(normed_two, w_gu)).astype(F32)
    gate, up = gu[:, : FF // 2], gu[:, FF // 2 :]
    act = low(silu(gate) * up)
    out_part = low(dot(act, w_dn)).reshape(4, span, width)
    by_core = lambda v: lax.dynamic_index_in_dim(v.reshape(2, 2, span, width), c, 1, keepdims=False)
    swap_rows = (lambda v: pair(v)) if fast else (lambda v: by_core(plain_pair(v)))
    out_rows = low(by_core(middle) + (by_core(out_part).astype(F32) + swap_rows(out_part).astype(F32)))

    g_act = low(dot(cots, w_dn, ((1,), (1,)))).astype(F32)
    grad_dn = low(dot(act, cots, ((0,), (0,))))
    sig = 1.0 / (1.0 + jnp.exp(-gate))
    g_gu = low(jnp.concatenate([g_act * up * (sig * (1.0 + gate * (1.0 - sig))), g_act * (gate * sig)], axis=1))
    grad_gu = low(dot(normed_two, g_gu, ((0,), (0,))))
    part = low(dot(g_gu, w_gu, ((1,), (1,))))
    g_two = low(part.astype(F32) + pair(part).astype(F32)).astype(F32)
    g_mid = cots.astype(F32) + rms_back(unit_ffn, scale_ffn, gain_ffn, g_two)
    grad_gain_ffn = 0.5 * jnp.sum(g_two * unit_ffn, axis=0)
    g_branch = low(g_mid)
    g_gated = low(dot(g_branch, w_ssm, ((1,), (1,))))
    g_attn = low(dot(g_branch, w_att, ((1,), (1,))))
    grad_ssm = low(dot(gated, g_branch, ((0,), (0,))))
    grad_att = low(dot(attn, g_branch, ((0,), (0,))))
    by_block = lambda v: v.reshape(groups, -1, v.shape[-1])
    if fast:
        parts = (by_block(grad_dn), by_block(grad_gu)) + tuple(by_block(v) for v in swap_columns(grad_ssm, grad_att))
        g_proj, g_par, *reduced, output = backward_and_reduce(proj, consts, saved, g_gated, g_attn, parts, out_rows)
    else:
        g_proj, g_par = mixer_backward(proj, consts, saved, g_gated, g_attn)
    grad_in = dot(normed, g_proj, ((0,), (0,)))
    part = low(dot(g_proj, w_in, ((1,), (1,)))).reshape(4, span, width)
    g_h1 = low(by_core(part).astype(F32) + swap_rows(part).astype(F32)).astype(F32)
    g_x = by_core(g_mid) + rms_back(by_core(unit_in), by_core(jnp.broadcast_to(scale_in, x.shape)), gain_in, g_h1)
    g_x = low(g_x)
    grad_gain_in = jnp.sum(g_h1 * by_core(unit_in), axis=(0, 1))
    head_grads = jnp.tile(jnp.pad(g_par[:3, :CHIP_HEADS].T, ((0, block - CHIP_HEADS), (0, 0))), (groups, 1))
    extra = jnp.concatenate([grad_gain_in[:, None], grad_gain_ffn[:, None], head_grads], axis=1)
    grad_in = low(lax.dynamic_update_slice(grad_in, extra, (0, T0 + CHIP_HEADS)))

    if fast:
        r_in, returned = end_transfers(by_block(grad_in), g_x)
        r_in, r_dn, r_gu, r_ssm, r_att = [v.astype(F32) for v in (r_in, *reduced)]
    else:
        parts = [by_block(grad_in), by_block(grad_dn), by_block(grad_gu)]
        for v in (grad_ssm, grad_att):
            both = jnp.stack([v, plain_pair(v)])
            both = jnp.where(c == 0, both, both[::-1]).reshape(-1, width)
            parts.append(by_block(cut(both, width // 2 * c, width // 2)))
        (r_in, r_dn, r_gu, r_ssm, r_att), output, returned = plain_reduce(parts, out_rows, g_x, y, c)
    both = lambda start, size: [r_in[0, :, start : start + size], r_in[1, :, start : start + size]]
    grad_in_proj = jnp.concatenate(
        both(Z0, XW)
        + both(X0, XW)
        + [r_in[0, :, B0:T0] + r_in[1, :, B0:T0]]
        + both(Q0, QW)
        + both(KV0, HEAD_WIDTH)
        + both(KV0 + HEAD_WIDTH, HEAD_WIDTH),
        axis=1,
    )
    grad_dt_proj = jnp.concatenate(both(T0, CHIP_HEADS), axis=1)
    tail = r_in[:, :, T0 + CHIP_HEADS : T0 + CHIP_HEADS + 5]
    gains = tail[0, :, :2] + tail[1, :, :2]
    heads = tail[:, :CHIP_HEADS, 2:5].reshape(MH, 3)
    grad_gate_up = jnp.stack(
        [r_gu[k].reshape(block, 2, groups, half_units) for k in range(2)], axis=3
    ).reshape(block, 2 * FF)
    side = lambda v: jnp.concatenate([v[0], v[1]], axis=1)
    return (
        output,
        jnp.take(returned, jnp.argsort(deal_order), axis=0),
        gains[:, 0],
        grad_in_proj,
        grad_dt_proj,
        heads[:, 0],
        heads[:, 1],
        heads[:, 2],
        side(r_ssm),
        side(r_att),
        gains[:, 1],
        grad_gate_up,
        r_dn.reshape(-1, width),
    )


def solution(mesh):
    return jax.shard_map(
        body,
        mesh=mesh,
        in_specs=(
            P(None, "seq", "dp"),
            P("dp", "seq", None),
            P(),
            P(),
            P("dp"),
            P("dp", None),
            P("dp", None),
            P(),
            P(),
            P(),
            P("dp", None),
            P("dp", None),
            P("dp"),
            P("dp", None),
            P("dp", None),
        ),
        out_specs=(
            P("dp", "seq", None),
            P(None, "seq", "dp"),
            P("dp"),
            P("dp", None),
            P("dp", None),
            P(),
            P(),
            P(),
            P("dp", None),
            P("dp", None),
            P("dp"),
            P("dp", None),
            P("dp", None),
        ),
        check_vma=False,
    )
```

```python
import types

import jax
import jax.numpy as jnp
import numpy as np
from jax import lax
from jax.experimental import pallas as pl
from jax.experimental.pallas import tpu as pltpu
from jax.sharding import PartitionSpec as P

FF = 2048
QUERY_HEADS = 8
KEY_VALUE_HEADS = 2
HEAD_WIDTH = 64
MH = 24
HP = 64
NS = 128
EPS = 1e-05
THETA = 100000000000.0
BF = jnp.bfloat16
F32 = jnp.float32
CORES = 2
CHIP_HEADS = MH // CORES
XW = CHIP_HEADS * HP
QW = QUERY_HEADS // CORES * HEAD_WIDTH
Z0, X0, Q0, KV0, B0, C0, T0 = 0, XW, 2 * XW, 2 * XW + QW, 2 * XW + QW + 128, 2 * XW + QW + 256, 2 * XW + QW + 384
COLS = T0 + 128
CHUNK = 256
QB = 256
FAR = -1e30
MIB = 1 << 20
MESH = pl.DeviceIdType.MESH
VM = pltpu.VMEM


def dot(a, b, dims=((1,), (0,)), precision=None):
    return lax.dot_general(a, b, (dims, ((), ())), precision=precision, preferred_element_type=F32)


def lanes(rows, width=128):
    return lax.broadcasted_iota(jnp.int32, (rows, width), 1)


def swap_halves(v):
    low = lanes(v.shape[0], v.shape[1]) % 64 < 32
    return jnp.where(low, pltpu.roll(v, v.shape[1] - 32, 1), pltpu.roll(v, 32, 1))


def turn(v, cosine, sine):
    return v * cosine + swap_halves(v) * sine


def turn_back(v, cosine, sine):
    return v * cosine - swap_halves(v) * sine


def widen(v, spread):
    v = jnp.where(lanes(v.shape[0]) < 64, v, 0.0)
    top = v.astype(BF)
    rest = (v - top.astype(F32)).astype(BF).astype(F32)
    both = top.astype(F32) + pltpu.roll(rest, 64, 1)
    return dot(both.astype(BF), spread)


def attn_masks(segc_ref, segr_ref, i, upto):
    rows = pl.ds(i * QB, QB)
    same = segc_ref[rows, 0:1] == segr_ref[0:1, 0:upto]
    t = lax.broadcasted_iota(jnp.int32, (QB, upto), 0) + i * QB
    u = lax.broadcasted_iota(jnp.int32, (QB, upto), 1)
    return jnp.where(same & (u <= t), 0.0, FAR)


def key_value_pairs(kv, cosine, sine):
    low = lanes(kv.shape[0]) < 64
    other = pltpu.roll(kv, 64, 1)
    kk = turn(jnp.where(low, kv, other), cosine, sine)
    vv = jnp.where(low, other, kv)
    return kk.astype(BF), vv.astype(BF)


def attention_forward(proj_ref, cos_ref, sin_ref, segc_ref, segr_ref, attn_ref, lse_ref, tick):
    seq_len = proj_ref.shape[0]
    kk, vv = key_value_pairs(proj_ref[:, KV0 : KV0 + 128].astype(F32), cos_ref[...], sin_ref[...])
    low = lanes(QB) < 64
    for i in range(seq_len // QB):
        rows = slice(i * QB, (i + 1) * QB)
        upto = (i + 1) * QB
        mask = attn_masks(segc_ref, segr_ref, i, upto)
        tops = jnp.zeros((QB, 128), F32)
        for pair in range(QW // 128):
            q = proj_ref[rows, Q0 + 128 * pair : Q0 + 128 * (pair + 1)].astype(F32)
            q = turn(q, cos_ref[rows, :], sin_ref[rows, :]) * HEAD_WIDTH**-0.5
            outs = []
            for half in range(2):
                qh = jnp.where(low if half == 0 else ~low, q, 0.0).astype(BF)
                s = dot(qh, kk[:upto], ((1,), (1,))) + mask
                top = jnp.max(s, axis=1, keepdims=True)
                e = jnp.exp(s - top)
                total = jnp.sum(e, axis=1, keepdims=True)
                outs.append(dot(e.astype(BF), vv[:upto]) / total)
                tops = jnp.where(lanes(QB) == 2 * pair + half, top + jnp.log(total), tops)
                tick()
            attn_ref[rows, 128 * pair : 128 * (pair + 1)] = jnp.where(low, outs[0], outs[1]).astype(BF)
        lse_ref[rows, :] = tops


def attention_backward(proj_ref, cos_ref, sin_ref, segc_ref, segr_ref, attn_ref, lse_ref, gattn_ref, gproj_ref, gkv, tick):
    seq_len = proj_ref.shape[0]
    kk, vv = key_value_pairs(proj_ref[:, KV0 : KV0 + 128].astype(F32), cos_ref[...], sin_ref[...])
    low = lanes(QB) < 64
    gkv[...] = jnp.zeros_like(gkv)
    pick = (lax.broadcasted_iota(jnp.int32, (QW, 128), 0) // 64 == lanes(QW)).astype(BF)
    for i in range(seq_len // QB):
        rows = slice(i * QB, (i + 1) * QB)
        upto = (i + 1) * QB
        same = segc_ref[0:upto, 0:1] == segr_ref[0:1, rows]
        t = lanes(upto, QB) + i * QB
        u = lax.broadcasted_iota(jnp.int32, (upto, QB), 0)
        mask = jnp.where(same & (u <= t), 0.0, FAR)
        weighed = gattn_ref[rows, :].astype(F32) * attn_ref[rows, :].astype(F32)
        deltas = dot(weighed.astype(BF), pick).T
        tops = lse_ref[rows, :].T
        for pair in range(QW // 128):
            cosine, sine = cos_ref[rows, :], sin_ref[rows, :]
            q = proj_ref[rows, Q0 + 128 * pair : Q0 + 128 * (pair + 1)].astype(F32)
            q = turn(q, cosine, sine) * HEAD_WIDTH**-0.5
            g = gattn_ref[rows, 128 * pair : 128 * (pair + 1)]
            grads = []
            for half in range(2):
                head = 2 * pair + half
                mine = low if half == 0 else ~low
                qh = jnp.where(mine, q, 0.0).astype(BF)
                gh = jnp.where(mine, g, jnp.zeros_like(g))
                s = dot(kk[:upto], qh, ((1,), (1,))) + mask
                p = jnp.exp(s - tops[head : head + 1, :])
                gp = dot(vv[:upto], gh, ((1,), (1,)))
                gs = (p * (gp - deltas[head : head + 1, :])).astype(BF)
                gkv[0:upto, 0:128] += dot(gs, qh)
                gkv[0:upto, 128:256] += dot(p.astype(BF), gh)
                grads.append(dot(gs, kk[:upto], ((0,), (0,))))
                tick()
            gq = jnp.where(low, grads[0], grads[1]) * HEAD_WIDTH**-0.5
            gproj_ref[rows, Q0 + 128 * pair : Q0 + 128 * (pair + 1)] = turn_back(gq, cosine, sine).astype(BF)
    gk = gkv[:, 0:128]
    gv = gkv[:, 128:256]
    gk = turn_back(gk + pltpu.roll(gk, 64, 1), cos_ref[...], sin_ref[...])
    gv = gv + pltpu.roll(gv, 64, 1)
    gproj_ref[:, KV0 : KV0 + 128] = jnp.where(lanes(seq_len) < 64, gk, gv).astype(BF)


def scan_pieces(j, proj_ref, segc_ref, segr_ref, par_ref):
    rows = pl.ds(j * CHUNK, CHUNK)
    seg = segc_ref[rows, :]
    prev = segc_ref[pl.ds(j * CHUNK - 1, 1), :] if j else jnp.full((1, 128), -1, jnp.int32)
    last = segc_ref[pl.ds(j * CHUNK + CHUNK - 1, 1), :]
    valid = lanes(CHUNK) < CHIP_HEADS
    raw = proj_ref[rows, T0 : T0 + 128].astype(F32) + par_ref[0:1, :]
    dt = jnp.where(valid, jnp.maximum(raw, 0.0) + jnp.log1p(jnp.exp(-jnp.abs(raw))), 0.0)
    decay = dt * par_ref[1:2, :]
    place = lax.broadcasted_iota(jnp.int32, (CHUNK, CHUNK), 0)
    under = (place >= lanes(CHUNK, CHUNK)).astype(F32)
    cum = dot(under, decay, precision=lax.Precision.HIGHEST)
    end = cum[CHUNK - 1 : CHUNK, :]
    from_start = jnp.where(seg == prev, jnp.exp(cum), 0.0)
    to_end = jnp.where(seg == last, jnp.exp(end - cum), 0.0)
    keep = jnp.where(last == prev, jnp.exp(end), 0.0)
    return rows, raw, dt, decay, cum, from_start, to_end, keep, under


def scan_forward(proj_ref, segc_ref, segr_ref, par_ref, spread_ref, wide_ref, gated_ref, y_ref, states_ref, state, tick):
    spread = spread_ref[...]
    state[...] = jnp.zeros_like(state)

    for j in range(proj_ref.shape[0] // CHUNK):
        rows, raw, dt, decay, cum, from_start, to_end, keep, under = scan_pieces(j, proj_ref, segc_ref, segr_ref, par_ref)
        place = lax.broadcasted_iota(jnp.int32, (CHUNK, CHUNK), 0)
        same = segc_ref[rows, 0:1] == segr_ref[0:1, rows]
        mask = jnp.where(same & (place >= lanes(CHUNK, CHUNK)), 0.0, FAR)
        cum_t = cum.T
        b = proj_ref[rows, B0 : B0 + 128]
        c = proj_ref[rows, C0 : C0 + 128]
        cb = dot(c, b, ((1,), (1,)))
        x = proj_ref[rows, X0 : X0 + XW].astype(F32)
        xdt = x * widen(dt, spread)
        xdt_low = xdt.astype(BF)
        old = state[...]
        states_ref[j] = old
        y_state = dot(c, old.astype(BF)) * widen(from_start, spread)
        low = lanes(CHUNK) < 64
        for pair in range(CHIP_HEADS // 2):
            cols = slice(128 * pair, 128 * (pair + 1))
            xp = xdt_low[:, cols]
            local = y_state[:, cols]
            for half in range(2):
                h = 2 * pair + half
                spread_h = jnp.exp(cum[:, h : h + 1] - cum_t[h : h + 1, :] + mask)
                mix = (cb * spread_h).astype(BF)
                xh = jnp.where(low if half == 0 else ~low, xp, jnp.zeros_like(xp))
                local = local + dot(mix, xh)
            y_ref[rows, cols] = local
            y = (local + x[:, cols] * wide_ref[0:1, cols]).astype(BF).astype(F32)
            z = proj_ref[rows, Z0 + 128 * pair : Z0 + 128 * (pair + 1)].astype(F32)
            gated_ref[rows, cols] = (y * (z / (1.0 + jnp.exp(-z)))).astype(BF)
            tick()
        weighted = (xdt * widen(to_end, spread)).astype(BF)
        keep_wide = widen(jnp.broadcast_to(keep, (8, 128)), spread)[0:1, :]
        state[...] = old * keep_wide + dot(b, weighted, ((0,), (0,)))


def gate_backward(proj_ref, wide_ref, y_ref, ggated_ref, gproj_ref, gy_ref, tick):
    for j in range(proj_ref.shape[0] // CHUNK):
        rows = pl.ds(j * CHUNK, CHUNK)
        x = proj_ref[rows, X0 : X0 + XW].astype(F32)
        z = proj_ref[rows, Z0 : Z0 + XW].astype(F32)
        gg = ggated_ref[rows, :].astype(F32)
        y = (y_ref[rows, :] + x * wide_ref[0:1, :]).astype(BF).astype(F32)
        sig = 1.0 / (1.0 + jnp.exp(-z))
        gy_ref[rows, :] = (gg * (z * sig)).astype(BF)
        gproj_ref[rows, Z0 : Z0 + XW] = (gg * y * (sig * (1.0 + z * (1.0 - sig)))).astype(BF)
        tick()


def scan_backward(proj_ref, segc_ref, segr_ref, par_ref, spread_ref, wide_ref, y_ref, states_ref, gy_ref, gproj_ref, gpar_ref, gstate, tick):
    spread = spread_ref[...]
    gstate[...] = jnp.zeros_like(gstate)
    gpar_ref[...] = jnp.zeros_like(gpar_ref)
    chunks = proj_ref.shape[0] // CHUNK

    def narrow(v):
        top = v.astype(BF)
        rest = (v - top.astype(F32)).astype(BF)
        return dot(top, spread, ((1,), (1,))) + dot(rest, spread, ((1,), (1,)))

    for j in reversed(range(chunks)):
        rows, raw, dt, decay, cum, from_start, to_end, keep, under = scan_pieces(j, proj_ref, segc_ref, segr_ref, par_ref)
        place = lax.broadcasted_iota(jnp.int32, (CHUNK, CHUNK), 0)
        same = segc_ref[rows, 0:1] == segr_ref[0:1, rows]
        mask = jnp.where(same & (place <= lanes(CHUNK, CHUNK)), 0.0, FAR)
        cum_t = cum.T
        b = proj_ref[rows, B0 : B0 + 128]
        c = proj_ref[rows, C0 : C0 + 128]
        bc = dot(b, c, ((1,), (1,)))
        x = proj_ref[rows, X0 : X0 + XW].astype(F32)
        dt_wide = widen(dt, spread)
        xdt_low = (x * dt_wide).astype(BF)
        start_wide = widen(from_start, spread)
        end_wide = widen(to_end, spread)
        old = states_ref[j]
        gnew = gstate[...]
        y_own = y_ref[rows, :]
        gy_low = gy_ref[rows, :]
        gy = gy_low.astype(F32)
        gx_state = end_wide * dot(b, gnew.astype(BF))
        gbc = jnp.zeros((CHUNK, CHUNK), F32)
        low = lanes(CHUNK) < 64
        gxdt = []
        for pair in range(CHIP_HEADS // 2):
            cols = slice(128 * pair, 128 * (pair + 1))
            xp, gp = xdt_low[:, cols], gy_low[:, cols]
            total = gx_state[:, cols]
            for half in range(2):
                h = 2 * pair + half
                mine = low if half == 0 else ~low
                spread_h = jnp.exp(cum_t[h : h + 1, :] - cum[:, h : h + 1] + mask)
                mix = (bc * spread_h).astype(BF)
                gh = jnp.where(mine, gp, jnp.zeros_like(gp))
                total = total + dot(mix, gh)
                gbc = gbc + dot(xp, gh, ((1,), (1,))) * spread_h
            gxdt.append(total)
            tick()
        gxdt = jnp.concatenate(gxdt, axis=1)
        gstart = (gy * start_wide).astype(BF)
        weighted = (xdt_low.astype(F32) * end_wide).astype(BF)
        gbc_low = gbc.astype(BF)
        gnew_low, old_low = gnew.astype(BF), old.astype(BF)
        gproj_ref[rows, C0 : C0 + 128] = (dot(gbc_low, b, ((0,), (0,))) + dot(gstart, old_low, ((1,), (1,)))).astype(BF)
        gproj_ref[rows, B0 : B0 + 128] = (dot(gbc_low, c) + dot(weighted, gnew_low, ((1,), (1,)))).astype(BF)
        keep_wide = widen(jnp.broadcast_to(keep, (8, 128)), spread)[0:1, :]
        kept = jnp.sum(old * gnew, axis=0, keepdims=True) * keep_wide
        gstate[...] = gnew * keep_wide + dot(c, gstart, ((0,), (0,)))
        xdt_f = xdt_low.astype(F32)
        gcum = narrow(gy * y_own) - narrow(xdt_f * gxdt)
        at_end = jnp.sum(xdt_f * gx_state, axis=0, keepdims=True) + kept
        at_end = narrow(jnp.broadcast_to(at_end, (8, XW)))[0:1, :]
        gdecay = dot(under, gcum, ((0,), (0,)), precision=lax.Precision.HIGHEST) + at_end
        gdt = narrow(gxdt * x) + gdecay * par_ref[1:2, :]
        graw = gdt / (1.0 + jnp.exp(-raw))
        graw = jnp.where(lanes(CHUNK) < CHIP_HEADS, graw, 0.0)
        gproj_ref[rows, T0 : T0 + 128] = graw.astype(BF)
        gproj_ref[rows, X0 : X0 + XW] = (gxdt * dt_wide + gy * wide_ref[0:1, :]).astype(BF)
        gpar_ref[0:1, :] += jnp.sum(graw, axis=0, keepdims=True)
        gpar_ref[1:2, :] += jnp.sum(gdecay * decay, axis=0, keepdims=True)
        skip = jnp.sum(gy * x, axis=0, keepdims=True)
        gpar_ref[2:3, :] += narrow(jnp.broadcast_to(skip, (8, XW)))[0:1, :]


class Ticker:
    def __init__(self, steps, ticks=1):
        self.steps, self.done = steps, 0
        self.plan(len(steps), ticks)

    def plan(self, count, ticks):
        self.first, self.last = self.done, min(self.done + count, len(self.steps))
        self.ticks, self.calls = ticks, 0

    def run(self, upto):
        while self.done < upto:
            if not isinstance(self.steps[self.done], int):
                self.steps[self.done]()
            self.done += 1

    def __call__(self):
        self.calls = min(self.calls + 1, self.ticks)
        self.run(self.first + (self.last - self.first) * self.calls // self.ticks)

    def reach(self, mark):
        if mark in self.steps[self.done :]:
            self.run(self.steps.index(mark) + 1)

    def drain(self):
        self.run(len(self.steps))


def whole(n):
    return [pl.BlockSpec(memory_space=VM)] * n


def place():
    d, s = lax.axis_index("dp"), lax.axis_index("seq")
    return d // 2, d % 2, s // 2, s % 2


def device(z, x, y, c):
    return (2 * z + x, 2 * y + c)


def greet(peers):
    barrier = pltpu.get_barrier_semaphore()
    for peer in peers:
        pl.semaphore_signal(barrier, inc=1, device_id=peer, device_id_type=MESH)
    pl.semaphore_wait(barrier, len(peers))


def send(src, dst, sems, k, target):
    copy = pltpu.make_async_remote_copy(
        src_ref=src, dst_ref=dst, send_sem=sems[0].at[k], recv_sem=sems[1].at[k], device_id=target, device_id_type=MESH
    )
    copy.start()
    return copy


def landed(dst, sems, k, target):
    pltpu.make_async_remote_copy(
        src_ref=dst, dst_ref=dst, send_sem=sems[0].at[k], recv_sem=sems[1].at[k], device_id=target, device_id_type=MESH
    ).wait_recv()


ARRAY_SENDS = 13
CORNER_X = 3


class Gather:
    def __init__(self, src, dst, sems, base, local_sem):
        self.src, self.dst, self.sems, self.base = src, dst, sems, base
        self.local_sem = local_sem
        self.z, self.x, self.y, self.c = place()
        half = src.shape[0] // 2
        self.mine = pl.ds(self.y * half, half)
        self.other = pl.ds((1 - self.y) * half, half)
        self.sent = []
        self.xpeer = device(self.z, 1 - self.x, self.y, self.c)
        self.ypeer = device(self.z, self.x, 1 - self.y, self.c)

    def block(self, r, x, rows):
        return self.dst.at[2 * (self.z ^ r) + x, rows]

    def push(self, k, ref, target, dst=None):
        self.sent.append(send(ref, ref if dst is None else dst, self.sems, self.base + k, target))

    def start(self):
        own = 2 * self.z + self.x
        self.local = pltpu.make_async_copy(self.src, self.dst.at[own], self.local_sem)
        self.local.start()
        for r in (1, 2, 3):
            target = device(self.z ^ r, self.x, self.y, self.c)
            self.push(r - 1, self.src.at[self.mine], target, self.dst.at[own, self.mine])
        self.push(3, self.src, self.xpeer, self.dst.at[own])

    def cross(self):
        landed(self.block(0, 1 - self.x, slice(None)), self.sems, self.base + 3, self.xpeer)
        self.push(4, self.block(0, 1 - self.x, self.mine), device(self.z ^ 1, self.x, self.y, self.c))

    def forward(self, r):
        ref = self.block(r, self.x, self.mine)
        landed(ref, self.sems, self.base + r - 1, self.xpeer)
        self.push(6 + r, ref, self.ypeer)
        if r > 1:
            self.push(3 + r, ref, self.xpeer)

    def corner(self, r):
        if r == CORNER_X:
            ref = self.block(r, self.x, self.other)
            landed(ref, self.sems, self.base + 6 + r, self.ypeer)
            self.push(9 + r, ref, self.xpeer)
        else:
            ref = self.block(r, 1 - self.x, self.mine)
            landed(ref, self.sems, self.base + 3 + r, self.xpeer)
            self.push(9 + r, ref, self.ypeer)

    def arrive(self):
        for r in (1, 2, 3):
            if r == CORNER_X:
                landed(self.block(r, 1 - self.x, self.mine), self.sems, self.base + 3 + r, self.xpeer)
            else:
                landed(self.block(r, self.x, self.other), self.sems, self.base + 6 + r, self.ypeer)
            landed(self.block(r, 1 - self.x, self.other), self.sems, self.base + 9 + r, self.ypeer)
        self.local.wait()

    def finish(self):
        for copy in self.sent:
            copy.wait_send()


def gather_steps(gathers):
    def one(g):
        return [
            lambda: g.forward(1),
            g.cross,
            lambda: g.forward(2),
            lambda: g.forward(3),
        ]

    def corners(g):
        return [lambda r=r: g.corner(r) for r in (2, 3, 1)]

    steps = []
    count = len(gathers)
    for k in range(count + 1):
        if k + 2 < count:
            steps.append(gathers[k + 2].start)
        steps += one(gathers[k]) if k < count else []
        steps += corners(gathers[k - 1]) + [k - 1] if k else []
    return steps


def reduce_steps(sums, partner):
    def early(s):
        return [
            lambda: s.relay(1),
            lambda: s.relay(2),
            lambda: s.root(1),
            lambda: s.relay(3),
            s.cross,
            lambda: s.relay(0),
        ]

    def late(s):
        return [lambda r=r: s.root(r) for r in (2, 3, 0)]

    steps = []
    count = len(sums)
    for k in range(count + 3):
        if k < count:
            steps += early(sums[k])
        if 0 <= k - 1 < count:
            steps += late(sums[k - 1])
        if 0 <= k - 2 < count:
            steps.append(lambda s=sums[k - 2]: s.total(partner))
        if 0 <= k - 3 < count:
            steps.append(lambda s=sums[k - 3]: s.spread(partner))
    return steps


def chip_peers():
    z, x, y, c = place()
    peers = [device(z ^ r, x, y, c) for r in (1, 2, 3)]
    peers += [device(z, 1 - x, y, c), device(z, x, 1 - y, c), device(z, x, y, 1 - c)]
    return peers


def start_kernel(dealt, in_proj, beside, rows, weights, w, kv, dsend, drecv, wsend, wrecv, local):
    z, x, y, c = place()
    own = 2 * z + x
    slot = 2 * y + c
    partner = device(z, x, y, 1 - c)
    others = [(r, i, j) for r in range(4) for i in range(2) for j in range(2) if r or i or j]
    targets = [device(z ^ r, x ^ i, y ^ j, c) for r, i, j in others]
    lane = lambda start, size: pl.ds(pl.multiple_of(start, 128), size)
    inner = MH * HP
    q_start = 2 * inner + 2 * NS
    kv_start = q_start + QUERY_HEADS * HEAD_WIDTH
    pieces = [
        (lane(XW * c, XW), w.at[:, Z0 : Z0 + XW]),
        (lane(inner + XW * c, XW), w.at[:, X0 : X0 + XW]),
        (lane(q_start + QW * c, QW), w.at[:, Q0 : Q0 + QW]),
        (lane(2 * inner, 2 * NS), w.at[:, B0 : B0 + 2 * NS]),
        (lane(kv_start, 256), kv),
    ]
    copies = [pltpu.make_async_copy(in_proj.at[:, cols], dst, local.at[2 + i]) for i, (cols, dst) in enumerate(pieces)]
    for copy in copies:
        copy.start()
    first = c == 0
    lane_of = lanes(w.shape[0])
    near = beside[...].astype(F32)
    far = pltpu.roll(near, 128 - CHIP_HEADS, 1)
    tail = jnp.where(lane_of < CHIP_HEADS, jnp.where(first, near, far), jnp.where(lane_of < CHIP_HEADS + 2, far, 0.0))
    w[:, T0 : T0 + 128] = tail.astype(BF)
    for copy in copies:
        copy.wait()
    keys, values = kv[:, :128].astype(F32), kv[:, 128:].astype(F32)
    keys = jnp.where(first, keys, pltpu.roll(keys, 64, 1))
    values = jnp.where(first, pltpu.roll(values, 64, 1), values)
    w[:, KV0 : KV0 + 128] = jnp.where(lane_of < 64, keys, values).astype(BF)
    greet(targets + [partner])
    sems = (dsend, drecv)
    gather = Gather(w, weights, (wsend, wrecv), 0, local.at[0])
    columns = lambda d: lane(d * 128, 128)
    sent = []
    gather.start()
    for k, (r, i, j) in enumerate(others):
        pack = 2 * (2 * (z ^ r) + (x ^ i)) + (y ^ j)
        sent.append(send(dealt.at[pack], rows.at[slot, :, columns(own)], sems, k, targets[k]))
    here = pltpu.make_async_copy(dealt.at[2 * own + y], rows.at[slot, :, columns(own)], local.at[1])
    here.start()
    gather.forward(1)
    gather.cross()
    gather.forward(2)
    gather.forward(3)
    here.wait()
    for same_y in (True, False):
        for k, (r, i, j) in enumerate(others):
            if (j == 0) == same_y:
                src = 2 * (z ^ r) + (x ^ i)
                landed(rows.at[2 * (y ^ j) + c, :, columns(src)], sems, k, targets[k])
        ref = rows.at[slot if same_y else 2 * (1 - y) + c]
        sent.append(send(ref, ref, sems, 15 if same_y else 16, partner))
    for r in (1, 2, 3):
        gather.corner(r)
    landed(rows.at[2 * y + 1 - c], sems, 15, partner)
    landed(rows.at[2 * (1 - y) + 1 - c], sems, 16, partner)
    gather.arrive()
    for copy in sent:
        copy.wait_send()
    gather.finish()


def start_transfers(dealt, in_proj, beside):
    packs, span, width = dealt.shape
    block = in_proj.shape[0]
    return pl.pallas_call(
        start_kernel,
        name="deal_and_gather",
        out_shape=(
            jax.ShapeDtypeStruct((4, span, 8 * width), BF),
            jax.ShapeDtypeStruct((8, block, COLS), BF),
        ),
        in_specs=whole(1) + any_specs(1) + whole(1),
        out_specs=tuple(any_specs(2)),
        scratch_shapes=[
            VM((block, COLS), BF),
            VM((block, 256), BF),
            pltpu.SemaphoreType.DMA((17,)),
            pltpu.SemaphoreType.DMA((17,)),
            pltpu.SemaphoreType.DMA((ARRAY_SENDS,)),
            pltpu.SemaphoreType.DMA((ARRAY_SENDS,)),
            pltpu.SemaphoreType.DMA((7,)),
        ],
        compiler_params=pltpu.CompilerParams(collective_id=0, has_side_effects=True),
    )(dealt, in_proj, beside)


def any_specs(n):
    return [pl.BlockSpec(memory_space=pl.ANY)] * n


class Cotangents:
    def __init__(self, src, dst, sems, local_sem):
        self.src, self.dst, self.sems, self.local_sem = src, dst, sems, local_sem
        self.z, self.x, self.y, self.c = place()
        self.slot = 2 * self.y + self.c
        self.partner = device(self.z, self.x, self.y, 1 - self.c)
        self.ypeer = device(self.z, self.x, 1 - self.y, self.c)

    def start(self):
        src, dst = self.src, self.dst
        self.sent = [
            send(src.at[1 - self.y], dst.at[self.slot], self.sems, 0, self.ypeer),
            send(src.at[self.y], dst.at[self.slot], self.sems, 1, self.partner),
        ]
        self.local = pltpu.make_async_copy(src.at[self.y], dst.at[self.slot], self.local_sem)
        self.local.start()

    def forward(self):
        ref = self.dst.at[2 * (1 - self.y) + self.c]
        landed(ref, self.sems, 0, self.ypeer)
        self.sent.append(send(ref, ref, self.sems, 2, self.partner))

    def arrive(self):
        landed(self.dst.at[2 * self.y + 1 - self.c], self.sems, 1, self.partner)
        landed(self.dst.at[2 * (1 - self.y) + 1 - self.c], self.sems, 2, self.partner)
        self.local.wait()

    def finish(self):
        for copy in self.sent:
            copy.wait_send()


class Halves:
    def __init__(self, gather, dst, sems, base, local_sem):
        self.gather, self.dst, self.sems, self.base, self.local_sem = gather, dst, sems, base, local_sem
        z, x, y, self.c = place()
        self.partner = device(z, x, y, 1 - self.c)

    def columns(self, k):
        half = self.gather.src.shape[1]
        return self.dst.at[:, :, pl.ds(pl.multiple_of(k * half, 128), half)]

    def start(self):
        src, c = self.gather.dst, self.c
        self.gather.arrive()
        self.local = pltpu.make_async_copy(src.at[pl.ds(4 * c, 4)], self.columns(c), self.local_sem)
        self.local.start()
        self.sent = send(src.at[pl.ds(4 * (1 - c), 4)], self.columns(c), self.sems, self.base, self.partner)

    def arrive(self):
        landed(self.columns(1 - self.c), self.sems, self.base, self.partner)
        self.local.wait()
        self.sent.wait_send()


def plain_forward_kernel(proj, cosine, sine, segc, segr, par, spread, wide, gated, attn, lse, y_own, states, state):
    tick = Ticker([])
    attention_forward(proj, cosine, sine, segc, segr, attn, lse, tick)
    scan_forward(proj, segc, segr, par, spread, wide, gated, y_own, states, state, tick)


def mixer_forward(proj, consts):
    seq_len = proj.shape[0]
    return pl.pallas_call(
        plain_forward_kernel,
        name="mixer_forward",
        out_shape=(
            jax.ShapeDtypeStruct((seq_len, XW), BF),
            jax.ShapeDtypeStruct((seq_len, QW), BF),
            jax.ShapeDtypeStruct((seq_len, 128), F32),
            jax.ShapeDtypeStruct((seq_len, XW), F32),
            jax.ShapeDtypeStruct((seq_len // CHUNK, NS, XW), F32),
        ),
        in_specs=whole(8),
        out_specs=tuple(whole(5)),
        scratch_shapes=[VM((NS, XW), F32)],
        compiler_params=pltpu.CompilerParams(vmem_limit_bytes=56 * MIB),
    )(proj, *consts)


class Reduce:
    def __init__(self, part, out, far, near_x, near_y, deep, sems, base):
        self.part, self.out, self.far, self.near_x, self.near_y, self.deep = part, out, far, near_x, near_y, deep
        self.sems, self.base = sems, base
        self.z, self.x, self.y, self.c = place()
        half = part.shape[1] // 2
        self.mine = pl.ds(self.y * half, half)
        self.other = pl.ds((1 - self.y) * half, half)
        self.xpeer = device(self.z, 1 - self.x, self.y, self.c)
        self.ypeer = device(self.z, self.x, 1 - self.y, self.c)
        self.sent = []

    def piece(self, r, x, rows):
        return self.part.at[2 * (self.z ^ r) + x, rows]

    def push(self, k, src, dst, target):
        self.sent.append(send(src, dst, self.sems, self.base + k, target))

    def start(self):
        for r in (1, 2, 3, 0):
            far = self.piece(r, 1 - self.x, self.other)
            self.push(r, far, self.far.at[r], self.ypeer if r == 1 else self.xpeer)

    def relay(self, r):
        landed(self.far.at[r], self.sems, self.base + r, self.xpeer)
        own = self.piece(r, 1 - self.x, self.mine) if r == 1 else self.piece(r, self.x, self.other)
        self.far[r] = (own[...].astype(F32) + self.far[r].astype(F32)).astype(BF)
        if r == 1:
            self.push(5, self.far.at[1], self.near_x.at[1], device(self.z ^ 1, self.x, self.y, self.c))
            self.push(9, self.piece(1, self.x, self.other), self.near_y.at[1], self.ypeer)
        else:
            self.push(8 + r, self.far.at[r], self.near_y.at[r], self.ypeer)
        if r > 1:
            self.push(4 + r, self.piece(r, 1 - self.x, self.mine), self.near_x.at[r], self.xpeer)

    def cross(self):
        landed(self.near_x.at[1], self.sems, self.base + 5, self.xpeer)
        own = self.piece(0, 1 - self.x, self.mine)[...].astype(F32)
        self.near_x[1] = (own + self.near_x[1].astype(F32)).astype(BF)
        self.push(4, self.near_x.at[1], self.near_x.at[0], self.xpeer)

    def root(self, r):
        landed(self.near_y.at[r], self.sems, self.base + 8 + r, self.ypeer)
        total = self.piece(r, self.x, self.mine)[...].astype(F32) + self.near_y[r].astype(F32)
        if r != 1:
            landed(self.near_x.at[r], self.sems, self.base + 4 + r, self.xpeer)
            total = total + self.near_x[r].astype(F32)
        self.near_y[r] = total.astype(BF)
        if r:
            target = device(self.z ^ r, self.x, self.y, self.c)
            self.push(11 + r, self.near_y.at[r], self.deep.at[r - 1], target)

    def total(self, partner):
        for r in (1, 2, 3):
            landed(self.deep.at[r - 1], self.sems, self.base + 11 + r, self.xpeer)
        total = self.near_y[0].astype(F32) + self.deep[0].astype(F32)
        total = total + (self.deep[1].astype(F32) + self.deep[2].astype(F32))
        self.out[self.c, self.mine] = total.astype(BF)
        ref = self.out.at[self.c, self.mine]
        self.push(15, ref, ref, self.ypeer)
        self.push(16, ref, ref, partner)

    def spread(self, partner):
        ref = self.out.at[self.c, self.other]
        landed(ref, self.sems, self.base + 15, self.ypeer)
        self.push(17, ref, ref, partner)

    def finish(self, partner):
        landed(self.out.at[1 - self.c, self.mine], self.sems, self.base + 16, partner)
        landed(self.out.at[1 - self.c, self.other], self.sems, self.base + 17, partner)
        for copy in self.sent:
            copy.wait_send()


REDUCE_SENDS = 18


def reduce_buffers(parts):
    scratch = []
    for p in parts:
        half = (p.shape[1] // 2, p.shape[2])
        scratch += [VM((4,) + half, BF)] * 3 + [VM((3,) + half, BF)]
    total = REDUCE_SENDS * len(parts)
    return scratch + [pltpu.SemaphoreType.DMA((total,))] * 2


def plain_backward_kernel(proj, cosine, sine, segc, segr, par, spread, wide, attn, lse, y_own, states, ggated, gattn, gproj, gpar, gkv, gstate, gy):
    tick = Ticker([])
    gate_backward(proj, wide, y_own, ggated, gproj, gy, tick)
    attention_backward(proj, cosine, sine, segc, segr, attn, lse, gattn, gproj, gkv, tick)
    scan_backward(proj, segc, segr, par, spread, wide, y_own, states, gy, gproj, gpar, gstate, tick)


def mixer_backward(proj, consts, saved, ggated, gattn):
    seq_len = proj.shape[0]
    return pl.pallas_call(
        plain_backward_kernel,
        name="mixer_backward",
        out_shape=(
            jax.ShapeDtypeStruct((seq_len, COLS), BF),
            jax.ShapeDtypeStruct((8, 128), F32),
        ),
        in_specs=whole(14),
        out_specs=tuple(whole(2)),
        scratch_shapes=[VM((seq_len, 256), F32), VM((NS, XW), F32), VM((seq_len, XW), BF)],
        compiler_params=pltpu.CompilerParams(vmem_limit_bytes=56 * MIB),
    )(proj, *consts, *saved, ggated, gattn)


class Mover:
    def __init__(self, sems):
        self.sems, self.used, self.loads, self.stores = sems, 0, {}, []

    def copy(self, src, dst):
        copy = pltpu.make_async_copy(src, dst, self.sems.at[self.used])
        self.used += 1
        copy.start()
        return copy

    def load(self, src, dst):
        self.loads.setdefault(id(dst), []).append(self.copy(src, dst))

    def need(self, *refs):
        for ref in refs:
            for copy in self.loads.pop(id(ref), []):
                copy.wait()

    def store(self, src, dst):
        copy = self.copy(src, dst)
        self.stores.append(copy)
        return copy

    def flush(self):
        for copies in self.loads.values():
            for copy in copies:
                copy.wait()
        for copy in self.stores:
            copy.wait()


def shape(dims, dtype=BF):
    return jax.ShapeDtypeStruct(tuple(dims), dtype)


def fused_call(kernel, name, inputs, outputs, scratch, spaces, collective_id):
    names = list(inputs) + list(outputs) + list(scratch)

    def wrapped(*refs):
        kernel(types.SimpleNamespace(**dict(zip(names, refs))))

    place_of = lambda n: pl.BlockSpec(memory_space=spaces.get(n, pl.ANY))
    outs = pl.pallas_call(
        wrapped,
        name=name,
        out_shape=tuple(outputs.values()),
        in_specs=[place_of(n) for n in inputs],
        out_specs=tuple(place_of(n) for n in outputs),
        scratch_shapes=list(scratch.values()),
        compiler_params=pltpu.CompilerParams(
            collective_id=collective_id, has_side_effects=True, vmem_limit_bytes=62 * MIB
        ),
    )(*inputs.values())
    return types.SimpleNamespace(**dict(zip(outputs, outs)))


def dma(n):
    return pltpu.SemaphoreType.DMA((n,))


def row_blocks(seq_len, size=256):
    return [slice(i, i + size) for i in range(0, seq_len, size)]


def mixer_constants(k, own, y, c):
    seq_len = k.segc_v.shape[0]
    pack = k.deal[2 * own + y]
    ends = [k.lengths[pack, 0]]
    for i in (1, 2):
        ends.append(ends[-1] + k.lengths[pack, i])
    for ref, dims, axis in ((k.segc_v, (seq_len, 128), 0), (k.segr_v, (8, seq_len), 1)):
        place_of = lax.broadcasted_iota(jnp.int32, dims, axis)
        ref[...] = sum((place_of >= end).astype(jnp.int32) for end in ends)
    heads = k.heads[...]
    heads = jnp.where(c == 0, heads, pltpu.roll(heads, 128 - CHIP_HEADS, 1))
    heads = jnp.where(lanes(8) < CHIP_HEADS, heads, 0.0)
    k.par_v[0:1, :] = heads[0:1, :]
    k.par_v[1:2, :] = jnp.where(lanes(1) < CHIP_HEADS, -jnp.exp(heads[1:2, :]), 0.0)
    k.wide_v[...] = dot(jnp.broadcast_to(heads[2:3, :], (8, 128)), k.spread_v[...].astype(F32), precision=lax.Precision.HIGHEST)


def forward_fused(k):
    z, x, y, c = place()
    own = 2 * z + x
    partner = device(z, x, y, 1 - c)
    mover = Mover(k.local)
    lane = lambda start, size: pl.ds(pl.multiple_of(start, 128), size)
    half = k.dn.shape[0] // 2
    for side in range(2):
        for d in range(8):
            mover.load(k.gu.at[:, lane(side * FF + (2 * d + c) * half, half)], k.gu_s.at[:, side * FF // 2 + d * half : side * FF // 2 + (d + 1) * half])
    shard_loads, mover.loads = mover.loads, {}
    for src, dst in ((k.rows, k.rows_v), (k.w_in, k.w_in_v), (k.spread, k.spread_v), (k.cosine, k.cosine_v), (k.sine, k.sine_v)):
        mover.load(src, dst)
    greet(chip_peers())
    columns = lane(k.part_v.shape[1] // 2 * c, k.part_v.shape[1] // 2)
    pairs = (
        (k.ssm.at[:, columns], k.ssm_all),
        (k.att.at[:, columns], k.att_all),
        (k.gu_s, k.gu_w),
        (k.dn.at[pl.ds(half * c, half)], k.dn_w),
    )
    gathers = [Gather(a, b, (k.gsend, k.grecv), ARRAY_SENDS * i, k.own.at[i]) for i, (a, b) in enumerate(pairs)]
    cots = Cotangents(k.cot, k.cots_v, (k.csend, k.crecv), k.own.at[4])
    halves = [Halves(g, out, (k.csend, k.crecv), 3 + i, k.own.at[5 + i]) for i, (g, out) in enumerate(zip(gathers, (k.ssm_v, k.att_v)))]
    gathers[0].start()
    gathers[1].start()
    cots.start()
    for copies in shard_loads.values():
        for copy in copies:
            copy.wait()
    steps = gather_steps(gathers)
    at = steps.index(1) + 6
    steps[at:at] = [h.start for h in halves] + [9]
    steps.insert(steps.index(3) - 2, cots.forward)
    tick = Ticker(steps, 60)

    blocks = row_blocks(k.rows_v.shape[0])
    mover.need(k.rows_v, k.w_in_v)
    tile = k.w_in_v[:, T0 : T0 + 128].astype(F32).T
    k.gains_v[0:1, :] = tile[CHIP_HEADS : CHIP_HEADS + 1, :]
    k.gains_v[1:2, :] = tile[CHIP_HEADS + 1 : CHIP_HEADS + 2, :]
    mover.store(k.gains_v, k.gains)
    for rows in blocks:
        xs = k.rows_v[rows, :].astype(F32)
        unit, _ = rms_parts(xs)
        normed = (unit * k.gains_v[0:1, :]).astype(BF)
        k.normed_v[rows, :] = normed
        for n in range(0, COLS, 768):
            k.proj_v[rows, n : n + 768] = dot(normed, k.w_in_v[:, n : n + 768]).astype(BF)
            tick()
    mover.store(k.proj_v, k.proj)
    kept_normed = mover.store(k.normed_v, k.normed)
    mover.need(k.spread_v, k.cosine_v, k.sine_v)
    mixer_constants(k, own, y, c)
    for src, dst in ((k.segc_v, k.segc), (k.segr_v, k.segr), (k.par_v, k.par), (k.wide_v, k.wide)):
        mover.store(src, dst)
    attention_forward(k.proj_v, k.cosine_v, k.sine_v, k.segc_v, k.segr_v, k.attn_v, k.lse_v, tick)
    mover.store(k.attn_v, k.attn)
    mover.store(k.lse_v, k.lse)
    scan_forward(k.proj_v, k.segc_v, k.segr_v, k.par_v, k.spread_v, k.wide_v, k.gated_v, k.y_v, k.states_v, k.state, tick)
    mover.store(k.gated_v, k.gated)
    mover.store(k.y_v, k.y)
    mover.store(k.states_v, k.states)

    tick.reach(9)
    for h in halves:
        h.arrive()
    mover.store(k.ssm_v, k.w_ssm)
    mover.store(k.att_v, k.w_att)
    sent = []
    for i, rows in enumerate(blocks):
        part = dot(k.gated_v[rows, :], k.ssm_v[...].reshape(XW, -1))
        part = part + dot(k.attn_v[rows, :], k.att_v[...].reshape(QW, -1))
        k.part_v[rows, :] = part.astype(BF)
        sent.append(send(k.part_v.at[rows], k.got_v.at[rows], (k.psend, k.precv), i, partner))
        tick()
    kept_normed.wait()
    mover.stores = [v for v in mover.stores if v is not kept_normed]
    for i, rows in enumerate(blocks):
        landed(k.got_v.at[rows], (k.psend, k.precv), i, partner)
        middle = k.rows_v[rows, :].astype(F32) + (k.part_v[rows, :].astype(F32) + k.got_v[rows, :].astype(F32))
        k.middle_v[rows, :] = middle
        unit, _ = rms_parts(middle)
        k.normed_v[rows, :] = (unit * k.gains_v[1:2, :]).astype(BF)
        tick()
    mover.store(k.middle_v, k.middle)
    mover.store(k.normed_v, k.h2)

    tick.reach(2)
    gathers[2].arrive()
    mover.store(k.gu_w, k.w_gu)
    for rows in blocks:
        for n in range(0, FF // 2, 512):
            for side in (0, FF // 2):
                cols = slice(side + n, side + n + 512)
                w = k.gu_w[:, :, cols].reshape(-1, 512)
                k.w_in_v[rows, cols] = dot(k.normed_v[rows, :], w).astype(BF)
            gate = k.w_in_v[rows, n : n + 512].astype(F32)
            up = k.w_in_v[rows, FF // 2 + n : FF // 2 + n + 512].astype(F32)
            k.act_v[rows, n : n + 512] = (silu(gate) * up).astype(BF)
            tick()
    mover.store(k.w_in_v.at[:, 0:FF], k.hidden)
    mover.store(k.act_v, k.act)
    tick.drain()
    cots.arrive()
    mover.store(k.cots_v, k.cots)
    width = k.rows_v.shape[1]
    for m in range(0, FF // 2, 256):
        k.gdn_v[m : m + 256, :] = dot(k.act_v[:, m : m + 256], k.cots_v[...].reshape(-1, width), ((0,), (0,))).astype(BF)
    mover.store(k.gdn_v, k.g_dn)
    gathers[3].arrive()
    mover.store(k.dn_w, k.w_dn)
    for g in gathers:
        g.finish()
    cots.finish()
    for copy in sent:
        copy.wait_send()
    mover.flush()


def forward_stage(rows, w_in, tables, heads, deal, lengths, cot, shards):
    seq_len, width = rows.shape
    ssm, att, gu, dn = shards
    cosine, sine, spread = tables
    chunks = seq_len // CHUNK
    total = 4 * ARRAY_SENDS
    half = dn.shape[0] // 2
    inputs = dict(
        rows=rows, w_in=w_in, cosine=cosine, sine=sine, spread=spread, heads=heads, deal=deal, lengths=lengths, cot=cot, ssm=ssm, att=att, gu=gu, dn=dn
    )
    spaces = dict(heads=VM, deal=pltpu.SMEM, lengths=pltpu.SMEM)
    square = shape((seq_len, width))
    outputs = dict(
        proj=shape((seq_len, COLS)),
        normed=square,
        gains=shape((8, width), F32),
        attn=shape((seq_len, QW)),
        lse=shape((seq_len, 128), F32),
        gated=shape((seq_len, XW)),
        y=shape((seq_len, XW), F32),
        states=shape((chunks, NS, XW), F32),
        w_ssm=shape((4, ssm.shape[0], width)),
        w_att=shape((4, att.shape[0], width)),
        w_gu=shape((8, gu.shape[0], FF)),
        w_dn=shape((8, half, width)),
        middle=shape((seq_len, width), F32),
        h2=square,
        hidden=shape((seq_len, FF)),
        act=shape((seq_len, FF // 2)),
        cots=shape((4,) + cot.shape[1:]),
        g_dn=shape((FF // 2, width)),
        segc=shape((seq_len, 128), jnp.int32),
        segr=shape((8, seq_len), jnp.int32),
        par=shape((8, 128), F32),
        wide=shape((8, XW), F32),
    )
    out = types.SimpleNamespace(**outputs)
    buffer = lambda v: VM(v.shape, v.dtype)
    scratch = dict(
        rows_v=buffer(rows),
        w_in_v=buffer(w_in),
        cosine_v=buffer(cosine),
        sine_v=buffer(sine),
        spread_v=buffer(spread),
        segc_v=buffer(out.segc),
        segr_v=buffer(out.segr),
        par_v=buffer(out.par),
        wide_v=buffer(out.wide),
        proj_v=buffer(out.proj),
        normed_v=buffer(square),
        gains_v=buffer(out.gains),
        attn_v=buffer(out.attn),
        lse_v=buffer(out.lse),
        gated_v=buffer(out.gated),
        y_v=buffer(out.y),
        states_v=buffer(out.states),
        middle_v=buffer(out.middle),
        act_v=buffer(out.act),
        cots_v=buffer(out.cots),
        ssm_v=buffer(out.w_ssm),
        att_v=buffer(out.w_att),
        gu_w=buffer(out.w_gu),
        dn_w=buffer(out.w_dn),
        gu_s=VM((gu.shape[0], FF), BF),
        ssm_all=VM((8, ssm.shape[0], width // 2), BF),
        att_all=VM((8, att.shape[0], width // 2), BF),
        gdn_v=buffer(out.g_dn),
        part_v=buffer(square),
        got_v=buffer(square),
        state=VM((NS, XW), F32),
        gsend=dma(total),
        grecv=dma(total),
        csend=dma(5),
        crecv=dma(5),
        psend=dma(4),
        precv=dma(4),
        own=dma(7),
        local=dma(48),
    )
    return fused_call(forward_fused, "forward", inputs, outputs, scratch, spaces, 1)


def feed_forward_fused(k):
    z, x, y, c = place()
    partner = device(z, x, y, 1 - c)
    ypeer = device(z, x, 1 - y, c)
    mover = Mover(k.local)
    for src, dst in k.loads:
        mover.load(src, dst)
    greet(chip_peers())
    pairs = ((k.g_dn_v, k.red_dn), (k.gate_v, k.red_gate))
    sums = [Reduce(part, out, *k.bufs[4 * i : 4 * i + 4], (k.rsend, k.rrecv), REDUCE_SENDS * i) for i, (part, out) in enumerate(pairs)]
    mover.need(k.g_dn_v)
    sums[0].start()
    tick = Ticker(reduce_steps(sums, partner))
    seq_len, width = k.middle_v.shape
    span = seq_len // 4
    blocks = row_blocks(seq_len)
    half = FF // 2
    flat = lambda ref: ref[...].reshape(-1, ref.shape[-1])
    pair = (k.psend, k.precv)

    mover.need(k.cots_v, k.w_dn_v, k.hidden_v)
    for i, rows in enumerate(blocks):
        g_act = dot(k.cots_v[i], flat(k.w_dn_v), ((1,), (1,))).astype(BF).astype(F32)
        gate = k.hidden_v[rows, :half].astype(F32)
        up = k.hidden_v[rows, half:].astype(F32)
        sig = 1.0 / (1.0 + jnp.exp(-gate))
        k.hidden_v[rows, :half] = (g_act * up * (sig * (1.0 + gate * (1.0 - sig)))).astype(BF)
        k.hidden_v[rows, half:] = (g_act * (gate * sig)).astype(BF)
    mover.need(k.h2_v)
    tick.plan(2, 4)
    for d in range(0, 8, 2):
        grad = dot(k.h2_v[:, 128 * d : 128 * d + 256], k.hidden_v[:, :half], ((0,), (0,))).astype(BF)
        k.gate_v[d : d + 2] = grad.reshape(2, 128, half)
        tick()
    sums[1].start()
    tick.plan(13, 24)
    mover.need(k.w_gu_v)
    sent = []
    for i, rows in enumerate(blocks):
        part = dot(k.hidden_v[rows, :], flat(k.w_gu_v), ((1,), (1,)))
        k.part_v[rows, :] = part.astype(BF)
        sent.append(send(k.part_v.at[rows], k.got_v.at[rows], pair, i, partner))
        tick()
    mover.need(k.act_v)
    for j in range(2):
        rows = pl.ds(pl.multiple_of((2 * j + 1 - c) * span, span), span)
        k.opart_v[j] = dot(k.act_v[rows, :], flat(k.w_dn_v)).astype(BF)
        sent.append(send(k.opart_v.at[j], k.ogot_v.at[j], pair, 4 + j, partner))
        tick()
    for d in range(0, 8, 2):
        grad = dot(k.h2_v[:, 128 * d : 128 * d + 256], k.hidden_v[:, half:], ((0,), (0,))).astype(BF)
        k.up_v[d : d + 2] = grad.reshape(2, 128, half)
        tick()
    mover.store(k.up_v, k.g_up)

    mover.need(k.middle_v)
    for j in range(2):
        rows = pl.ds(pl.multiple_of((2 * j + c) * span, span), span)
        own = k.middle_v[rows, :] + dot(k.act_v[rows, :], flat(k.w_dn_v)).astype(BF).astype(F32)
        landed(k.ogot_v.at[j], pair, 4 + j, partner)
        k.out_v[j] = (own + k.ogot_v[j].astype(F32)).astype(BF)
        tick()
    sent.append(send(k.out_v.at[1 - y], k.output.at[y], pair, 14, ypeer))
    mover.store(k.out_v.at[y], k.output.at[y])

    mover.need(k.middle_v, k.gains_v, k.w_ssm_v, k.w_att_v)
    gain = k.gains_v[1:2, :]
    grad_gain = jnp.zeros((1, width), F32)
    for i, rows in enumerate(blocks):
        landed(k.got_v.at[rows], pair, i, partner)
        g_two = (k.part_v[rows, :].astype(F32) + k.got_v[rows, :].astype(F32)).astype(BF).astype(F32)
        unit, scale = rms_parts(k.middle_v[rows, :])
        grad_gain = grad_gain + jnp.sum(g_two * unit, axis=0, keepdims=True)
        g_mid = k.cots_v[i].astype(F32) + rms_back(unit, scale, gain, g_two)
        k.got_f32[rows, :] = g_mid
        branch = g_mid.astype(BF)
        k.branch_v[rows, :] = branch
        tick()
        k.ggated_v[rows, :] = dot(branch, flat(k.w_ssm_v), ((1,), (1,))).astype(BF)
        k.gattn_v[rows, :] = dot(branch, flat(k.w_att_v), ((1,), (1,))).astype(BF)
        tick()
    k.gffn_v[0:1, :] = 0.5 * grad_gain
    mover.store(k.gffn_v, k.gffn)
    mover.store(k.ggated_v, k.ggated)
    mover.store(k.gattn_v, k.gattn)
    for j in range(2):
        mover.store(k.got_f32.at[pl.ds(pl.multiple_of((2 * j + c) * span, span), span)], k.g_mid.at[j])

    mover.need(k.gated_v, k.attn_v)
    moves = []
    n = 6
    for source, rows, hold, out in ((k.gated_v, XW, k.gssm_v, k.g_ssm), (k.attn_v, QW, k.gatt_v, k.g_att)):
        for m in range(0, rows, 256):
            hold[m : m + 256, :] = dot(source[:, m : m + 256], k.branch_v[...], ((0,), (0,))).astype(BF)
            tick()
        own = rows // 4
        for d in range(4):
            columns = lambda e: hold.at[pl.ds(d * own, own), pl.ds(pl.multiple_of(e * (width // 2), 128), width // 2)]
            mover.store(columns(c), out.at[4 * c + d])
            moves.append((out.at[4 * (1 - c) + d], n))
            sent.append(send(columns(1 - c), out.at[4 * c + d], pair, n, partner))
            n += 1

    tick.drain()
    for s in sums:
        s.finish(partner)
    for ref, i in moves:
        landed(ref, pair, i, partner)
    landed(k.output.at[1 - y], pair, 14, ypeer)
    for copy in sent:
        copy.wait_send()
    mover.flush()


def reduce_scratch(shapes):
    bufs = []
    for dims in shapes:
        half = (dims[1] // 2, dims[2])
        bufs += [VM((4,) + half, BF)] * 3 + [VM((3,) + half, BF)]
    return {"b" + str(i): b for i, b in enumerate(bufs)}


def loaded(inputs, names=None):
    return {n + "_v": VM(v.shape, v.dtype) for n, v in inputs.items()}


def with_lists(kernel, inputs, bufs):
    def run(k):
        refs = vars(k)
        k.loads = [(refs[n], refs[n + "_v"]) for n in inputs if n + "_v" in refs]
        k.bufs = [refs[n] for n in bufs]
        kernel(k)

    return run


def feed_forward_stage(f):
    seq_len, width = f.middle.shape
    inputs = dict(
        g_dn=f.g_dn.reshape(8, -1, width),
        cots=f.cots,
        w_dn=f.w_dn,
        hidden=f.hidden,
        h2=f.h2,
        w_gu=f.w_gu,
        act=f.act,
        middle=f.middle,
        gains=f.gains,
        w_ssm=f.w_ssm,
        w_att=f.w_att,
        gated=f.gated,
        attn=f.attn,
    )
    span = seq_len // 4
    part = (8, width // 8, FF // 2)
    outputs = dict(
        output=shape((2, span, width)),
        red_dn=shape((2,) + inputs["g_dn"].shape[1:]),
        red_gate=shape((2,) + part[1:]),
        g_up=shape(part),
        g_ssm=shape((8, XW // 4, width // 2)),
        g_att=shape((8, QW // 4, width // 2)),
        ggated=shape((seq_len, XW)),
        gattn=shape((seq_len, QW)),
        g_mid=shape((2, span, width), F32),
        gffn=shape((8, width), F32),
    )
    bufs = reduce_scratch([inputs["g_dn"].shape, part])
    scratch = dict(
        **loaded(inputs),
        **bufs,
        gate_v=VM(part, BF),
        up_v=VM(part, BF),
        part_v=VM((seq_len, width), BF),
        got_v=VM((seq_len, width), BF),
        opart_v=VM((2, span, width), BF),
        ogot_v=VM((2, span, width), BF),
        out_v=VM((2, span, width), BF),
        got_f32=VM((seq_len, width), F32),
        branch_v=VM((seq_len, width), BF),
        ggated_v=VM((seq_len, XW), BF),
        gattn_v=VM((seq_len, QW), BF),
        gssm_v=VM((XW, width), BF),
        gatt_v=VM((QW, width), BF),
        gffn_v=VM((8, width), F32),
        rsend=dma(2 * REDUCE_SENDS),
        rrecv=dma(2 * REDUCE_SENDS),
        psend=dma(15),
        precv=dma(15),
        local=dma(32),
    )
    kernel = with_lists(feed_forward_fused, inputs, bufs)
    return fused_call(kernel, "feed_forward", inputs, outputs, scratch, dict(red_dn=VM, red_gate=VM), 2)


def backward_fused(k):
    z, x, y, c = place()
    own = 2 * z + x
    slot = 2 * own + y
    partner = device(z, x, y, 1 - c)
    others = [(r, i, j) for r in range(4) for i in range(2) for j in range(2) if r or i or j]
    targets = [device(z ^ r, x ^ i, y ^ j, c) for r, i, j in others]
    mover = Mover(k.local)
    for src, dst in k.loads:
        mover.load(src, dst)
    greet(targets + [partner])
    pairs = (
        (k.up_v, k.red_up),
        (k.ssm_v, k.red_ssm),
        (k.att_v, k.red_att),
        (k.gz_v, k.red_gz),
        (k.xbc_v, k.red_xbc),
        (k.qkv_v, k.red_qkv),
        (k.steps_v, k.red_steps),
    )
    sums = [Reduce(part, out, *k.bufs[4 * i : 4 * i + 4], (k.rsend, k.rrecv), REDUCE_SENDS * i) for i, (part, out) in enumerate(pairs)]
    mover.need(k.up_v)
    sums[0].start()
    mover.need(k.ssm_v, k.att_v)
    for step in sums[1:3]:
        step.start()
    tick = Ticker(reduce_steps(sums, partner))
    tick.plan(2, 8)
    seq_len, width = k.normed_v.shape
    span = seq_len // 4

    def grad_of(lo, hi, out, at):
        for d in range(0, 8, 2):
            grad = dot(k.normed_v[:, 128 * d : 128 * d + 256], k.gproj_v[:, lo:hi], ((0,), (0,))).astype(BF)
            out[d : d + 2, :, at : at + hi - lo] = grad.reshape(2, 128, hi - lo)
            tick()

    mover.need(k.proj_v, k.segc_v, k.segr_v, k.par_v, k.spread_v, k.wide_v, k.ggated_v, k.y_v)
    gate_backward(k.proj_v, k.wide_v, k.y_v, k.ggated_v, k.gproj_v, k.ggated_v, tick)
    mover.need(k.normed_v)
    grad_of(Z0, Z0 + XW, k.gz_v, 0)
    sums[3].start()
    mover.need(k.states_v)
    tick.plan(14, 24)
    scan_backward(k.proj_v, k.segc_v, k.segr_v, k.par_v, k.spread_v, k.wide_v, k.y_v, k.states_v, k.ggated_v, k.gproj_v, k.gpar_v, k.gstate, tick)
    grad_of(X0, X0 + XW, k.xbc_v, 0)
    grad_of(B0, T0, k.xbc_v, XW)
    sums[4].start()
    tick.plan(13, 20)
    mover.need(k.gattn_v, k.attn_v, k.lse_v, k.cosine_v, k.sine_v)
    attention_backward(k.proj_v, k.cosine_v, k.sine_v, k.segc_v, k.segr_v, k.attn_v, k.lse_v, k.gattn_v, k.gproj_v, k.gkv, tick)
    grad_of(Q0, B0, k.qkv_v, 0)
    sums[5].start()
    tick.plan(6, 4)
    pair = (k.psend, k.precv)
    mover.need(k.w_in_v, k.rows_v, k.g_mid_v, k.gains_v, k.gffn_v)
    sent = []
    for j in range(2):
        rows = pl.ds(pl.multiple_of((2 * j + 1 - c) * span, span), span)
        k.opart_v[j] = dot(k.gproj_v[rows, :], k.w_in_v[...], ((1,), (1,))).astype(BF)
        sent.append(send(k.opart_v.at[j], k.ogot_v.at[j], pair, j, partner))
        tick()
    gain = k.gains_v[0:1, :]
    grad_gain = jnp.zeros((1, width), F32)
    columns = lambda d: pl.ds(pl.multiple_of(d * 128, 128), 128)
    sems = (k.dsend, k.drecv)
    for j in range(2):
        rows = pl.ds(pl.multiple_of((2 * j + c) * span, span), span)
        part = dot(k.gproj_v[rows, :], k.w_in_v[...], ((1,), (1,))).astype(BF).astype(F32)
        landed(k.ogot_v.at[j], pair, j, partner)
        g_h1 = (part + k.ogot_v[j].astype(F32)).astype(BF).astype(F32)
        unit, scale = rms_parts(k.rows_v[rows, :].astype(F32))
        grad_gain = grad_gain + jnp.sum(g_h1 * unit, axis=0, keepdims=True)
        k.ogot_v[j] = (k.g_mid_v[j] + rms_back(unit, scale, gain, g_h1)).astype(BF)
        tick()
    mover.store(k.ogot_v.at[y, :, columns(own)], k.returned.at[slot])
    for i, (r, a, b) in enumerate(others):
        d = 2 * (z ^ r) + (x ^ a)
        sent.append(send(k.ogot_v.at[y ^ b, :, columns(d)], k.returned.at[slot], sems, i, targets[i]))
    valid = lanes(1) < CHIP_HEADS
    heads = [jnp.where(valid, k.gpar_v[p : p + 1, :], 0.0) for p in range(3)]
    lines = [grad_gain, k.gffn_v[0:1, :]] + [jnp.concatenate([h] * (width // 128), axis=1) for h in heads]
    extra = jnp.concatenate([jnp.zeros((CHIP_HEADS, width), F32)] + lines + [jnp.zeros((STEP_ROWS - CHIP_HEADS - 5, width), F32)], axis=0)
    grad = dot(k.gproj_v[:, T0:COLS], k.normed_v[...], ((0,), (0,)))[0:STEP_ROWS, :] + extra
    for d in range(8):
        k.steps_v[d] = grad[:, 128 * d : 128 * (d + 1)].astype(BF)
    sums[6].start()
    tick.drain()
    for s in sums:
        s.finish(partner)
    for i, (r, a, b) in enumerate(others):
        landed(k.returned.at[2 * (2 * (z ^ r) + (x ^ a)) + (y ^ b)], sems, i, targets[i])
    for copy in sent:
        copy.wait_send()
    mover.flush()


STEP_ROWS = 32


def backward_stage(f, m, rows, w_in, tables):
    seq_len, width = rows.shape
    span = seq_len // 4
    cosine, sine, spread = tables
    inputs = dict(
        up=m.g_up,
        ssm=m.g_ssm,
        att=m.g_att,
        proj=f.proj,
        segc=f.segc,
        segr=f.segr,
        par=f.par,
        spread=spread,
        wide=f.wide,
        ggated=m.ggated,
        y=f.y,
        normed=f.normed,
        states=f.states,
        gattn=m.gattn,
        attn=f.attn,
        lse=f.lse,
        cosine=cosine,
        sine=sine,
        w_in=w_in,
        rows=rows,
        g_mid=m.g_mid,
        gains=f.gains,
        gffn=m.gffn,
    )
    block = width // 8
    new = dict(
        gz_v=(8, block, XW), xbc_v=(8, block, XW + 256), qkv_v=(8, block, QW + 128), steps_v=(8, STEP_ROWS, block)
    )
    parts = [m.g_up.shape, m.g_ssm.shape, m.g_att.shape] + list(new.values())
    out = [shape((2,) + d[1:]) for d in parts]
    outputs = dict(
        red_up=out[0],
        red_ssm=out[1],
        red_att=out[2],
        red_gz=out[3],
        red_xbc=out[4],
        red_qkv=out[5],
        red_steps=out[6],
    )
    spaces = {n: VM for n in outputs}
    outputs.update(returned=shape((16, span, 128)))
    bufs = reduce_scratch(parts)
    scratch = dict(
        **loaded(inputs),
        **bufs,
        **{n: VM(d, BF) for n, d in new.items()},
        gproj_v=VM((seq_len, COLS), BF),
        gpar_v=VM((8, 128), F32),
        gkv=VM((seq_len, 256), F32),
        gstate=VM((NS, XW), F32),
        opart_v=VM((2, span, width), BF),
        ogot_v=VM((2, span, width), BF),
        rsend=dma(len(parts) * REDUCE_SENDS),
        rrecv=dma(len(parts) * REDUCE_SENDS),
        psend=dma(2),
        precv=dma(2),
        dsend=dma(15),
        drecv=dma(15),
        local=dma(28),
    )
    return fused_call(with_lists(backward_fused, inputs, bufs), "mixer_backward", inputs, outputs, scratch, spaces, 3)


def finish_kernel(deal, up, gate, dn, ssm, att, gz, xbc, qkv, steps, returned, tokens, g_in, g_dt, g_ssm, g_att, g_gu, g_dn, small, sems):
    copies = [pltpu.make_async_copy(returned.at[j], tokens.at[deal[j]], sems.at[j]) for j in range(16)]
    for copy in copies:
        copy.start()
    wide = lambda v: v.astype(F32)
    inner = MH * HP
    q_start = 2 * inner + 2 * NS
    kv_start = q_start + QUERY_HEADS * HEAD_WIDTH
    half = dn.shape[1]
    for c in range(2):
        g_in[:, XW * c : XW * (c + 1)] = wide(gz[c])
        g_in[:, inner + XW * c : inner + XW * (c + 1)] = wide(xbc[c, :, 0:XW])
        g_in[:, q_start + QW * c : q_start + QW * (c + 1)] = wide(qkv[c, :, 0:QW])
        g_ssm[:, ssm.shape[2] * c : ssm.shape[2] * (c + 1)] = wide(ssm[c])
        g_att[:, att.shape[2] * c : att.shape[2] * (c + 1)] = wide(att[c])
        g_dn[half * c : half * (c + 1), :] = wide(dn[c])
        for d in range(8):
            at = (2 * d + c) * half
            g_gu[:, at : at + half] = wide(gate[c, :, half * d : half * (d + 1)])
            g_gu[:, FF + at : FF + at + half] = wide(up[c, :, half * d : half * (d + 1)])
    g_in[:, 2 * inner : q_start] = wide(xbc[0, :, XW:]) + wide(xbc[1, :, XW:])
    kv = [wide(qkv[c, :, QW : QW + 128]) for c in range(2)]
    low_lanes = lanes(kv[0].shape[0]) < 64
    g_in[:, kv_start : kv_start + 128] = jnp.where(low_lanes, kv[0], pltpu.roll(kv[1], 64, 1))
    g_in[:, kv_start + 128 : kv_start + 256] = jnp.where(low_lanes, pltpu.roll(kv[0], 64, 1), kv[1])
    first, second = wide(steps[0]), wide(steps[1])
    line = lax.broadcasted_iota(jnp.int32, first.shape, 0)
    heads = jnp.where(line < CHIP_HEADS, first, pltpu.roll(second, CHIP_HEADS, 0))
    heads = jnp.concatenate([heads, jnp.zeros((128 - STEP_ROWS, 128), F32)], axis=0).T
    g_dt[...] = heads[:, 0:MH]
    small[...] = jnp.zeros_like(small)
    for i in range(2):
        row = CHIP_HEADS + i
        small[i : i + 1, :] = first[row : row + 1, :] + second[row : row + 1, :]
    for i in range(3):
        row = CHIP_HEADS + 2 + i
        moved = pltpu.roll(second[row : row + 1, :], CHIP_HEADS, 1)
        small[2 + i : 3 + i, :] = jnp.where(lanes(1) < CHIP_HEADS, first[row : row + 1, :], moved)
    for copy in copies:
        copy.wait()


def finish_stage(deal, m, b, ssm_out, attn_out, down_proj, in_proj):
    returned = b.returned
    wide = lambda v: shape(v.shape, F32)
    block = in_proj.shape[0]
    return pl.pallas_call(
        finish_kernel,
        name="place_gradients",
        out_shape=(
            shape(returned.shape),
            wide(in_proj),
            shape((block, MH), F32),
            wide(ssm_out),
            wide(attn_out),
            shape((block, 2 * FF), F32),
            wide(down_proj),
            shape((8, 128), F32),
        ),
        in_specs=[pl.BlockSpec(memory_space=pltpu.SMEM)] + whole(10),
        out_specs=tuple(any_specs(1) + whole(7)),
        scratch_shapes=[dma(16)],
        compiler_params=pltpu.CompilerParams(vmem_limit_bytes=48 * MIB),
    )(deal, b.red_up, m.red_gate, m.red_dn, b.red_ssm, b.red_att, b.red_gz, b.red_xbc, b.red_qkv, b.red_steps, returned)


def mixer_tables(seq_len):
    half = HEAD_WIDTH // 2
    frequency = np.float32(THETA) ** (-np.arange(half, dtype=np.float32) * np.float32(2.0 / HEAD_WIDTH))
    angles = np.arange(seq_len, dtype=np.float32)[:, None] * frequency[None, :].astype(np.float32)
    cosine = np.tile(np.cos(angles), (1, 4)).astype(np.float32)
    sine = np.tile(np.concatenate([-np.sin(angles), np.sin(angles)], axis=1), (1, 2)).astype(np.float32)
    head_of = np.arange(XW) // HP
    spread = np.arange(128)[:, None] % 64 == head_of[None, :]
    return jnp.asarray(cosine), jnp.asarray(sine), jnp.asarray(spread, BF)


def fused_layer(dealt, cot, seq_lengths, deal_order, gains, in_proj, dt_proj, head_values, ssm_out, attn_out, gate_up, down_proj):
    block = in_proj.shape[0]
    width = cot.shape[2]
    seq_len = 4 * cot.shape[1]
    beside = jnp.concatenate([dt_proj] + [g[:, None] for g in gains] + [jnp.zeros((block, 128 - MH - 2), BF)], axis=1)
    heads = jnp.pad(jnp.stack(head_values), ((0, 5), (0, 128 - MH)))
    tables = mixer_tables(seq_len)
    rows, w_in = start_transfers(dealt, in_proj, beside)
    rows, w_in = rows.reshape(seq_len, width), w_in.reshape(width, COLS)
    first = forward_stage(rows, w_in, tables, heads, deal_order, seq_lengths, cot, (ssm_out, attn_out, gate_up, down_proj))
    mid = feed_forward_stage(first)
    last = backward_stage(first, mid, rows, w_in, tables)
    tokens, g_in, g_dt, g_ssm, g_att, g_gu, g_dn, small = finish_stage(deal_order, mid, last, ssm_out, attn_out, down_proj, in_proj)
    heads = [small[2 + i, :MH] for i in range(3)]
    return (mid.output, tokens, small[0], g_in, g_dt, *heads, g_ssm, g_att, small[1], g_gu, g_dn)


def rms_parts(v):
    scale = lax.rsqrt(jnp.mean(v * v, axis=-1, keepdims=True) + EPS)
    return v * scale, scale


def rms_back(normed, scale, gain, grad):
    inner = grad * gain
    return scale * (inner - normed * jnp.mean(inner * normed, axis=-1, keepdims=True))


def silu(v):
    return v / (1.0 + jnp.exp(-v))


def low(v):
    return v.astype(BF)


def plain_start(dealt, cot, w, y):
    arrived = lax.all_to_all(dealt, "dp", split_axis=0, concat_axis=2, tiled=True)
    rows = lax.all_gather(arrived, "seq", axis=1, tiled=True)
    cots = lax.all_gather(cot, "seq", axis=1, tiled=True)
    pick = lambda v: lax.dynamic_index_in_dim(v, y, 0, keepdims=False)
    return pick(rows), lax.all_gather(w, "dp", axis=0, tiled=True), pick(cots)


def plain_gather(ssm, att, gu, dn, c):
    every = [lax.all_gather(v, "dp", axis=0, tiled=True) for v in (ssm, att, gu, dn)]
    out = []
    for v in every[:2]:
        rows = v.shape[0] // 2
        mine = lax.all_gather(v, "seq", axis=1, tiled=True)[:, : 2 * v.shape[1]]
        out.append(lax.dynamic_slice_in_dim(mine, c * rows, rows))
    return out + every[2:]


def plain_pair(part):
    return lax.ppermute(part, "seq", [(0, 1), (1, 0), (2, 3), (3, 2)])


def plain_reduce(parts, out_rows, gx, y, c):
    reduced = []
    for p in parts:
        total = lax.psum_scatter(p.reshape(-1, p.shape[-1]), "dp", scatter_dimension=0, tiled=True)
        every = lax.all_gather(total, "seq", axis=0).astype(F32)
        reduced.append(jnp.stack([every[0] + every[2], every[1] + every[3]]))
    peer = lax.ppermute(out_rows, "seq", [(0, 2), (1, 3), (2, 0), (3, 1)])
    output = jnp.where(jnp.arange(2)[:, None, None] == y, out_rows, jnp.flip(peer, 0))
    whole_rows = lax.all_gather(gx, "seq", axis=0)
    slot = 2 * y + c
    by_pack = lax.dynamic_index_in_dim(whole_rows, c, 0, False), lax.dynamic_index_in_dim(whole_rows, c + 2, 0, False)
    both = jnp.stack([lax.dynamic_index_in_dim(v, y, 0, False) for v in by_pack])
    returned = lax.all_to_all(both, "dp", split_axis=2, concat_axis=0, tiled=True)
    return reduced, output, returned


def plain_layer(dealt, cot, w_in, shards, consts, y, c):
    groups = lax.axis_size("dp")
    rows, w_in, cots = plain_start(dealt, cot, w_in, y)
    w_ssm, w_att, w_gu, w_dn = plain_gather(*shards, c)
    span, width = cot.shape[1:]
    block = width // groups
    cut = lambda v, start, size: lax.dynamic_slice_in_dim(v, start, size, axis=1)

    x = rows.astype(F32)
    gain_in = w_in[:, T0 + CHIP_HEADS].astype(F32)[None, :]
    gain_ffn = w_in[:, T0 + CHIP_HEADS + 1].astype(F32)[None, :]
    unit_in, scale_in = rms_parts(x)
    normed = low(unit_in * gain_in)
    proj = low(dot(normed, w_in))
    gated, *saved = mixer_forward(proj, consts)
    attn = saved[0]
    part = low(dot(gated, w_ssm) + dot(attn, w_att))
    middle = x + (part.astype(F32) + plain_pair(part).astype(F32))
    unit_ffn, scale_ffn = rms_parts(middle)
    normed_two = low(unit_ffn * gain_ffn)
    gu = low(dot(normed_two, w_gu)).astype(F32)
    gate, up = gu[:, : FF // 2], gu[:, FF // 2 :]
    act = low(silu(gate) * up)
    out_part = low(dot(act, w_dn))
    by_core = lambda v: lax.dynamic_index_in_dim(v.reshape(2, 2, span, width), c, 1, keepdims=False)
    out_rows = low(by_core(middle) + (by_core(out_part).astype(F32) + by_core(plain_pair(out_part)).astype(F32)))

    g_act = low(dot(cots, w_dn, ((1,), (1,)))).astype(F32)
    grad_dn = low(dot(act, cots, ((0,), (0,))))
    sig = 1.0 / (1.0 + jnp.exp(-gate))
    g_gu = low(jnp.concatenate([g_act * up * (sig * (1.0 + gate * (1.0 - sig))), g_act * (gate * sig)], axis=1))
    grad_gu = low(dot(normed_two, g_gu, ((0,), (0,))))
    part = low(dot(g_gu, w_gu, ((1,), (1,))))
    g_two = low(part.astype(F32) + plain_pair(part).astype(F32)).astype(F32)
    g_mid = cots.astype(F32) + rms_back(unit_ffn, scale_ffn, gain_ffn, g_two)
    grad_gain_ffn = 0.5 * jnp.sum(g_two * unit_ffn, axis=0)
    g_branch = low(g_mid)
    g_gated = low(dot(g_branch, w_ssm, ((1,), (1,))))
    g_attn = low(dot(g_branch, w_att, ((1,), (1,))))
    grad_ssm = low(dot(gated, g_branch, ((0,), (0,))))
    grad_att = low(dot(attn, g_branch, ((0,), (0,))))
    g_proj, g_par = mixer_backward(proj, consts, saved, g_gated, g_attn)
    grad_in = dot(normed, g_proj, ((0,), (0,)))
    part = low(dot(g_proj, w_in, ((1,), (1,))))
    g_h1 = low(by_core(part).astype(F32) + by_core(plain_pair(part)).astype(F32)).astype(F32)
    scale_rows = by_core(jnp.broadcast_to(scale_in, x.shape))
    g_x = low(by_core(g_mid) + rms_back(by_core(unit_in), scale_rows, gain_in, g_h1))
    grad_gain_in = jnp.sum(g_h1 * by_core(unit_in), axis=(0, 1))
    head_grads = jnp.tile(jnp.pad(g_par[:3, :CHIP_HEADS].T, ((0, block - CHIP_HEADS), (0, 0))), (groups, 1))
    extra = jnp.concatenate([grad_gain_in[:, None], grad_gain_ffn[:, None], head_grads], axis=1)
    grad_in = low(lax.dynamic_update_slice(grad_in, extra, (0, T0 + CHIP_HEADS)))

    by_block = lambda v: v.reshape(groups, -1, v.shape[-1])
    parts = [by_block(grad_in), by_block(grad_dn), by_block(grad_gu)]
    for v in (grad_ssm, grad_att):
        both = jnp.stack([v, plain_pair(v)])
        both = jnp.where(c == 0, both, both[::-1]).reshape(-1, width)
        parts.append(by_block(cut(both, width // 2 * c, width // 2)))
    reduced, output, returned = plain_reduce(parts, out_rows, g_x, y, c)
    return output, returned, reduced


def body(tokens, cot, seq_lengths, deal_order, in_gain, in_proj, dt_proj, dt_bias, a_log, d_skip, ssm_out, attn_out, ffn_gain, gate_up, down_proj):
    groups = lax.axis_size("dp")
    dealt = tokens.at[deal_order].get(mode="promise_in_bounds")
    if groups == 8:
        return fused_layer(
            dealt, cot, seq_lengths, deal_order, (in_gain, ffn_gain), in_proj, dt_proj, (dt_bias, a_log, d_skip), ssm_out, attn_out, gate_up, down_proj
        )
    dp_index, seq_index = lax.axis_index("dp"), lax.axis_index("seq")
    y, c = seq_index // 2, seq_index % 2
    packs, span, width = cot.shape
    seq_len = span * lax.axis_size("seq")
    inner = MH * HP
    block = in_proj.shape[0]

    cut = lambda v, start, size: lax.dynamic_slice_in_dim(v, start, size, axis=1)
    q_start = 2 * inner + 2 * NS
    k_start = q_start + QUERY_HEADS * HEAD_WIDTH
    v_start = k_start + KEY_VALUE_HEADS * HEAD_WIDTH
    w_in = jnp.concatenate(
        [
            cut(in_proj, XW * c, XW),
            cut(in_proj, inner + XW * c, XW),
            cut(in_proj, q_start + QW * c, QW),
            cut(in_proj, k_start + HEAD_WIDTH * c, HEAD_WIDTH),
            cut(in_proj, v_start + HEAD_WIDTH * c, HEAD_WIDTH),
            in_proj[:, 2 * inner : q_start],
            cut(dt_proj, CHIP_HEADS * c, CHIP_HEADS),
            in_gain[:, None],
            ffn_gain[:, None],
            jnp.zeros((block, 128 - CHIP_HEADS - 2), BF),
        ],
        axis=1,
    )
    half_units = down_proj.shape[0] // 2
    w_gu = gate_up.reshape(block, 2, groups, 2, half_units)
    w_gu = lax.dynamic_index_in_dim(w_gu, c, 3, keepdims=False).reshape(block, FF)
    w_dn = lax.dynamic_slice_in_dim(down_proj, half_units * c, half_units, axis=0)
    w_ssm = cut(ssm_out, width // 2 * c, width // 2)
    w_att = cut(attn_out, width // 2 * c, width // 2)

    pack = lax.dynamic_index_in_dim(deal_order, dp_index * packs + y, 0, keepdims=False)
    ends = jnp.cumsum(lax.dynamic_index_in_dim(seq_lengths, pack, 0, keepdims=False))[:-1]
    places = jnp.arange(seq_len, dtype=jnp.int32)
    seg = jnp.sum((places[:, None] >= ends[None, :]).astype(jnp.int32), axis=1)
    segc = jnp.broadcast_to(seg[:, None], (seq_len, 128))
    segr = jnp.broadcast_to(seg[None, :], (8, seq_len))
    half = HEAD_WIDTH // 2
    frequency = THETA ** (-jnp.arange(half, dtype=F32) * 2.0 / HEAD_WIDTH)
    angles = places.astype(F32)[:, None] * frequency[None, :]
    cosine = jnp.tile(jnp.cos(angles), (1, 4))
    sine = jnp.tile(jnp.concatenate([-jnp.sin(angles), jnp.sin(angles)], axis=1), (1, 2))
    own_heads = lambda v: lax.dynamic_slice_in_dim(v, CHIP_HEADS * c, CHIP_HEADS)
    par = jnp.zeros((8, 128), F32)
    par = par.at[0, :CHIP_HEADS].set(own_heads(dt_bias)).at[1, :CHIP_HEADS].set(-jnp.exp(own_heads(a_log)))
    wide = jnp.broadcast_to(jnp.repeat(own_heads(d_skip), HP)[None, :], (8, XW))
    head_of = jnp.arange(XW) // HP
    spread = (jnp.arange(128)[:, None] % 64 == head_of[None, :]).astype(BF)
    consts = (cosine, sine, segc, segr, par, spread, wide)

    shards = (w_ssm, w_att, w_gu, w_dn)
    output, returned, (r_in, r_dn, r_gu, r_ssm, r_att) = plain_layer(dealt, cot, w_in, shards, consts, y, c)

    both = lambda start, size: [r_in[0, :, start : start + size], r_in[1, :, start : start + size]]
    grad_in_proj = jnp.concatenate(
        both(Z0, XW)
        + both(X0, XW)
        + [r_in[0, :, B0:T0] + r_in[1, :, B0:T0]]
        + both(Q0, QW)
        + both(KV0, HEAD_WIDTH)
        + both(KV0 + HEAD_WIDTH, HEAD_WIDTH),
        axis=1,
    )
    grad_dt_proj = jnp.concatenate(both(T0, CHIP_HEADS), axis=1)
    tail = r_in[:, :, T0 + CHIP_HEADS : T0 + CHIP_HEADS + 5]
    gains = tail[0, :, :2] + tail[1, :, :2]
    heads = tail[:, :CHIP_HEADS, 2:5].reshape(MH, 3)
    grad_gate_up = jnp.stack(
        [r_gu[k].reshape(block, 2, groups, half_units) for k in range(2)], axis=3
    ).reshape(block, 2 * FF)
    side = lambda v: jnp.concatenate([v[0], v[1]], axis=1)
    return (
        output,
        jnp.take(returned, jnp.argsort(deal_order), axis=0),
        gains[:, 0],
        grad_in_proj,
        grad_dt_proj,
        heads[:, 0],
        heads[:, 1],
        heads[:, 2],
        side(r_ssm),
        side(r_att),
        gains[:, 1],
        grad_gate_up,
        r_dn.reshape(-1, width),
    )


def solution(mesh):
    return jax.shard_map(
        body,
        mesh=mesh,
        in_specs=(
            P(None, "seq", "dp"),
            P("dp", "seq", None),
            P(),
            P(),
            P("dp"),
            P("dp", None),
            P("dp", None),
            P(),
            P(),
            P(),
            P("dp", None),
            P("dp", None),
            P("dp"),
            P("dp", None),
            P("dp", None),
        ),
        out_specs=(
            P("dp", "seq", None),
            P(None, "seq", "dp"),
            P("dp"),
            P("dp", None),
            P("dp", None),
            P(),
            P(),
            P(),
            P("dp", None),
            P("dp", None),
            P("dp"),
            P("dp", None),
            P("dp", None),
        ),
        check_vma=False,
    )
```

```python
import types

import jax
import jax.numpy as jnp
import numpy as np
from jax import lax
from jax.experimental import pallas as pl
from jax.experimental.pallas import tpu as pltpu
from jax.sharding import PartitionSpec as P

FF = 2048
QUERY_HEADS = 8
KEY_VALUE_HEADS = 2
HEAD_WIDTH = 64
MH = 24
HP = 64
NS = 128
EPS = 1e-05
THETA = 100000000000.0
BF = jnp.bfloat16
F32 = jnp.float32
CORES = 2
CHIP_HEADS = MH // CORES
XW = CHIP_HEADS * HP
QW = QUERY_HEADS // CORES * HEAD_WIDTH
Z0, X0, Q0, KV0, B0, C0, T0 = 0, XW, 2 * XW, 2 * XW + QW, 2 * XW + QW + 128, 2 * XW + QW + 256, 2 * XW + QW + 384
COLS = T0 + 128
CHUNK = 256
QB = 256
FAR = -1e30
MIB = 1 << 20
MESH = pl.DeviceIdType.MESH
VM = pltpu.VMEM


def dot(a, b, dims=((1,), (0,)), precision=None):
    return lax.dot_general(a, b, (dims, ((), ())), precision=precision, preferred_element_type=F32)


def lanes(rows, width=128):
    return lax.broadcasted_iota(jnp.int32, (rows, width), 1)


def swap_halves(v):
    low = lanes(v.shape[0], v.shape[1]) % 64 < 32
    return jnp.where(low, pltpu.roll(v, v.shape[1] - 32, 1), pltpu.roll(v, 32, 1))


def turn(v, cosine, sine):
    return v * cosine + swap_halves(v) * sine


def turn_back(v, cosine, sine):
    return v * cosine - swap_halves(v) * sine


def widen(v, spread):
    v = jnp.where(lanes(v.shape[0]) < 64, v, 0.0)
    top = v.astype(BF)
    rest = (v - top.astype(F32)).astype(BF).astype(F32)
    both = top.astype(F32) + pltpu.roll(rest, 64, 1)
    return dot(both.astype(BF), spread)


def attn_masks(segc_ref, segr_ref, i, upto):
    rows = pl.ds(i * QB, QB)
    same = segc_ref[rows, 0:1] == segr_ref[0:1, 0:upto]
    t = lax.broadcasted_iota(jnp.int32, (QB, upto), 0) + i * QB
    u = lax.broadcasted_iota(jnp.int32, (QB, upto), 1)
    return jnp.where(same & (u <= t), 0.0, FAR)


def key_value_pairs(kv, cosine, sine):
    low = lanes(kv.shape[0]) < 64
    other = pltpu.roll(kv, 64, 1)
    kk = turn(jnp.where(low, kv, other), cosine, sine)
    vv = jnp.where(low, other, kv)
    return kk.astype(BF), vv.astype(BF)


def attention_forward(proj_ref, cos_ref, sin_ref, segc_ref, segr_ref, attn_ref, lse_ref, tick):
    seq_len = proj_ref.shape[0]
    kk, vv = key_value_pairs(proj_ref[:, KV0 : KV0 + 128].astype(F32), cos_ref[...], sin_ref[...])
    low = lanes(QB) < 64
    for i in range(seq_len // QB):
        rows = slice(i * QB, (i + 1) * QB)
        upto = (i + 1) * QB
        mask = attn_masks(segc_ref, segr_ref, i, upto)
        tops = jnp.zeros((QB, 128), F32)
        for pair in range(QW // 128):
            q = proj_ref[rows, Q0 + 128 * pair : Q0 + 128 * (pair + 1)].astype(F32)
            q = turn(q, cos_ref[rows, :], sin_ref[rows, :]) * HEAD_WIDTH**-0.5
            outs = []
            for half in range(2):
                qh = jnp.where(low if half == 0 else ~low, q, 0.0).astype(BF)
                s = dot(qh, kk[:upto], ((1,), (1,))) + mask
                top = jnp.max(s, axis=1, keepdims=True)
                e = jnp.exp(s - top)
                total = jnp.sum(e, axis=1, keepdims=True)
                outs.append(dot(e.astype(BF), vv[:upto]) / total)
                tops = jnp.where(lanes(QB) == 2 * pair + half, top + jnp.log(total), tops)
                tick()
            attn_ref[rows, 128 * pair : 128 * (pair + 1)] = jnp.where(low, outs[0], outs[1]).astype(BF)
        lse_ref[rows, :] = tops


def attention_backward(proj_ref, cos_ref, sin_ref, segc_ref, segr_ref, attn_ref, lse_ref, gattn_ref, gproj_ref, gkv, tick):
    seq_len = proj_ref.shape[0]
    kk, vv = key_value_pairs(proj_ref[:, KV0 : KV0 + 128].astype(F32), cos_ref[...], sin_ref[...])
    low = lanes(QB) < 64
    gkv[...] = jnp.zeros_like(gkv)
    pick = (lax.broadcasted_iota(jnp.int32, (QW, 128), 0) // 64 == lanes(QW)).astype(BF)
    for i in range(seq_len // QB):
        rows = slice(i * QB, (i + 1) * QB)
        upto = (i + 1) * QB
        same = segc_ref[0:upto, 0:1] == segr_ref[0:1, rows]
        t = lanes(upto, QB) + i * QB
        u = lax.broadcasted_iota(jnp.int32, (upto, QB), 0)
        mask = jnp.where(same & (u <= t), 0.0, FAR)
        weighed = gattn_ref[rows, :].astype(F32) * attn_ref[rows, :].astype(F32)
        deltas = dot(weighed.astype(BF), pick).T
        tops = lse_ref[rows, :].T
        for pair in range(QW // 128):
            cosine, sine = cos_ref[rows, :], sin_ref[rows, :]
            q = proj_ref[rows, Q0 + 128 * pair : Q0 + 128 * (pair + 1)].astype(F32)
            q = turn(q, cosine, sine) * HEAD_WIDTH**-0.5
            g = gattn_ref[rows, 128 * pair : 128 * (pair + 1)]
            grads = []
            for half in range(2):
                head = 2 * pair + half
                mine = low if half == 0 else ~low
                qh = jnp.where(mine, q, 0.0).astype(BF)
                gh = jnp.where(mine, g, jnp.zeros_like(g))
                s = dot(kk[:upto], qh, ((1,), (1,))) + mask
                p = jnp.exp(s - tops[head : head + 1, :])
                gp = dot(vv[:upto], gh, ((1,), (1,)))
                gs = (p * (gp - deltas[head : head + 1, :])).astype(BF)
                gkv[0:upto, 0:128] += dot(gs, qh)
                gkv[0:upto, 128:256] += dot(p.astype(BF), gh)
                grads.append(dot(gs, kk[:upto], ((0,), (0,))))
                tick()
            gq = jnp.where(low, grads[0], grads[1]) * HEAD_WIDTH**-0.5
            gproj_ref[rows, Q0 + 128 * pair : Q0 + 128 * (pair + 1)] = turn_back(gq, cosine, sine).astype(BF)
    gk = gkv[:, 0:128]
    gv = gkv[:, 128:256]
    gk = turn_back(gk + pltpu.roll(gk, 64, 1), cos_ref[...], sin_ref[...])
    gv = gv + pltpu.roll(gv, 64, 1)
    gproj_ref[:, KV0 : KV0 + 128] = jnp.where(lanes(seq_len) < 64, gk, gv).astype(BF)


def scan_pieces(j, proj_ref, segc_ref, segr_ref, par_ref):
    rows = pl.ds(j * CHUNK, CHUNK)
    seg = segc_ref[rows, :]
    prev = segc_ref[pl.ds(j * CHUNK - 1, 1), :] if j else jnp.full((1, 128), -1, jnp.int32)
    last = segc_ref[pl.ds(j * CHUNK + CHUNK - 1, 1), :]
    valid = lanes(CHUNK) < CHIP_HEADS
    raw = proj_ref[rows, T0 : T0 + 128].astype(F32) + par_ref[0:1, :]
    dt = jnp.where(valid, jnp.maximum(raw, 0.0) + jnp.log1p(jnp.exp(-jnp.abs(raw))), 0.0)
    decay = dt * par_ref[1:2, :]
    place = lax.broadcasted_iota(jnp.int32, (CHUNK, CHUNK), 0)
    under = (place >= lanes(CHUNK, CHUNK)).astype(F32)
    cum = dot(under, decay, precision=lax.Precision.HIGHEST)
    end = cum[CHUNK - 1 : CHUNK, :]
    from_start = jnp.where(seg == prev, jnp.exp(cum), 0.0)
    to_end = jnp.where(seg == last, jnp.exp(end - cum), 0.0)
    keep = jnp.where(last == prev, jnp.exp(end), 0.0)
    return rows, raw, dt, decay, cum, from_start, to_end, keep, under


def scan_forward(proj_ref, segc_ref, segr_ref, par_ref, spread_ref, wide_ref, gated_ref, y_ref, states_ref, state, tick):
    spread = spread_ref[...]
    state[...] = jnp.zeros_like(state)

    for j in range(proj_ref.shape[0] // CHUNK):
        rows, raw, dt, decay, cum, from_start, to_end, keep, under = scan_pieces(j, proj_ref, segc_ref, segr_ref, par_ref)
        place = lax.broadcasted_iota(jnp.int32, (CHUNK, CHUNK), 0)
        same = segc_ref[rows, 0:1] == segr_ref[0:1, rows]
        mask = jnp.where(same & (place >= lanes(CHUNK, CHUNK)), 0.0, FAR)
        cum_t = cum.T
        b = proj_ref[rows, B0 : B0 + 128]
        c = proj_ref[rows, C0 : C0 + 128]
        cb = dot(c, b, ((1,), (1,)))
        x = proj_ref[rows, X0 : X0 + XW].astype(F32)
        xdt = x * widen(dt, spread)
        xdt_low = xdt.astype(BF)
        old = state[...]
        states_ref[j] = old
        y_state = dot(c, old.astype(BF)) * widen(from_start, spread)
        low = lanes(CHUNK) < 64
        for pair in range(CHIP_HEADS // 2):
            cols = slice(128 * pair, 128 * (pair + 1))
            xp = xdt_low[:, cols]
            local = y_state[:, cols]
            for half in range(2):
                h = 2 * pair + half
                spread_h = jnp.exp(cum[:, h : h + 1] - cum_t[h : h + 1, :] + mask)
                mix = (cb * spread_h).astype(BF)
                xh = jnp.where(low if half == 0 else ~low, xp, jnp.zeros_like(xp))
                local = local + dot(mix, xh)
            y_ref[rows, cols] = local
            y = (local + x[:, cols] * wide_ref[0:1, cols]).astype(BF).astype(F32)
            z = proj_ref[rows, Z0 + 128 * pair : Z0 + 128 * (pair + 1)].astype(F32)
            gated_ref[rows, cols] = (y * (z / (1.0 + jnp.exp(-z)))).astype(BF)
            tick()
        weighted = (xdt * widen(to_end, spread)).astype(BF)
        keep_wide = widen(jnp.broadcast_to(keep, (8, 128)), spread)[0:1, :]
        state[...] = old * keep_wide + dot(b, weighted, ((0,), (0,)))


def gate_backward(proj_ref, wide_ref, y_ref, ggated_ref, gproj_ref, gy_ref, tick):
    for j in range(proj_ref.shape[0] // CHUNK):
        rows = pl.ds(j * CHUNK, CHUNK)
        x = proj_ref[rows, X0 : X0 + XW].astype(F32)
        z = proj_ref[rows, Z0 : Z0 + XW].astype(F32)
        gg = ggated_ref[rows, :].astype(F32)
        y = (y_ref[rows, :] + x * wide_ref[0:1, :]).astype(BF).astype(F32)
        sig = 1.0 / (1.0 + jnp.exp(-z))
        gy_ref[rows, :] = (gg * (z * sig)).astype(BF)
        gproj_ref[rows, Z0 : Z0 + XW] = (gg * y * (sig * (1.0 + z * (1.0 - sig)))).astype(BF)
        tick()


def scan_backward(proj_ref, segc_ref, segr_ref, par_ref, spread_ref, wide_ref, y_ref, states_ref, gy_ref, gproj_ref, gpar_ref, gstate, tick):
    spread = spread_ref[...]
    gstate[...] = jnp.zeros_like(gstate)
    gpar_ref[...] = jnp.zeros_like(gpar_ref)
    chunks = proj_ref.shape[0] // CHUNK

    def narrow(v):
        top = v.astype(BF)
        rest = (v - top.astype(F32)).astype(BF)
        return dot(top, spread, ((1,), (1,))) + dot(rest, spread, ((1,), (1,)))

    for j in reversed(range(chunks)):
        rows, raw, dt, decay, cum, from_start, to_end, keep, under = scan_pieces(j, proj_ref, segc_ref, segr_ref, par_ref)
        place = lax.broadcasted_iota(jnp.int32, (CHUNK, CHUNK), 0)
        same = segc_ref[rows, 0:1] == segr_ref[0:1, rows]
        mask = jnp.where(same & (place <= lanes(CHUNK, CHUNK)), 0.0, FAR)
        cum_t = cum.T
        b = proj_ref[rows, B0 : B0 + 128]
        c = proj_ref[rows, C0 : C0 + 128]
        bc = dot(b, c, ((1,), (1,)))
        x = proj_ref[rows, X0 : X0 + XW].astype(F32)
        dt_wide = widen(dt, spread)
        xdt_low = (x * dt_wide).astype(BF)
        start_wide = widen(from_start, spread)
        end_wide = widen(to_end, spread)
        old = states_ref[j]
        gnew = gstate[...]
        y_own = y_ref[rows, :]
        gy_low = gy_ref[rows, :]
        gy = gy_low.astype(F32)
        gx_state = end_wide * dot(b, gnew.astype(BF))
        gbc = jnp.zeros((CHUNK, CHUNK), F32)
        low = lanes(CHUNK) < 64
        gxdt = []
        for pair in range(CHIP_HEADS // 2):
            cols = slice(128 * pair, 128 * (pair + 1))
            xp, gp = xdt_low[:, cols], gy_low[:, cols]
            total = gx_state[:, cols]
            for half in range(2):
                h = 2 * pair + half
                mine = low if half == 0 else ~low
                spread_h = jnp.exp(cum_t[h : h + 1, :] - cum[:, h : h + 1] + mask)
                mix = (bc * spread_h).astype(BF)
                gh = jnp.where(mine, gp, jnp.zeros_like(gp))
                total = total + dot(mix, gh)
                gbc = gbc + dot(xp, gh, ((1,), (1,))) * spread_h
            gxdt.append(total)
            tick()
        gxdt = jnp.concatenate(gxdt, axis=1)
        gstart = (gy * start_wide).astype(BF)
        weighted = (xdt_low.astype(F32) * end_wide).astype(BF)
        gbc_low = gbc.astype(BF)
        gnew_low, old_low = gnew.astype(BF), old.astype(BF)
        gproj_ref[rows, C0 : C0 + 128] = (dot(gbc_low, b, ((0,), (0,))) + dot(gstart, old_low, ((1,), (1,)))).astype(BF)
        gproj_ref[rows, B0 : B0 + 128] = (dot(gbc_low, c) + dot(weighted, gnew_low, ((1,), (1,)))).astype(BF)
        keep_wide = widen(jnp.broadcast_to(keep, (8, 128)), spread)[0:1, :]
        kept = jnp.sum(old * gnew, axis=0, keepdims=True) * keep_wide
        gstate[...] = gnew * keep_wide + dot(c, gstart, ((0,), (0,)))
        xdt_f = xdt_low.astype(F32)
        gcum = narrow(gy * y_own) - narrow(xdt_f * gxdt)
        at_end = jnp.sum(xdt_f * gx_state, axis=0, keepdims=True) + kept
        at_end = narrow(jnp.broadcast_to(at_end, (8, XW)))[0:1, :]
        gdecay = dot(under, gcum, ((0,), (0,)), precision=lax.Precision.HIGHEST) + at_end
        gdt = narrow(gxdt * x) + gdecay * par_ref[1:2, :]
        graw = gdt / (1.0 + jnp.exp(-raw))
        graw = jnp.where(lanes(CHUNK) < CHIP_HEADS, graw, 0.0)
        gproj_ref[rows, T0 : T0 + 128] = graw.astype(BF)
        gproj_ref[rows, X0 : X0 + XW] = (gxdt * dt_wide + gy * wide_ref[0:1, :]).astype(BF)
        gpar_ref[0:1, :] += jnp.sum(graw, axis=0, keepdims=True)
        gpar_ref[1:2, :] += jnp.sum(gdecay * decay, axis=0, keepdims=True)
        skip = jnp.sum(gy * x, axis=0, keepdims=True)
        gpar_ref[2:3, :] += narrow(jnp.broadcast_to(skip, (8, XW)))[0:1, :]


class Ticker:
    def __init__(self, steps, ticks=1):
        self.steps, self.done = steps, 0
        self.plan(len(steps), ticks)

    def plan(self, count, ticks):
        self.first, self.last = self.done, min(self.done + count, len(self.steps))
        self.ticks, self.calls = ticks, 0

    def run(self, upto):
        while self.done < upto:
            if not isinstance(self.steps[self.done], int):
                self.steps[self.done]()
            self.done += 1

    def __call__(self):
        self.calls = min(self.calls + 1, self.ticks)
        self.run(self.first + (self.last - self.first) * self.calls // self.ticks)

    def reach(self, mark):
        if mark in self.steps[self.done :]:
            self.run(self.steps.index(mark) + 1)

    def drain(self):
        self.run(len(self.steps))


def whole(n):
    return [pl.BlockSpec(memory_space=VM)] * n


def place():
    d, s = lax.axis_index("dp"), lax.axis_index("seq")
    return d // 2, d % 2, s // 2, s % 2


def device(z, x, y, c):
    return (2 * z + x, 2 * y + c)


def greet(peers):
    barrier = pltpu.get_barrier_semaphore()
    for peer in peers:
        pl.semaphore_signal(barrier, inc=1, device_id=peer, device_id_type=MESH)
    pl.semaphore_wait(barrier, len(peers))


def send(src, dst, sems, k, target):
    copy = pltpu.make_async_remote_copy(
        src_ref=src, dst_ref=dst, send_sem=sems[0].at[k], recv_sem=sems[1].at[k], device_id=target, device_id_type=MESH
    )
    copy.start()
    return copy


def landed(dst, sems, k, target):
    pltpu.make_async_remote_copy(
        src_ref=dst, dst_ref=dst, send_sem=sems[0].at[k], recv_sem=sems[1].at[k], device_id=target, device_id_type=MESH
    ).wait_recv()


ARRAY_SENDS = 14
CORNER_X = 3
W_CUTS = 3


class Gather:
    def __init__(self, src, dst, sems, base, local_sem):
        self.src, self.dst, self.sems, self.base = src, dst, sems, base
        self.local_sem = local_sem
        self.z, self.x, self.y, self.c = place()
        half = src.shape[0] // 2
        self.mine = pl.ds(self.y * half, half)
        self.other = pl.ds((1 - self.y) * half, half)
        self.sent, self.sent_inner = [], []
        self.inner = (self.z == 1) | (self.z == 2)
        self.xpeer = device(self.z, 1 - self.x, self.y, self.c)
        self.ypeer = device(self.z, self.x, 1 - self.y, self.c)

    def push_inner(self, k, src, dst, target):
        def copy():
            return pltpu.make_async_remote_copy(
                src_ref=src,
                dst_ref=dst,
                send_sem=self.sems[0].at[self.base + k],
                recv_sem=self.sems[1].at[self.base + 2],
                device_id=target,
                device_id_type=MESH,
            )

        pl.when(self.inner)(lambda: copy().start())
        self.sent_inner.append(copy)

    def block(self, r, x, rows):
        return self.dst.at[2 * (self.z ^ r) + x, rows]

    def push(self, k, ref, target, dst=None):
        self.sent.append(send(ref, ref if dst is None else dst, self.sems, self.base + k, target))

    def start(self):
        own = 2 * self.z + self.x
        self.local = pltpu.make_async_copy(self.src, self.dst.at[own], self.local_sem)
        self.local.start()
        for r in (1, 2):
            target = device(self.z ^ r, self.x, self.y, self.c)
            self.push(r - 1, self.src.at[self.mine], target, self.dst.at[own, self.mine])
        target = device(self.z ^ 3, self.x, self.y, self.c)
        self.push_inner(2, self.src.at[self.mine], self.dst.at[own, self.mine], target)
        self.push(3, self.src, self.xpeer, self.dst.at[own])

    def cross(self):
        landed(self.block(0, 1 - self.x, slice(None)), self.sems, self.base + 3, self.xpeer)
        self.push(4, self.block(0, 1 - self.x, self.mine), device(self.z ^ 1, self.x, self.y, self.c))

    def forward(self, r):
        ref = self.block(r, self.x, self.mine)
        landed(ref, self.sems, self.base + r - 1, self.xpeer)
        if r == 2:
            self.push_inner(13, ref, ref, device(self.z ^ 1, self.x, self.y, self.c))
        self.push(6 + r, ref, self.ypeer)
        if r > 1:
            self.push(3 + r, ref, self.xpeer)

    def corner(self, r):
        if r == CORNER_X:
            ref = self.block(r, self.x, self.other)
            landed(ref, self.sems, self.base + 6 + r, self.ypeer)
            self.push(9 + r, ref, self.xpeer)
        else:
            ref = self.block(r, 1 - self.x, self.mine)
            landed(ref, self.sems, self.base + 3 + r, self.xpeer)
            self.push(9 + r, ref, self.ypeer)

    def arrive(self):
        for r in (1, 2, 3):
            if r == CORNER_X:
                landed(self.block(r, 1 - self.x, self.mine), self.sems, self.base + 3 + r, self.xpeer)
            else:
                landed(self.block(r, self.x, self.other), self.sems, self.base + 6 + r, self.ypeer)
            landed(self.block(r, 1 - self.x, self.other), self.sems, self.base + 9 + r, self.ypeer)
        self.local.wait()

    def finish(self):
        for copy in self.sent:
            copy.wait_send()
        for copy in self.sent_inner:
            pl.when(self.inner)(lambda copy=copy: copy().wait_send())


def gather_steps(gathers):
    def one(g):
        return [
            lambda: g.forward(1),
            g.cross,
            lambda: g.forward(2),
            lambda: g.forward(3),
        ]

    def corners(g):
        return [lambda r=r: g.corner(r) for r in (2, 3, 1)]

    steps = []
    count = len(gathers)
    for k in range(count + 1):
        if k + 2 < count:
            steps.append(gathers[k + 2].start)
        steps += one(gathers[k]) if k < count else []
        steps += corners(gathers[k - 1]) + [k - 1] if k else []
    return steps


def reduce_steps(sums, partner):
    def early(s):
        return [
            s.cross,
            lambda: s.relay(2),
            lambda: s.root(1),
            lambda: s.relay(3),
            lambda: s.relay(0),
        ]

    def late(s):
        return [lambda r=r: s.root(r) for r in (2, 3, 0)]

    steps = []
    count = len(sums)
    for k in range(count + 3):
        if k < count:
            steps += early(sums[k])
        if 0 <= k - 1 < count:
            steps += late(sums[k - 1])
        if 0 <= k - 2 < count:
            steps.append(lambda s=sums[k - 2]: s.total(partner))
        if 0 <= k - 3 < count:
            steps.append(lambda s=sums[k - 3]: s.spread(partner))
    return steps


def chip_peers():
    z, x, y, c = place()
    peers = [device(z ^ r, x, y, c) for r in (1, 2, 3)]
    peers += [device(z, 1 - x, y, c), device(z, x, 1 - y, c), device(z, x, y, 1 - c)]
    return peers


def start_kernel(dealt, in_proj, beside, rows, weights, w, kv, dsend, drecv, wsend, wrecv, local):
    z, x, y, c = place()
    own = 2 * z + x
    slot = 2 * y + c
    partner = device(z, x, y, 1 - c)
    others = [(r, i, j) for r in range(4) for i in range(2) for j in range(2) if r or i or j]
    targets = [device(z ^ r, x ^ i, y ^ j, c) for r, i, j in others]
    lane = lambda start, size: pl.ds(pl.multiple_of(start, 128), size)
    inner = MH * HP
    q_start = 2 * inner + 2 * NS
    kv_start = q_start + QUERY_HEADS * HEAD_WIDTH
    pieces = [
        (lane(XW * c, XW), w.at[:, Z0 : Z0 + XW]),
        (lane(inner + XW * c, XW), w.at[:, X0 : X0 + XW]),
        (lane(q_start + QW * c, QW), w.at[:, Q0 : Q0 + QW]),
        (lane(2 * inner, 2 * NS), w.at[:, B0 : B0 + 2 * NS]),
        (lane(kv_start, 256), kv),
    ]
    copies = [pltpu.make_async_copy(in_proj.at[:, cols], dst, local.at[2 + i]) for i, (cols, dst) in enumerate(pieces)]
    for copy in copies:
        copy.start()
    barrier = pltpu.get_barrier_semaphore()
    for peer in targets + [partner]:
        pl.semaphore_signal(barrier, inc=1, device_id=peer, device_id_type=MESH)
    first = c == 0
    lane_of = lanes(w.shape[0])
    near = beside[...].astype(F32).T
    far = pltpu.roll(near, 128 - CHIP_HEADS, 1)
    tail = jnp.where(lane_of < CHIP_HEADS, jnp.where(first, near, far), jnp.where(lane_of < CHIP_HEADS + 2, far, 0.0))
    w[:, T0 : T0 + 128] = tail.astype(BF)
    for copy in copies:
        copy.wait()
    keys, values = kv[:, :128].astype(F32), kv[:, 128:].astype(F32)
    keys = jnp.where(first, keys, pltpu.roll(keys, 64, 1))
    values = jnp.where(first, pltpu.roll(values, 64, 1), values)
    w[:, KV0 : KV0 + 128] = jnp.where(lane_of < 64, keys, values).astype(BF)
    pl.semaphore_wait(barrier, len(targets) + 1)
    sems = (dsend, drecv)
    cuts = [slice(i * COLS // W_CUTS, (i + 1) * COLS // W_CUTS) for i in range(W_CUTS)]
    gathers = [
        Gather(w.at[:, cols], weights.at[:, :, cols], (wsend, wrecv), ARRAY_SENDS * i, local.at[7 + i])
        for i, cols in enumerate(cuts)
    ]
    columns = lambda d: lane(d * 128, 128)
    sent = []
    for gather in gathers[:2]:
        gather.start()
    for k, (r, i, j) in enumerate(others):
        pack = 2 * (2 * (z ^ r) + (x ^ i)) + (y ^ j)
        sent.append(send(dealt.at[pack], rows.at[slot, :, columns(own)], sems, k, targets[k]))
    here = pltpu.make_async_copy(dealt.at[2 * own + y], rows.at[slot, :, columns(own)], local.at[1])
    here.start()
    for step in gather_steps(gathers):
        if not isinstance(step, int):
            step()
    here.wait()
    for same_y in (True, False):
        for k, (r, i, j) in enumerate(others):
            if (j == 0) == same_y:
                src = 2 * (z ^ r) + (x ^ i)
                landed(rows.at[2 * (y ^ j) + c, :, columns(src)], sems, k, targets[k])
        ref = rows.at[slot if same_y else 2 * (1 - y) + c]
        sent.append(send(ref, ref, sems, 15 if same_y else 16, partner))
    landed(rows.at[2 * y + 1 - c], sems, 15, partner)
    landed(rows.at[2 * (1 - y) + 1 - c], sems, 16, partner)
    for gather in gathers:
        gather.arrive()
    for copy in sent:
        copy.wait_send()
    for gather in gathers:
        gather.finish()


def start_transfers(dealt, in_proj, beside):
    packs, span, width = dealt.shape
    block = in_proj.shape[0]
    return pl.pallas_call(
        start_kernel,
        name="deal_and_gather",
        out_shape=(
            jax.ShapeDtypeStruct((4, span, 8 * width), BF),
            jax.ShapeDtypeStruct((8, block, COLS), BF),
        ),
        in_specs=whole(1) + any_specs(1) + whole(1),
        out_specs=tuple(any_specs(2)),
        scratch_shapes=[
            VM((block, COLS), BF),
            VM((block, 256), BF),
            pltpu.SemaphoreType.DMA((17,)),
            pltpu.SemaphoreType.DMA((17,)),
            pltpu.SemaphoreType.DMA((W_CUTS * ARRAY_SENDS,)),
            pltpu.SemaphoreType.DMA((W_CUTS * ARRAY_SENDS,)),
            pltpu.SemaphoreType.DMA((7 + W_CUTS,)),
        ],
        compiler_params=pltpu.CompilerParams(collective_id=0, has_side_effects=True),
    )(dealt, in_proj, beside)


def any_specs(n):
    return [pl.BlockSpec(memory_space=pl.ANY)] * n


class Cotangents:
    def __init__(self, src, dst, sems, local_sem):
        self.src, self.dst, self.sems, self.local_sem = src, dst, sems, local_sem
        self.z, self.x, self.y, self.c = place()
        self.slot = 2 * self.y + self.c
        self.partner = device(self.z, self.x, self.y, 1 - self.c)
        self.ypeer = device(self.z, self.x, 1 - self.y, self.c)

    def start(self):
        src, dst = self.src, self.dst
        self.sent = [
            send(src.at[1 - self.y], dst.at[self.slot], self.sems, 0, self.ypeer),
            send(src.at[self.y], dst.at[self.slot], self.sems, 1, self.partner),
        ]
        self.local = pltpu.make_async_copy(src.at[self.y], dst.at[self.slot], self.local_sem)
        self.local.start()

    def forward(self):
        ref = self.dst.at[2 * (1 - self.y) + self.c]
        landed(ref, self.sems, 0, self.ypeer)
        self.sent.append(send(ref, ref, self.sems, 2, self.partner))

    def arrive(self):
        landed(self.dst.at[2 * self.y + 1 - self.c], self.sems, 1, self.partner)
        landed(self.dst.at[2 * (1 - self.y) + 1 - self.c], self.sems, 2, self.partner)
        self.local.wait()

    def finish(self):
        for copy in self.sent:
            copy.wait_send()


class Halves:
    def __init__(self, gather, dst, sems, base, local_sem):
        self.gather, self.dst, self.sems, self.base, self.local_sem = gather, dst, sems, base, local_sem
        z, x, y, self.c = place()
        self.partner = device(z, x, y, 1 - self.c)

    def columns(self, k):
        half = self.gather.src.shape[1]
        return self.dst.at[:, :, pl.ds(pl.multiple_of(k * half, 128), half)]

    def start(self):
        src, c = self.gather.dst, self.c
        self.gather.arrive()
        self.local = pltpu.make_async_copy(src.at[pl.ds(4 * c, 4)], self.columns(c), self.local_sem)
        self.local.start()
        self.sent = send(src.at[pl.ds(4 * (1 - c), 4)], self.columns(c), self.sems, self.base, self.partner)

    def arrive(self):
        landed(self.columns(1 - self.c), self.sems, self.base, self.partner)
        self.local.wait()
        self.sent.wait_send()


def plain_forward_kernel(proj, cosine, sine, segc, segr, par, spread, wide, gated, attn, lse, y_own, states, state):
    tick = Ticker([])
    attention_forward(proj, cosine, sine, segc, segr, attn, lse, tick)
    scan_forward(proj, segc, segr, par, spread, wide, gated, y_own, states, state, tick)


def mixer_forward(proj, consts):
    seq_len = proj.shape[0]
    return pl.pallas_call(
        plain_forward_kernel,
        name="mixer_forward",
        out_shape=(
            jax.ShapeDtypeStruct((seq_len, XW), BF),
            jax.ShapeDtypeStruct((seq_len, QW), BF),
            jax.ShapeDtypeStruct((seq_len, 128), F32),
            jax.ShapeDtypeStruct((seq_len, XW), F32),
            jax.ShapeDtypeStruct((seq_len // CHUNK, NS, XW), F32),
        ),
        in_specs=whole(8),
        out_specs=tuple(whole(5)),
        scratch_shapes=[VM((NS, XW), F32)],
        compiler_params=pltpu.CompilerParams(vmem_limit_bytes=56 * MIB),
    )(proj, *consts)


class Reduce:
    def __init__(self, part, out, far, near_x, near_y, deep, sems, base):
        self.part, self.out, self.far, self.near_x, self.near_y, self.deep = part, out, far, near_x, near_y, deep
        self.sems, self.base = sems, base
        self.z, self.x, self.y, self.c = place()
        half = part.shape[1] // 2
        self.mine = pl.ds(self.y * half, half)
        self.other = pl.ds((1 - self.y) * half, half)
        self.xpeer = device(self.z, 1 - self.x, self.y, self.c)
        self.ypeer = device(self.z, self.x, 1 - self.y, self.c)
        self.sent = []

    def piece(self, r, x, rows):
        return self.part.at[2 * (self.z ^ r) + x, rows]

    def push(self, k, src, dst, target):
        self.sent.append(send(src, dst, self.sems, self.base + k, target))

    def start(self):
        zpeer = device(self.z ^ 1, self.x, self.y, self.c)
        self.push(5, self.piece(1, 1 - self.x, self.mine), self.near_x.at[1], zpeer)
        self.push(1, self.piece(1, 1 - self.x, self.other), self.far.at[1], zpeer)
        for r in (2, 3):
            far = self.piece(r, 1 - self.x, self.other)
            self.push(r, far, self.far.at[r], self.ypeer if r == 2 else self.xpeer)
        self.push(9, self.piece(1, self.x, self.other), self.near_y.at[1], self.ypeer)

    def add(self, ref, r, own):
        ref[r] = (own[...].astype(F32) + ref[r].astype(F32)).astype(BF)

    def cross(self):
        landed(self.far.at[1], self.sems, self.base + 1, self.xpeer)
        self.add(self.far, 1, self.piece(0, 1 - self.x, self.other))
        self.push(0, self.far.at[1], self.far.at[0], self.xpeer)
        landed(self.near_x.at[1], self.sems, self.base + 5, self.xpeer)
        self.add(self.near_x, 1, self.piece(0, 1 - self.x, self.mine))
        self.push(4, self.near_x.at[1], self.near_x.at[0], self.xpeer)

    def relay(self, r):
        landed(self.far.at[r], self.sems, self.base + r, self.xpeer)
        if r == 2:
            self.add(self.far, r, self.piece(r, 1 - self.x, self.mine))
            self.push(4 + r, self.far.at[r], self.near_x.at[r], self.xpeer)
            self.push(8 + r, self.piece(r, self.x, self.other), self.near_y.at[r], self.ypeer)
            return
        self.add(self.far, r, self.piece(r, self.x, self.other))
        self.push(8 + r, self.far.at[r], self.near_y.at[r], self.ypeer)
        if r:
            self.push(4 + r, self.piece(r, 1 - self.x, self.mine), self.near_x.at[r], self.xpeer)

    def root(self, r):
        landed(self.near_y.at[r], self.sems, self.base + 8 + r, self.ypeer)
        total = self.piece(r, self.x, self.mine)[...].astype(F32) + self.near_y[r].astype(F32)
        if r != 1:
            landed(self.near_x.at[r], self.sems, self.base + 4 + r, self.xpeer)
            total = total + self.near_x[r].astype(F32)
        self.near_y[r] = total.astype(BF)
        if r:
            target = device(self.z ^ r, self.x, self.y, self.c)
            self.push(11 + r, self.near_y.at[r], self.deep.at[r - 1], target)

    def total(self, partner):
        for r in (1, 2, 3):
            landed(self.deep.at[r - 1], self.sems, self.base + 11 + r, self.xpeer)
        total = self.near_y[0].astype(F32) + self.deep[0].astype(F32)
        total = total + (self.deep[1].astype(F32) + self.deep[2].astype(F32))
        self.out[self.c, self.mine] = total.astype(BF)
        ref = self.out.at[self.c, self.mine]
        self.push(15, ref, ref, self.ypeer)
        self.push(16, ref, ref, partner)

    def spread(self, partner):
        ref = self.out.at[self.c, self.other]
        landed(ref, self.sems, self.base + 15, self.ypeer)
        self.push(17, ref, ref, partner)

    def finish(self, partner):
        landed(self.out.at[1 - self.c, self.mine], self.sems, self.base + 16, partner)
        landed(self.out.at[1 - self.c, self.other], self.sems, self.base + 17, partner)
        for copy in self.sent:
            copy.wait_send()


REDUCE_SENDS = 18


def reduce_buffers(parts):
    scratch = []
    for p in parts:
        half = (p.shape[1] // 2, p.shape[2])
        scratch += [VM((4,) + half, BF)] * 3 + [VM((3,) + half, BF)]
    total = REDUCE_SENDS * len(parts)
    return scratch + [pltpu.SemaphoreType.DMA((total,))] * 2


def plain_backward_kernel(proj, cosine, sine, segc, segr, par, spread, wide, attn, lse, y_own, states, ggated, gattn, gproj, gpar, gkv, gstate, gy):
    tick = Ticker([])
    gate_backward(proj, wide, y_own, ggated, gproj, gy, tick)
    attention_backward(proj, cosine, sine, segc, segr, attn, lse, gattn, gproj, gkv, tick)
    scan_backward(proj, segc, segr, par, spread, wide, y_own, states, gy, gproj, gpar, gstate, tick)


def mixer_backward(proj, consts, saved, ggated, gattn):
    seq_len = proj.shape[0]
    return pl.pallas_call(
        plain_backward_kernel,
        name="mixer_backward",
        out_shape=(
            jax.ShapeDtypeStruct((seq_len, COLS), BF),
            jax.ShapeDtypeStruct((8, 128), F32),
        ),
        in_specs=whole(14),
        out_specs=tuple(whole(2)),
        scratch_shapes=[VM((seq_len, 256), F32), VM((NS, XW), F32), VM((seq_len, XW), BF)],
        compiler_params=pltpu.CompilerParams(vmem_limit_bytes=56 * MIB),
    )(proj, *consts, *saved, ggated, gattn)


class Mover:
    def __init__(self, sems):
        self.sems, self.used, self.loads, self.stores = sems, 0, {}, []

    def copy(self, src, dst):
        copy = pltpu.make_async_copy(src, dst, self.sems.at[self.used])
        self.used += 1
        copy.start()
        return copy

    def load(self, src, dst):
        self.loads.setdefault(id(dst), []).append(self.copy(src, dst))

    def need(self, *refs):
        for ref in refs:
            for copy in self.loads.pop(id(ref), []):
                copy.wait()

    def store(self, src, dst):
        copy = self.copy(src, dst)
        self.stores.append(copy)
        return copy

    def flush(self):
        for copies in self.loads.values():
            for copy in copies:
                copy.wait()
        for copy in self.stores:
            copy.wait()


def shape(dims, dtype=BF):
    return jax.ShapeDtypeStruct(tuple(dims), dtype)


def fused_call(kernel, name, inputs, outputs, scratch, spaces, collective_id):
    names = list(inputs) + list(outputs) + list(scratch)

    def wrapped(*refs):
        kernel(types.SimpleNamespace(**dict(zip(names, refs))))

    place_of = lambda n: pl.BlockSpec(memory_space=spaces.get(n, pl.ANY))
    outs = pl.pallas_call(
        wrapped,
        name=name,
        out_shape=tuple(outputs.values()),
        in_specs=[place_of(n) for n in inputs],
        out_specs=tuple(place_of(n) for n in outputs),
        scratch_shapes=list(scratch.values()),
        compiler_params=pltpu.CompilerParams(
            collective_id=collective_id, has_side_effects=True, vmem_limit_bytes=62 * MIB
        ),
    )(*inputs.values())
    return types.SimpleNamespace(**dict(zip(outputs, outs)))


def dma(n):
    return pltpu.SemaphoreType.DMA((n,))


def row_blocks(seq_len, size=256):
    return [slice(i, i + size) for i in range(0, seq_len, size)]


def mixer_constants(k, own, y, c):
    seq_len = k.segc_v.shape[0]
    pack = k.deal[2 * own + y]
    ends = [k.lengths[0, pack]]
    for i in (1, 2):
        ends.append(ends[-1] + k.lengths[i, pack])
    for ref, dims, axis in ((k.segc_v, (seq_len, 128), 0), (k.segr_v, (8, seq_len), 1)):
        place_of = lax.broadcasted_iota(jnp.int32, dims, axis)
        ref[...] = sum((place_of >= end).astype(jnp.int32) for end in ends)
    heads = k.heads[...]
    heads = jnp.where(c == 0, heads, pltpu.roll(heads, 128 - CHIP_HEADS, 1))
    heads = jnp.where(lanes(8) < CHIP_HEADS, heads, 0.0)
    k.par_v[0:1, :] = heads[0:1, :]
    k.par_v[1:2, :] = jnp.where(lanes(1) < CHIP_HEADS, -jnp.exp(heads[1:2, :]), 0.0)
    k.wide_v[...] = dot(jnp.broadcast_to(heads[2:3, :], (8, 128)), k.spread_v[...].astype(F32), precision=lax.Precision.HIGHEST)


def forward_fused(k):
    z, x, y, c = place()
    own = 2 * z + x
    partner = device(z, x, y, 1 - c)
    mover = Mover(k.local)
    lane = lambda start, size: pl.ds(pl.multiple_of(start, 128), size)
    half = k.dn.shape[0] // 2
    for side in range(2):
        for d in range(8):
            mover.load(k.gu.at[:, lane(side * FF + (2 * d + c) * half, half)], k.gu_s.at[:, side * FF // 2 + d * half : side * FF // 2 + (d + 1) * half])
    shard_loads, mover.loads = mover.loads, {}
    for src, dst in ((k.rows, k.rows_v), (k.w_in, k.w_in_v), (k.spread, k.spread_v), (k.cosine, k.cosine_v), (k.sine, k.sine_v)):
        mover.load(src, dst)
    greet(chip_peers())
    columns = lane(k.part_v.shape[1] // 2 * c, k.part_v.shape[1] // 2)
    pairs = (
        (k.ssm.at[:, columns], k.ssm_all),
        (k.att.at[:, columns], k.att_all),
        (k.gu_s, k.gu_w),
        (k.dn.at[pl.ds(half * c, half)], k.dn_w),
    )
    gathers = [Gather(a, b, (k.gsend, k.grecv), ARRAY_SENDS * i, k.own.at[i]) for i, (a, b) in enumerate(pairs)]
    cots = Cotangents(k.cot, k.cots_v, (k.csend, k.crecv), k.own.at[4])
    halves = [Halves(g, out, (k.csend, k.crecv), 3 + i, k.own.at[5 + i]) for i, (g, out) in enumerate(zip(gathers, (k.ssm_v, k.att_v)))]
    gathers[0].start()
    gathers[1].start()
    cots.start()
    for copies in shard_loads.values():
        for copy in copies:
            copy.wait()
    steps = gather_steps(gathers)
    at = steps.index(1) + 6
    steps[at:at] = [h.start for h in halves] + [9]
    steps.insert(steps.index(3) - 2, cots.forward)
    tick = Ticker(steps, 60)

    blocks = row_blocks(k.rows_v.shape[0])
    mover.need(k.rows_v, k.w_in_v)
    tile = k.w_in_v[:, T0 : T0 + 128].astype(F32).T
    k.gains_v[0:1, :] = tile[CHIP_HEADS : CHIP_HEADS + 1, :]
    k.gains_v[1:2, :] = tile[CHIP_HEADS + 1 : CHIP_HEADS + 2, :]
    mover.store(k.gains_v, k.gains)
    for rows in blocks:
        xs = k.rows_v[rows, :].astype(F32)
        unit, _ = rms_parts(xs)
        normed = (unit * k.gains_v[0:1, :]).astype(BF)
        k.normed_v[rows, :] = normed
        for n in range(0, COLS, 768):
            k.proj_v[rows, n : n + 768] = dot(normed, k.w_in_v[:, n : n + 768]).astype(BF)
            tick()
    mover.store(k.proj_v, k.proj)
    kept_normed = mover.store(k.normed_v, k.normed)
    mover.need(k.spread_v, k.cosine_v, k.sine_v)
    mixer_constants(k, own, y, c)
    for src, dst in ((k.segc_v, k.segc), (k.segr_v, k.segr), (k.par_v, k.par), (k.wide_v, k.wide)):
        mover.store(src, dst)
    attention_forward(k.proj_v, k.cosine_v, k.sine_v, k.segc_v, k.segr_v, k.attn_v, k.lse_v, tick)
    mover.store(k.attn_v, k.attn)
    mover.store(k.lse_v, k.lse)
    scan_forward(k.proj_v, k.segc_v, k.segr_v, k.par_v, k.spread_v, k.wide_v, k.gated_v, k.y_v, k.states_v, k.state, tick)
    mover.store(k.gated_v, k.gated)
    mover.store(k.y_v, k.y)
    mover.store(k.states_v, k.states)

    tick.reach(9)
    for h in halves:
        h.arrive()
    mover.store(k.ssm_v, k.w_ssm)
    mover.store(k.att_v, k.w_att)
    sent = []
    for i, rows in enumerate(blocks):
        part = dot(k.gated_v[rows, :], k.ssm_v[...].reshape(XW, -1))
        part = part + dot(k.attn_v[rows, :], k.att_v[...].reshape(QW, -1))
        k.part_v[rows, :] = part.astype(BF)
        sent.append(send(k.part_v.at[rows], k.got_v.at[rows], (k.psend, k.precv), i, partner))
        tick()
    kept_normed.wait()
    mover.stores = [v for v in mover.stores if v is not kept_normed]
    for i, rows in enumerate(blocks):
        landed(k.got_v.at[rows], (k.psend, k.precv), i, partner)
        middle = k.rows_v[rows, :].astype(F32) + (k.part_v[rows, :].astype(F32) + k.got_v[rows, :].astype(F32))
        k.middle_v[rows, :] = middle
        unit, _ = rms_parts(middle)
        k.normed_v[rows, :] = (unit * k.gains_v[1:2, :]).astype(BF)
        tick()
    mover.store(k.middle_v, k.middle)
    mover.store(k.normed_v, k.h2)

    tick.reach(2)
    gathers[2].arrive()
    mover.store(k.gu_w, k.w_gu)
    for rows in blocks:
        for n in range(0, FF // 2, 512):
            for side in (0, FF // 2):
                cols = slice(side + n, side + n + 512)
                w = k.gu_w[:, :, cols].reshape(-1, 512)
                k.w_in_v[rows, cols] = dot(k.normed_v[rows, :], w).astype(BF)
            gate = k.w_in_v[rows, n : n + 512].astype(F32)
            up = k.w_in_v[rows, FF // 2 + n : FF // 2 + n + 512].astype(F32)
            k.act_v[rows, n : n + 512] = (silu(gate) * up).astype(BF)
            tick()
    mover.store(k.w_in_v.at[:, 0:FF], k.hidden)
    mover.store(k.act_v, k.act)
    tick.drain()
    cots.arrive()
    mover.store(k.cots_v, k.cots)
    width = k.rows_v.shape[1]
    for m in range(0, FF // 2, 256):
        k.gdn_v[m : m + 256, :] = dot(k.act_v[:, m : m + 256], k.cots_v[...].reshape(-1, width), ((0,), (0,))).astype(BF)
    mover.store(k.gdn_v, k.g_dn)
    gathers[3].arrive()
    mover.store(k.dn_w, k.w_dn)
    for g in gathers:
        g.finish()
    cots.finish()
    for copy in sent:
        copy.wait_send()
    mover.flush()


def forward_stage(rows, w_in, tables, heads, deal, lengths, cot, shards):
    seq_len, width = rows.shape
    ssm, att, gu, dn = shards
    cosine, sine, spread = tables
    chunks = seq_len // CHUNK
    total = 4 * ARRAY_SENDS
    half = dn.shape[0] // 2
    inputs = dict(
        rows=rows, w_in=w_in, cosine=cosine, sine=sine, spread=spread, heads=heads, deal=deal, lengths=lengths, cot=cot, ssm=ssm, att=att, gu=gu, dn=dn
    )
    spaces = dict(heads=VM, deal=pltpu.SMEM, lengths=pltpu.SMEM)
    square = shape((seq_len, width))
    outputs = dict(
        proj=shape((seq_len, COLS)),
        normed=square,
        gains=shape((8, width), F32),
        attn=shape((seq_len, QW)),
        lse=shape((seq_len, 128), F32),
        gated=shape((seq_len, XW)),
        y=shape((seq_len, XW), F32),
        states=shape((chunks, NS, XW), F32),
        w_ssm=shape((4, ssm.shape[0], width)),
        w_att=shape((4, att.shape[0], width)),
        w_gu=shape((8, gu.shape[0], FF)),
        w_dn=shape((8, half, width)),
        middle=shape((seq_len, width), F32),
        h2=square,
        hidden=shape((seq_len, FF)),
        act=shape((seq_len, FF // 2)),
        cots=shape((4,) + cot.shape[1:]),
        g_dn=shape((FF // 2, width)),
        segc=shape((seq_len, 128), jnp.int32),
        segr=shape((8, seq_len), jnp.int32),
        par=shape((8, 128), F32),
        wide=shape((8, XW), F32),
    )
    out = types.SimpleNamespace(**outputs)
    buffer = lambda v: VM(v.shape, v.dtype)
    scratch = dict(
        rows_v=buffer(rows),
        w_in_v=buffer(w_in),
        cosine_v=buffer(cosine),
        sine_v=buffer(sine),
        spread_v=buffer(spread),
        segc_v=buffer(out.segc),
        segr_v=buffer(out.segr),
        par_v=buffer(out.par),
        wide_v=buffer(out.wide),
        proj_v=buffer(out.proj),
        normed_v=buffer(square),
        gains_v=buffer(out.gains),
        attn_v=buffer(out.attn),
        lse_v=buffer(out.lse),
        gated_v=buffer(out.gated),
        y_v=buffer(out.y),
        states_v=buffer(out.states),
        middle_v=buffer(out.middle),
        act_v=buffer(out.act),
        cots_v=buffer(out.cots),
        ssm_v=buffer(out.w_ssm),
        att_v=buffer(out.w_att),
        gu_w=buffer(out.w_gu),
        dn_w=buffer(out.w_dn),
        gu_s=VM((gu.shape[0], FF), BF),
        ssm_all=VM((8, ssm.shape[0], width // 2), BF),
        att_all=VM((8, att.shape[0], width // 2), BF),
        gdn_v=buffer(out.g_dn),
        part_v=buffer(square),
        got_v=buffer(square),
        state=VM((NS, XW), F32),
        gsend=dma(total),
        grecv=dma(total),
        csend=dma(5),
        crecv=dma(5),
        psend=dma(4),
        precv=dma(4),
        own=dma(7),
        local=dma(48),
    )
    return fused_call(forward_fused, "forward", inputs, outputs, scratch, spaces, 1)


def feed_forward_fused(k):
    z, x, y, c = place()
    partner = device(z, x, y, 1 - c)
    ypeer = device(z, x, 1 - y, c)
    mover = Mover(k.local)
    for src, dst in k.loads:
        mover.load(src, dst)
    greet(chip_peers())
    pairs = ((k.g_dn_v, k.red_dn), (k.gate_v, k.red_gate))
    sums = [Reduce(part, out, *k.bufs[4 * i : 4 * i + 4], (k.rsend, k.rrecv), REDUCE_SENDS * i) for i, (part, out) in enumerate(pairs)]
    mover.need(k.g_dn_v)
    sums[0].start()
    tick = Ticker(reduce_steps(sums, partner))
    seq_len, width = k.middle_v.shape
    span = seq_len // 4
    blocks = row_blocks(seq_len)
    half = FF // 2
    flat = lambda ref: ref[...].reshape(-1, ref.shape[-1])
    pair = (k.psend, k.precv)

    mover.need(k.cots_v, k.w_dn_v, k.hidden_v)
    for i, rows in enumerate(blocks):
        g_act = dot(k.cots_v[i], flat(k.w_dn_v), ((1,), (1,))).astype(BF).astype(F32)
        gate = k.hidden_v[rows, :half].astype(F32)
        up = k.hidden_v[rows, half:].astype(F32)
        sig = 1.0 / (1.0 + jnp.exp(-gate))
        k.hidden_v[rows, :half] = (g_act * up * (sig * (1.0 + gate * (1.0 - sig)))).astype(BF)
        k.hidden_v[rows, half:] = (g_act * (gate * sig)).astype(BF)
    mover.need(k.h2_v)
    tick.plan(2, 4)
    for d in range(0, 8, 2):
        grad = dot(k.h2_v[:, 128 * d : 128 * d + 256], k.hidden_v[:, :half], ((0,), (0,))).astype(BF)
        k.gate_v[d : d + 2] = grad.reshape(2, 128, half)
        tick()
    sums[1].start()
    tick.plan(13, 24)
    mover.need(k.w_gu_v)
    sent = []
    for i, rows in enumerate(blocks):
        part = dot(k.hidden_v[rows, :], flat(k.w_gu_v), ((1,), (1,)))
        k.part_v[rows, :] = part.astype(BF)
        sent.append(send(k.part_v.at[rows], k.got_v.at[rows], pair, i, partner))
        tick()
    mover.need(k.act_v)
    for j in range(2):
        rows = pl.ds(pl.multiple_of((2 * j + 1 - c) * span, span), span)
        k.opart_v[j] = dot(k.act_v[rows, :], flat(k.w_dn_v)).astype(BF)
        sent.append(send(k.opart_v.at[j], k.ogot_v.at[j], pair, 4 + j, partner))
        tick()
    for d in range(0, 8, 2):
        grad = dot(k.h2_v[:, 128 * d : 128 * d + 256], k.hidden_v[:, half:], ((0,), (0,))).astype(BF)
        k.up_v[d : d + 2] = grad.reshape(2, 128, half)
        tick()
    mover.store(k.up_v, k.g_up)

    mover.need(k.middle_v)
    for j in range(2):
        rows = pl.ds(pl.multiple_of((2 * j + c) * span, span), span)
        own = k.middle_v[rows, :] + dot(k.act_v[rows, :], flat(k.w_dn_v)).astype(BF).astype(F32)
        landed(k.ogot_v.at[j], pair, 4 + j, partner)
        k.out_v[j] = (own + k.ogot_v[j].astype(F32)).astype(BF)
        tick()
    sent.append(send(k.out_v.at[1 - y], k.output.at[y], pair, 14, ypeer))
    mover.store(k.out_v.at[y], k.output.at[y])

    mover.need(k.middle_v, k.gains_v, k.w_ssm_v, k.w_att_v)
    gain = k.gains_v[1:2, :]
    grad_gain = jnp.zeros((1, width), F32)
    for i, rows in enumerate(blocks):
        landed(k.got_v.at[rows], pair, i, partner)
        g_two = (k.part_v[rows, :].astype(F32) + k.got_v[rows, :].astype(F32)).astype(BF).astype(F32)
        unit, scale = rms_parts(k.middle_v[rows, :])
        grad_gain = grad_gain + jnp.sum(g_two * unit, axis=0, keepdims=True)
        g_mid = k.cots_v[i].astype(F32) + rms_back(unit, scale, gain, g_two)
        k.got_f32[rows, :] = g_mid
        branch = g_mid.astype(BF)
        k.branch_v[rows, :] = branch
        tick()
        k.ggated_v[rows, :] = dot(branch, flat(k.w_ssm_v), ((1,), (1,))).astype(BF)
        k.gattn_v[rows, :] = dot(branch, flat(k.w_att_v), ((1,), (1,))).astype(BF)
        tick()
    k.gffn_v[0:1, :] = 0.5 * grad_gain
    mover.store(k.gffn_v, k.gffn)
    mover.store(k.ggated_v, k.ggated)
    mover.store(k.gattn_v, k.gattn)
    for j in range(2):
        mover.store(k.got_f32.at[pl.ds(pl.multiple_of((2 * j + c) * span, span), span)], k.g_mid.at[j])

    mover.need(k.gated_v, k.attn_v)
    moves = []
    n = 6
    for source, rows, hold, out in ((k.gated_v, XW, k.gssm_v, k.g_ssm), (k.attn_v, QW, k.gatt_v, k.g_att)):
        for m in range(0, rows, 256):
            hold[m : m + 256, :] = dot(source[:, m : m + 256], k.branch_v[...], ((0,), (0,))).astype(BF)
            tick()
        own = rows // 4
        for d in range(4):
            columns = lambda e: hold.at[pl.ds(d * own, own), pl.ds(pl.multiple_of(e * (width // 2), 128), width // 2)]
            mover.store(columns(c), out.at[4 * c + d])
            moves.append((out.at[4 * (1 - c) + d], n))
            sent.append(send(columns(1 - c), out.at[4 * c + d], pair, n, partner))
            n += 1

    tick.drain()
    for s in sums:
        s.finish(partner)
    for ref, i in moves:
        landed(ref, pair, i, partner)
    landed(k.output.at[1 - y], pair, 14, ypeer)
    for copy in sent:
        copy.wait_send()
    mover.flush()


def reduce_scratch(shapes):
    bufs = []
    for dims in shapes:
        half = (dims[1] // 2, dims[2])
        bufs += [VM((4,) + half, BF)] * 3 + [VM((3,) + half, BF)]
    return {"b" + str(i): b for i, b in enumerate(bufs)}


def loaded(inputs, names=None):
    return {n + "_v": VM(v.shape, v.dtype) for n, v in inputs.items()}


def with_lists(kernel, inputs, bufs):
    def run(k):
        refs = vars(k)
        k.loads = [(refs[n], refs[n + "_v"]) for n in inputs if n + "_v" in refs]
        k.bufs = [refs[n] for n in bufs]
        kernel(k)

    return run


def feed_forward_stage(f):
    seq_len, width = f.middle.shape
    inputs = dict(
        g_dn=f.g_dn.reshape(8, -1, width),
        cots=f.cots,
        w_dn=f.w_dn,
        hidden=f.hidden,
        h2=f.h2,
        w_gu=f.w_gu,
        act=f.act,
        middle=f.middle,
        gains=f.gains,
        w_ssm=f.w_ssm,
        w_att=f.w_att,
        gated=f.gated,
        attn=f.attn,
    )
    span = seq_len // 4
    part = (8, width // 8, FF // 2)
    outputs = dict(
        output=shape((2, span, width)),
        red_dn=shape((2,) + inputs["g_dn"].shape[1:]),
        red_gate=shape((2,) + part[1:]),
        g_up=shape(part),
        g_ssm=shape((8, XW // 4, width // 2)),
        g_att=shape((8, QW // 4, width // 2)),
        ggated=shape((seq_len, XW)),
        gattn=shape((seq_len, QW)),
        g_mid=shape((2, span, width), F32),
        gffn=shape((8, width), F32),
    )
    bufs = reduce_scratch([inputs["g_dn"].shape, part])
    scratch = dict(
        **loaded(inputs),
        **bufs,
        gate_v=VM(part, BF),
        up_v=VM(part, BF),
        part_v=VM((seq_len, width), BF),
        got_v=VM((seq_len, width), BF),
        opart_v=VM((2, span, width), BF),
        ogot_v=VM((2, span, width), BF),
        out_v=VM((2, span, width), BF),
        got_f32=VM((seq_len, width), F32),
        branch_v=VM((seq_len, width), BF),
        ggated_v=VM((seq_len, XW), BF),
        gattn_v=VM((seq_len, QW), BF),
        gssm_v=VM((XW, width), BF),
        gatt_v=VM((QW, width), BF),
        gffn_v=VM((8, width), F32),
        rsend=dma(2 * REDUCE_SENDS),
        rrecv=dma(2 * REDUCE_SENDS),
        psend=dma(15),
        precv=dma(15),
        local=dma(32),
    )
    kernel = with_lists(feed_forward_fused, inputs, bufs)
    return fused_call(kernel, "feed_forward", inputs, outputs, scratch, dict(red_dn=VM, red_gate=VM), 2)


def backward_fused(k):
    z, x, y, c = place()
    own = 2 * z + x
    slot = 2 * own + y
    partner = device(z, x, y, 1 - c)
    others = [(r, i, j) for r in range(4) for i in range(2) for j in range(2) if r or i or j]
    targets = [device(z ^ r, x ^ i, y ^ j, c) for r, i, j in others]
    mover = Mover(k.local)
    for src, dst in k.loads:
        mover.load(src, dst)
    greet(targets + [partner])
    pairs = (
        (k.up_v, k.red_up),
        (k.ssm_v, k.red_ssm),
        (k.att_v, k.red_att),
        (k.gz_v, k.red_gz),
        (k.xbc_v, k.red_xbc),
        (k.qkv_v, k.red_qkv),
        (k.steps_v, k.red_steps),
    )
    sums = [Reduce(part, out, *k.bufs[4 * i : 4 * i + 4], (k.rsend, k.rrecv), REDUCE_SENDS * i) for i, (part, out) in enumerate(pairs)]
    mover.need(k.up_v)
    sums[0].start()
    mover.need(k.ssm_v, k.att_v)
    for step in sums[1:3]:
        step.start()
    tick = Ticker(reduce_steps(sums, partner))
    tick.plan(2, 8)
    seq_len, width = k.normed_v.shape
    span = seq_len // 4

    def grad_of(lo, hi, out, at):
        for d in range(0, 8, 2):
            grad = dot(k.normed_v[:, 128 * d : 128 * d + 256], k.gproj_v[:, lo:hi], ((0,), (0,))).astype(BF)
            out[d : d + 2, :, at : at + hi - lo] = grad.reshape(2, 128, hi - lo)
            tick()

    mover.need(k.proj_v, k.segc_v, k.segr_v, k.par_v, k.spread_v, k.wide_v, k.ggated_v, k.y_v)
    gate_backward(k.proj_v, k.wide_v, k.y_v, k.ggated_v, k.gproj_v, k.ggated_v, tick)
    mover.need(k.normed_v)
    grad_of(Z0, Z0 + XW, k.gz_v, 0)
    sums[3].start()
    mover.need(k.states_v)
    tick.plan(14, 24)
    scan_backward(k.proj_v, k.segc_v, k.segr_v, k.par_v, k.spread_v, k.wide_v, k.y_v, k.states_v, k.ggated_v, k.gproj_v, k.gpar_v, k.gstate, tick)
    grad_of(X0, X0 + XW, k.xbc_v, 0)
    grad_of(B0, T0, k.xbc_v, XW)
    sums[4].start()
    tick.plan(13, 20)
    mover.need(k.gattn_v, k.attn_v, k.lse_v, k.cosine_v, k.sine_v)
    attention_backward(k.proj_v, k.cosine_v, k.sine_v, k.segc_v, k.segr_v, k.attn_v, k.lse_v, k.gattn_v, k.gproj_v, k.gkv, tick)
    grad_of(Q0, B0, k.qkv_v, 0)
    sums[5].start()
    tick.plan(6, 4)
    pair = (k.psend, k.precv)
    mover.need(k.w_in_v, k.rows_v, k.g_mid_v, k.gains_v, k.gffn_v)
    sent = []
    for j in range(2):
        rows = pl.ds(pl.multiple_of((2 * j + 1 - c) * span, span), span)
        k.opart_v[j] = dot(k.gproj_v[rows, :], k.w_in_v[...], ((1,), (1,))).astype(BF)
        sent.append(send(k.opart_v.at[j], k.ogot_v.at[j], pair, j, partner))
        tick()
    gain = k.gains_v[0:1, :]
    grad_gain = jnp.zeros((1, width), F32)
    columns = lambda d: pl.ds(pl.multiple_of(d * 128, 128), 128)
    sems = (k.dsend, k.drecv)
    for j in range(2):
        rows = pl.ds(pl.multiple_of((2 * j + c) * span, span), span)
        part = dot(k.gproj_v[rows, :], k.w_in_v[...], ((1,), (1,))).astype(BF).astype(F32)
        landed(k.ogot_v.at[j], pair, j, partner)
        g_h1 = (part + k.ogot_v[j].astype(F32)).astype(BF).astype(F32)
        unit, scale = rms_parts(k.rows_v[rows, :].astype(F32))
        grad_gain = grad_gain + jnp.sum(g_h1 * unit, axis=0, keepdims=True)
        k.ogot_v[j] = (k.g_mid_v[j] + rms_back(unit, scale, gain, g_h1)).astype(BF)
        tick()
    mover.store(k.ogot_v.at[y, :, columns(own)], k.returned.at[slot])
    for i, (r, a, b) in enumerate(others):
        d = 2 * (z ^ r) + (x ^ a)
        sent.append(send(k.ogot_v.at[y ^ b, :, columns(d)], k.returned.at[slot], sems, i, targets[i]))
    valid = lanes(1) < CHIP_HEADS
    heads = [jnp.where(valid, k.gpar_v[p : p + 1, :], 0.0) for p in range(3)]
    lines = [grad_gain, k.gffn_v[0:1, :]] + [jnp.concatenate([h] * (width // 128), axis=1) for h in heads]
    extra = jnp.concatenate([jnp.zeros((CHIP_HEADS, width), F32)] + lines + [jnp.zeros((STEP_ROWS - CHIP_HEADS - 5, width), F32)], axis=0)
    grad = dot(k.gproj_v[:, T0:COLS], k.normed_v[...], ((0,), (0,)))[0:STEP_ROWS, :] + extra
    for d in range(8):
        k.steps_v[d] = grad[:, 128 * d : 128 * (d + 1)].astype(BF)
    sums[6].start()
    tick.drain()
    for s in sums:
        s.finish(partner)
    for i, (r, a, b) in enumerate(others):
        landed(k.returned.at[2 * (2 * (z ^ r) + (x ^ a)) + (y ^ b)], sems, i, targets[i])
    for copy in sent:
        copy.wait_send()
    mover.flush()


STEP_ROWS = 32


def backward_stage(f, m, rows, w_in, tables):
    seq_len, width = rows.shape
    span = seq_len // 4
    cosine, sine, spread = tables
    inputs = dict(
        up=m.g_up,
        ssm=m.g_ssm,
        att=m.g_att,
        proj=f.proj,
        segc=f.segc,
        segr=f.segr,
        par=f.par,
        spread=spread,
        wide=f.wide,
        ggated=m.ggated,
        y=f.y,
        normed=f.normed,
        states=f.states,
        gattn=m.gattn,
        attn=f.attn,
        lse=f.lse,
        cosine=cosine,
        sine=sine,
        w_in=w_in,
        rows=rows,
        g_mid=m.g_mid,
        gains=f.gains,
        gffn=m.gffn,
    )
    block = width // 8
    new = dict(
        gz_v=(8, block, XW), xbc_v=(8, block, XW + 256), qkv_v=(8, block, QW + 128), steps_v=(8, STEP_ROWS, block)
    )
    parts = [m.g_up.shape, m.g_ssm.shape, m.g_att.shape] + list(new.values())
    out = [shape((2,) + d[1:]) for d in parts]
    outputs = dict(
        red_up=out[0],
        red_ssm=out[1],
        red_att=out[2],
        red_gz=out[3],
        red_xbc=out[4],
        red_qkv=out[5],
        red_steps=out[6],
    )
    spaces = {n: VM for n in outputs}
    outputs.update(returned=shape((16, span, 128)))
    bufs = reduce_scratch(parts)
    scratch = dict(
        **loaded(inputs),
        **bufs,
        **{n: VM(d, BF) for n, d in new.items()},
        gproj_v=VM((seq_len, COLS), BF),
        gpar_v=VM((8, 128), F32),
        gkv=VM((seq_len, 256), F32),
        gstate=VM((NS, XW), F32),
        opart_v=VM((2, span, width), BF),
        ogot_v=VM((2, span, width), BF),
        rsend=dma(len(parts) * REDUCE_SENDS),
        rrecv=dma(len(parts) * REDUCE_SENDS),
        psend=dma(2),
        precv=dma(2),
        dsend=dma(15),
        drecv=dma(15),
        local=dma(28),
    )
    return fused_call(with_lists(backward_fused, inputs, bufs), "mixer_backward", inputs, outputs, scratch, spaces, 3)


def finish_kernel(deal, *refs):
    sources, (tokens, g_in, g_dt, g_ssm, g_att, g_gu, g_dn, small), refs = refs[:10], refs[10:18], refs[18:]
    held, (sems, load_sems) = refs[:10], refs[10:]
    up, gate, dn, ssm, att, gz, xbc, qkv, steps, returned = held
    loads = [pltpu.make_async_copy(src, dst, load_sems.at[i]) for i, (src, dst) in enumerate(zip(sources, held))]
    for copy in reversed(loads):
        copy.start()
    for copy in reversed(loads):
        copy.wait()
    copies = [pltpu.make_async_copy(returned.at[j], tokens.at[deal[j]], sems.at[j]) for j in range(16)]
    for copy in copies:
        copy.start()
    wide = lambda v: v.astype(F32)
    inner = MH * HP
    q_start = 2 * inner + 2 * NS
    kv_start = q_start + QUERY_HEADS * HEAD_WIDTH
    half = dn.shape[1]
    for c in range(2):
        g_in[:, XW * c : XW * (c + 1)] = wide(gz[c])
        g_in[:, inner + XW * c : inner + XW * (c + 1)] = wide(xbc[c, :, 0:XW])
        g_in[:, q_start + QW * c : q_start + QW * (c + 1)] = wide(qkv[c, :, 0:QW])
        g_ssm[:, ssm.shape[2] * c : ssm.shape[2] * (c + 1)] = wide(ssm[c])
        g_att[:, att.shape[2] * c : att.shape[2] * (c + 1)] = wide(att[c])
        g_dn[half * c : half * (c + 1), :] = wide(dn[c])
        for d in range(8):
            at = (2 * d + c) * half
            g_gu[:, at : at + half] = wide(gate[c, :, half * d : half * (d + 1)])
            g_gu[:, FF + at : FF + at + half] = wide(up[c, :, half * d : half * (d + 1)])
    g_in[:, 2 * inner : q_start] = wide(xbc[0, :, XW:]) + wide(xbc[1, :, XW:])
    kv = [wide(qkv[c, :, QW : QW + 128]) for c in range(2)]
    low_lanes = lanes(kv[0].shape[0]) < 64
    g_in[:, kv_start : kv_start + 128] = jnp.where(low_lanes, kv[0], pltpu.roll(kv[1], 64, 1))
    g_in[:, kv_start + 128 : kv_start + 256] = jnp.where(low_lanes, pltpu.roll(kv[0], 64, 1), kv[1])
    first, second = wide(steps[0]), wide(steps[1])
    line = lax.broadcasted_iota(jnp.int32, first.shape, 0)
    heads = jnp.where(line < CHIP_HEADS, first, pltpu.roll(second, CHIP_HEADS, 0))
    heads = jnp.concatenate([heads, jnp.zeros((128 - STEP_ROWS, 128), F32)], axis=0).T
    g_dt[...] = heads[:, 0:MH]
    small[...] = jnp.zeros_like(small)
    for i in range(2):
        row = CHIP_HEADS + i
        small[i : i + 1, :] = first[row : row + 1, :] + second[row : row + 1, :]
    for i in range(3):
        row = CHIP_HEADS + 2 + i
        moved = pltpu.roll(second[row : row + 1, :], CHIP_HEADS, 1)
        small[2 + i : 3 + i, :] = jnp.where(lanes(1) < CHIP_HEADS, first[row : row + 1, :], moved)
    for copy in copies:
        copy.wait()


def finish_stage(deal, m, b, ssm_out, attn_out, down_proj, in_proj):
    returned = b.returned
    sources = (b.red_up, m.red_gate, m.red_dn, b.red_ssm, b.red_att, b.red_gz, b.red_xbc, b.red_qkv, b.red_steps, returned)
    wide = lambda v: shape(v.shape, F32)
    block = in_proj.shape[0]
    return pl.pallas_call(
        finish_kernel,
        name="place_gradients",
        out_shape=(
            shape(returned.shape),
            wide(in_proj),
            shape((block, MH), F32),
            wide(ssm_out),
            wide(attn_out),
            shape((block, 2 * FF), F32),
            wide(down_proj),
            shape((8, 128), F32),
        ),
        in_specs=[pl.BlockSpec(memory_space=pltpu.SMEM)] + any_specs(10),
        out_specs=tuple(any_specs(1) + whole(7)),
        scratch_shapes=[VM(v.shape, v.dtype) for v in sources] + [dma(16), dma(10)],
        compiler_params=pltpu.CompilerParams(vmem_limit_bytes=62 * MIB),
    )(deal, *sources)


def mixer_tables(seq_len):
    half = HEAD_WIDTH // 2
    frequency = np.float32(THETA) ** (-np.arange(half, dtype=np.float32) * np.float32(2.0 / HEAD_WIDTH))
    angles = np.arange(seq_len, dtype=np.float32)[:, None] * frequency[None, :].astype(np.float32)
    cosine = np.tile(np.cos(angles), (1, 4)).astype(np.float32)
    sine = np.tile(np.concatenate([-np.sin(angles), np.sin(angles)], axis=1), (1, 2)).astype(np.float32)
    head_of = np.arange(XW) // HP
    spread = np.arange(128)[:, None] % 64 == head_of[None, :]
    return jnp.asarray(cosine), jnp.asarray(sine), jnp.asarray(spread, BF)


def fused_layer(dealt, cot, seq_lengths, deal_order, gains, in_proj, dt_proj, head_values, ssm_out, attn_out, gate_up, down_proj):
    block = in_proj.shape[0]
    width = cot.shape[2]
    seq_len = 4 * cot.shape[1]
    beside = jnp.concatenate([dt_proj.T] + [g[None] for g in gains] + [jnp.zeros((128 - MH - 2, block), BF)], axis=0)
    heads = jnp.pad(jnp.stack(head_values), ((0, 5), (0, 128 - MH)))
    tables = mixer_tables(seq_len)
    rows, w_in = start_transfers(dealt, in_proj, beside)
    rows, w_in = rows.reshape(seq_len, width), w_in.reshape(width, COLS)
    first = forward_stage(rows, w_in, tables, heads, deal_order, seq_lengths.T, cot, (ssm_out, attn_out, gate_up, down_proj))
    mid = feed_forward_stage(first)
    last = backward_stage(first, mid, rows, w_in, tables)
    tokens, g_in, g_dt, g_ssm, g_att, g_gu, g_dn, small = finish_stage(deal_order, mid, last, ssm_out, attn_out, down_proj, in_proj)
    heads = [small[2 + i, :MH] for i in range(3)]
    return (mid.output, tokens, small[0], g_in, g_dt, *heads, g_ssm, g_att, small[1], g_gu, g_dn)


def rms_parts(v):
    scale = lax.rsqrt(jnp.mean(v * v, axis=-1, keepdims=True) + EPS)
    return v * scale, scale


def rms_back(normed, scale, gain, grad):
    inner = grad * gain
    return scale * (inner - normed * jnp.mean(inner * normed, axis=-1, keepdims=True))


def silu(v):
    return v / (1.0 + jnp.exp(-v))


def low(v):
    return v.astype(BF)


def plain_start(dealt, cot, w, y):
    arrived = lax.all_to_all(dealt, "dp", split_axis=0, concat_axis=2, tiled=True)
    rows = lax.all_gather(arrived, "seq", axis=1, tiled=True)
    cots = lax.all_gather(cot, "seq", axis=1, tiled=True)
    pick = lambda v: lax.dynamic_index_in_dim(v, y, 0, keepdims=False)
    return pick(rows), lax.all_gather(w, "dp", axis=0, tiled=True), pick(cots)


def plain_gather(ssm, att, gu, dn, c):
    every = [lax.all_gather(v, "dp", axis=0, tiled=True) for v in (ssm, att, gu, dn)]
    out = []
    for v in every[:2]:
        rows = v.shape[0] // 2
        mine = lax.all_gather(v, "seq", axis=1, tiled=True)[:, : 2 * v.shape[1]]
        out.append(lax.dynamic_slice_in_dim(mine, c * rows, rows))
    return out + every[2:]


def plain_pair(part):
    return lax.ppermute(part, "seq", [(0, 1), (1, 0), (2, 3), (3, 2)])


def plain_reduce(parts, out_rows, gx, y, c):
    reduced = []
    for p in parts:
        total = lax.psum_scatter(p.reshape(-1, p.shape[-1]), "dp", scatter_dimension=0, tiled=True)
        every = lax.all_gather(total, "seq", axis=0).astype(F32)
        reduced.append(jnp.stack([every[0] + every[2], every[1] + every[3]]))
    peer = lax.ppermute(out_rows, "seq", [(0, 2), (1, 3), (2, 0), (3, 1)])
    output = jnp.where(jnp.arange(2)[:, None, None] == y, out_rows, jnp.flip(peer, 0))
    whole_rows = lax.all_gather(gx, "seq", axis=0)
    slot = 2 * y + c
    by_pack = lax.dynamic_index_in_dim(whole_rows, c, 0, False), lax.dynamic_index_in_dim(whole_rows, c + 2, 0, False)
    both = jnp.stack([lax.dynamic_index_in_dim(v, y, 0, False) for v in by_pack])
    returned = lax.all_to_all(both, "dp", split_axis=2, concat_axis=0, tiled=True)
    return reduced, output, returned


def plain_layer(dealt, cot, w_in, shards, consts, y, c):
    groups = lax.axis_size("dp")
    rows, w_in, cots = plain_start(dealt, cot, w_in, y)
    w_ssm, w_att, w_gu, w_dn = plain_gather(*shards, c)
    span, width = cot.shape[1:]
    block = width // groups
    cut = lambda v, start, size: lax.dynamic_slice_in_dim(v, start, size, axis=1)

    x = rows.astype(F32)
    gain_in = w_in[:, T0 + CHIP_HEADS].astype(F32)[None, :]
    gain_ffn = w_in[:, T0 + CHIP_HEADS + 1].astype(F32)[None, :]
    unit_in, scale_in = rms_parts(x)
    normed = low(unit_in * gain_in)
    proj = low(dot(normed, w_in))
    gated, *saved = mixer_forward(proj, consts)
    attn = saved[0]
    part = low(dot(gated, w_ssm) + dot(attn, w_att))
    middle = x + (part.astype(F32) + plain_pair(part).astype(F32))
    unit_ffn, scale_ffn = rms_parts(middle)
    normed_two = low(unit_ffn * gain_ffn)
    gu = low(dot(normed_two, w_gu)).astype(F32)
    gate, up = gu[:, : FF // 2], gu[:, FF // 2 :]
    act = low(silu(gate) * up)
    out_part = low(dot(act, w_dn))
    by_core = lambda v: lax.dynamic_index_in_dim(v.reshape(2, 2, span, width), c, 1, keepdims=False)
    out_rows = low(by_core(middle) + (by_core(out_part).astype(F32) + by_core(plain_pair(out_part)).astype(F32)))

    g_act = low(dot(cots, w_dn, ((1,), (1,)))).astype(F32)
    grad_dn = low(dot(act, cots, ((0,), (0,))))
    sig = 1.0 / (1.0 + jnp.exp(-gate))
    g_gu = low(jnp.concatenate([g_act * up * (sig * (1.0 + gate * (1.0 - sig))), g_act * (gate * sig)], axis=1))
    grad_gu = low(dot(normed_two, g_gu, ((0,), (0,))))
    part = low(dot(g_gu, w_gu, ((1,), (1,))))
    g_two = low(part.astype(F32) + plain_pair(part).astype(F32)).astype(F32)
    g_mid = cots.astype(F32) + rms_back(unit_ffn, scale_ffn, gain_ffn, g_two)
    grad_gain_ffn = 0.5 * jnp.sum(g_two * unit_ffn, axis=0)
    g_branch = low(g_mid)
    g_gated = low(dot(g_branch, w_ssm, ((1,), (1,))))
    g_attn = low(dot(g_branch, w_att, ((1,), (1,))))
    grad_ssm = low(dot(gated, g_branch, ((0,), (0,))))
    grad_att = low(dot(attn, g_branch, ((0,), (0,))))
    g_proj, g_par = mixer_backward(proj, consts, saved, g_gated, g_attn)
    grad_in = dot(normed, g_proj, ((0,), (0,)))
    part = low(dot(g_proj, w_in, ((1,), (1,))))
    g_h1 = low(by_core(part).astype(F32) + by_core(plain_pair(part)).astype(F32)).astype(F32)
    scale_rows = by_core(jnp.broadcast_to(scale_in, x.shape))
    g_x = low(by_core(g_mid) + rms_back(by_core(unit_in), scale_rows, gain_in, g_h1))
    grad_gain_in = jnp.sum(g_h1 * by_core(unit_in), axis=(0, 1))
    head_grads = jnp.tile(jnp.pad(g_par[:3, :CHIP_HEADS].T, ((0, block - CHIP_HEADS), (0, 0))), (groups, 1))
    extra = jnp.concatenate([grad_gain_in[:, None], grad_gain_ffn[:, None], head_grads], axis=1)
    grad_in = low(lax.dynamic_update_slice(grad_in, extra, (0, T0 + CHIP_HEADS)))

    by_block = lambda v: v.reshape(groups, -1, v.shape[-1])
    parts = [by_block(grad_in), by_block(grad_dn), by_block(grad_gu)]
    for v in (grad_ssm, grad_att):
        both = jnp.stack([v, plain_pair(v)])
        both = jnp.where(c == 0, both, both[::-1]).reshape(-1, width)
        parts.append(by_block(cut(both, width // 2 * c, width // 2)))
    reduced, output, returned = plain_reduce(parts, out_rows, g_x, y, c)
    return output, returned, reduced


def body(tokens, cot, seq_lengths, deal_order, in_gain, in_proj, dt_proj, dt_bias, a_log, d_skip, ssm_out, attn_out, ffn_gain, gate_up, down_proj):
    groups = lax.axis_size("dp")
    dealt = tokens.at[deal_order].get(mode="promise_in_bounds")
    if groups == 8:
        return fused_layer(
            dealt, cot, seq_lengths, deal_order, (in_gain, ffn_gain), in_proj, dt_proj, (dt_bias, a_log, d_skip), ssm_out, attn_out, gate_up, down_proj
        )
    dp_index, seq_index = lax.axis_index("dp"), lax.axis_index("seq")
    y, c = seq_index // 2, seq_index % 2
    packs, span, width = cot.shape
    seq_len = span * lax.axis_size("seq")
    inner = MH * HP
    block = in_proj.shape[0]

    cut = lambda v, start, size: lax.dynamic_slice_in_dim(v, start, size, axis=1)
    q_start = 2 * inner + 2 * NS
    k_start = q_start + QUERY_HEADS * HEAD_WIDTH
    v_start = k_start + KEY_VALUE_HEADS * HEAD_WIDTH
    w_in = jnp.concatenate(
        [
            cut(in_proj, XW * c, XW),
            cut(in_proj, inner + XW * c, XW),
            cut(in_proj, q_start + QW * c, QW),
            cut(in_proj, k_start + HEAD_WIDTH * c, HEAD_WIDTH),
            cut(in_proj, v_start + HEAD_WIDTH * c, HEAD_WIDTH),
            in_proj[:, 2 * inner : q_start],
            cut(dt_proj, CHIP_HEADS * c, CHIP_HEADS),
            in_gain[:, None],
            ffn_gain[:, None],
            jnp.zeros((block, 128 - CHIP_HEADS - 2), BF),
        ],
        axis=1,
    )
    half_units = down_proj.shape[0] // 2
    w_gu = gate_up.reshape(block, 2, groups, 2, half_units)
    w_gu = lax.dynamic_index_in_dim(w_gu, c, 3, keepdims=False).reshape(block, FF)
    w_dn = lax.dynamic_slice_in_dim(down_proj, half_units * c, half_units, axis=0)
    w_ssm = cut(ssm_out, width // 2 * c, width // 2)
    w_att = cut(attn_out, width // 2 * c, width // 2)

    pack = lax.dynamic_index_in_dim(deal_order, dp_index * packs + y, 0, keepdims=False)
    ends = jnp.cumsum(lax.dynamic_index_in_dim(seq_lengths, pack, 0, keepdims=False))[:-1]
    places = jnp.arange(seq_len, dtype=jnp.int32)
    seg = jnp.sum((places[:, None] >= ends[None, :]).astype(jnp.int32), axis=1)
    segc = jnp.broadcast_to(seg[:, None], (seq_len, 128))
    segr = jnp.broadcast_to(seg[None, :], (8, seq_len))
    half = HEAD_WIDTH // 2
    frequency = THETA ** (-jnp.arange(half, dtype=F32) * 2.0 / HEAD_WIDTH)
    angles = places.astype(F32)[:, None] * frequency[None, :]
    cosine = jnp.tile(jnp.cos(angles), (1, 4))
    sine = jnp.tile(jnp.concatenate([-jnp.sin(angles), jnp.sin(angles)], axis=1), (1, 2))
    own_heads = lambda v: lax.dynamic_slice_in_dim(v, CHIP_HEADS * c, CHIP_HEADS)
    par = jnp.zeros((8, 128), F32)
    par = par.at[0, :CHIP_HEADS].set(own_heads(dt_bias)).at[1, :CHIP_HEADS].set(-jnp.exp(own_heads(a_log)))
    wide = jnp.broadcast_to(jnp.repeat(own_heads(d_skip), HP)[None, :], (8, XW))
    head_of = jnp.arange(XW) // HP
    spread = (jnp.arange(128)[:, None] % 64 == head_of[None, :]).astype(BF)
    consts = (cosine, sine, segc, segr, par, spread, wide)

    shards = (w_ssm, w_att, w_gu, w_dn)
    output, returned, (r_in, r_dn, r_gu, r_ssm, r_att) = plain_layer(dealt, cot, w_in, shards, consts, y, c)

    both = lambda start, size: [r_in[0, :, start : start + size], r_in[1, :, start : start + size]]
    grad_in_proj = jnp.concatenate(
        both(Z0, XW)
        + both(X0, XW)
        + [r_in[0, :, B0:T0] + r_in[1, :, B0:T0]]
        + both(Q0, QW)
        + both(KV0, HEAD_WIDTH)
        + both(KV0 + HEAD_WIDTH, HEAD_WIDTH),
        axis=1,
    )
    grad_dt_proj = jnp.concatenate(both(T0, CHIP_HEADS), axis=1)
    tail = r_in[:, :, T0 + CHIP_HEADS : T0 + CHIP_HEADS + 5]
    gains = tail[0, :, :2] + tail[1, :, :2]
    heads = tail[:, :CHIP_HEADS, 2:5].reshape(MH, 3)
    grad_gate_up = jnp.stack(
        [r_gu[k].reshape(block, 2, groups, half_units) for k in range(2)], axis=3
    ).reshape(block, 2 * FF)
    side = lambda v: jnp.concatenate([v[0], v[1]], axis=1)
    return (
        output,
        jnp.take(returned, jnp.argsort(deal_order), axis=0),
        gains[:, 0],
        grad_in_proj,
        grad_dt_proj,
        heads[:, 0],
        heads[:, 1],
        heads[:, 2],
        side(r_ssm),
        side(r_att),
        gains[:, 1],
        grad_gate_up,
        r_dn.reshape(-1, width),
    )


def solution(mesh):
    return jax.shard_map(
        body,
        mesh=mesh,
        in_specs=(
            P(None, "seq", "dp"),
            P("dp", "seq", None),
            P(),
            P(),
            P("dp"),
            P("dp", None),
            P("dp", None),
            P(),
            P(),
            P(),
            P("dp", None),
            P("dp", None),
            P("dp"),
            P("dp", None),
            P("dp", None),
        ),
        out_specs=(
            P("dp", "seq", None),
            P(None, "seq", "dp"),
            P("dp"),
            P("dp", None),
            P("dp", None),
            P(),
            P(),
            P(),
            P("dp", None),
            P("dp", None),
            P("dp"),
            P("dp", None),
            P("dp", None),
        ),
        check_vma=False,
    )
```

```python
import types

import jax
import jax.numpy as jnp
import numpy as np
from jax import lax
from jax.experimental import pallas as pl
from jax.experimental.pallas import tpu as pltpu
from jax.sharding import PartitionSpec as P

FF = 2048
QUERY_HEADS = 8
KEY_VALUE_HEADS = 2
HEAD_WIDTH = 64
MH = 24
HP = 64
NS = 128
EPS = 1e-05
THETA = 100000000000.0
BF = jnp.bfloat16
F32 = jnp.float32
CORES = 2
CHIP_HEADS = MH // CORES
XW = CHIP_HEADS * HP
QW = QUERY_HEADS // CORES * HEAD_WIDTH
Z0, X0, Q0, KV0, B0, C0, T0 = 0, XW, 2 * XW, 2 * XW + QW, 2 * XW + QW + 128, 2 * XW + QW + 256, 2 * XW + QW + 384
COLS = T0 + 128
CHUNK = 256
QB = 256
FAR = -1e30
MIB = 1 << 20
MESH = pl.DeviceIdType.MESH
VM = pltpu.VMEM


def dot(a, b, dims=((1,), (0,)), precision=None):
    return lax.dot_general(a, b, (dims, ((), ())), precision=precision, preferred_element_type=F32)


def lanes(rows, width=128):
    return lax.broadcasted_iota(jnp.int32, (rows, width), 1)


def swap_halves(v):
    low = lanes(v.shape[0], v.shape[1]) % 64 < 32
    return jnp.where(low, pltpu.roll(v, v.shape[1] - 32, 1), pltpu.roll(v, 32, 1))


def turn(v, cosine, sine):
    return v * cosine + swap_halves(v) * sine


def turn_back(v, cosine, sine):
    return v * cosine - swap_halves(v) * sine


def widen(v, spread):
    v = jnp.where(lanes(v.shape[0]) < 64, v, 0.0)
    top = v.astype(BF)
    rest = (v - top.astype(F32)).astype(BF).astype(F32)
    both = top.astype(F32) + pltpu.roll(rest, 64, 1)
    return dot(both.astype(BF), spread)


def attn_masks(segc_ref, segr_ref, i, upto):
    rows = pl.ds(i * QB, QB)
    same = segc_ref[rows, 0:1] == segr_ref[0:1, 0:upto]
    t = lax.broadcasted_iota(jnp.int32, (QB, upto), 0) + i * QB
    u = lax.broadcasted_iota(jnp.int32, (QB, upto), 1)
    return jnp.where(same & (u <= t), 0.0, FAR)


def key_value_pairs(kv, cosine, sine):
    low = lanes(kv.shape[0]) < 64
    other = pltpu.roll(kv, 64, 1)
    kk = turn(jnp.where(low, kv, other), cosine, sine)
    vv = jnp.where(low, other, kv)
    return kk.astype(BF), vv.astype(BF)


def attention_forward(proj_ref, cos_ref, sin_ref, segc_ref, segr_ref, attn_ref, lse_ref, tick):
    seq_len = proj_ref.shape[0]
    kk, vv = key_value_pairs(proj_ref[:, KV0 : KV0 + 128].astype(F32), cos_ref[...], sin_ref[...])
    low = lanes(QB) < 64
    for i in range(seq_len // QB):
        rows = slice(i * QB, (i + 1) * QB)
        upto = (i + 1) * QB
        mask = attn_masks(segc_ref, segr_ref, i, upto)
        tops = jnp.zeros((QB, 128), F32)
        for pair in range(QW // 128):
            q = proj_ref[rows, Q0 + 128 * pair : Q0 + 128 * (pair + 1)].astype(F32)
            q = turn(q, cos_ref[rows, :], sin_ref[rows, :]) * HEAD_WIDTH**-0.5
            outs = []
            for half in range(2):
                qh = jnp.where(low if half == 0 else ~low, q, 0.0).astype(BF)
                s = dot(qh, kk[:upto], ((1,), (1,))) + mask
                top = jnp.max(s, axis=1, keepdims=True)
                e = jnp.exp(s - top)
                total = jnp.sum(e, axis=1, keepdims=True)
                outs.append(dot(e.astype(BF), vv[:upto]) / total)
                tops = jnp.where(lanes(QB) == 2 * pair + half, top + jnp.log(total), tops)
                tick()
            attn_ref[rows, 128 * pair : 128 * (pair + 1)] = jnp.where(low, outs[0], outs[1]).astype(BF)
        lse_ref[rows, :] = tops


def attention_backward(proj_ref, cos_ref, sin_ref, segc_ref, segr_ref, attn_ref, lse_ref, gattn_ref, gproj_ref, gkv, tick):
    seq_len = proj_ref.shape[0]
    kk, vv = key_value_pairs(proj_ref[:, KV0 : KV0 + 128].astype(F32), cos_ref[...], sin_ref[...])
    low = lanes(QB) < 64
    gkv[...] = jnp.zeros_like(gkv)
    pick = (lax.broadcasted_iota(jnp.int32, (QW, 128), 0) // 64 == lanes(QW)).astype(BF)
    for i in range(seq_len // QB):
        rows = slice(i * QB, (i + 1) * QB)
        upto = (i + 1) * QB
        same = segc_ref[0:upto, 0:1] == segr_ref[0:1, rows]
        t = lanes(upto, QB) + i * QB
        u = lax.broadcasted_iota(jnp.int32, (upto, QB), 0)
        mask = jnp.where(same & (u <= t), 0.0, FAR)
        weighed = gattn_ref[rows, :].astype(F32) * attn_ref[rows, :].astype(F32)
        deltas = dot(weighed.astype(BF), pick).T
        tops = lse_ref[rows, :].T
        for pair in range(QW // 128):
            cosine, sine = cos_ref[rows, :], sin_ref[rows, :]
            q = proj_ref[rows, Q0 + 128 * pair : Q0 + 128 * (pair + 1)].astype(F32)
            q = turn(q, cosine, sine) * HEAD_WIDTH**-0.5
            g = gattn_ref[rows, 128 * pair : 128 * (pair + 1)]
            grads = []
            for half in range(2):
                head = 2 * pair + half
                mine = low if half == 0 else ~low
                qh = jnp.where(mine, q, 0.0).astype(BF)
                gh = jnp.where(mine, g, jnp.zeros_like(g))
                s = dot(kk[:upto], qh, ((1,), (1,))) + mask
                p = jnp.exp(s - tops[head : head + 1, :])
                gp = dot(vv[:upto], gh, ((1,), (1,)))
                gs = (p * (gp - deltas[head : head + 1, :])).astype(BF)
                gkv[0:upto, 0:128] += dot(gs, qh)
                gkv[0:upto, 128:256] += dot(p.astype(BF), gh)
                grads.append(dot(gs, kk[:upto], ((0,), (0,))))
                tick()
            gq = jnp.where(low, grads[0], grads[1]) * HEAD_WIDTH**-0.5
            gproj_ref[rows, Q0 + 128 * pair : Q0 + 128 * (pair + 1)] = turn_back(gq, cosine, sine).astype(BF)
    gk = gkv[:, 0:128]
    gv = gkv[:, 128:256]
    gk = turn_back(gk + pltpu.roll(gk, 64, 1), cos_ref[...], sin_ref[...])
    gv = gv + pltpu.roll(gv, 64, 1)
    gproj_ref[:, KV0 : KV0 + 128] = jnp.where(lanes(seq_len) < 64, gk, gv).astype(BF)


def scan_pieces(j, proj_ref, segc_ref, segr_ref, par_ref):
    rows = pl.ds(j * CHUNK, CHUNK)
    seg = segc_ref[rows, :]
    prev = segc_ref[pl.ds(j * CHUNK - 1, 1), :] if j else jnp.full((1, 128), -1, jnp.int32)
    last = segc_ref[pl.ds(j * CHUNK + CHUNK - 1, 1), :]
    valid = lanes(CHUNK) < CHIP_HEADS
    raw = proj_ref[rows, T0 : T0 + 128].astype(F32) + par_ref[0:1, :]
    dt = jnp.where(valid, jnp.maximum(raw, 0.0) + jnp.log1p(jnp.exp(-jnp.abs(raw))), 0.0)
    decay = dt * par_ref[1:2, :]
    place = lax.broadcasted_iota(jnp.int32, (CHUNK, CHUNK), 0)
    under = (place >= lanes(CHUNK, CHUNK)).astype(F32)
    cum = dot(under, decay, precision=lax.Precision.HIGHEST)
    end = cum[CHUNK - 1 : CHUNK, :]
    from_start = jnp.where(seg == prev, jnp.exp(cum), 0.0)
    to_end = jnp.where(seg == last, jnp.exp(end - cum), 0.0)
    keep = jnp.where(last == prev, jnp.exp(end), 0.0)
    return rows, raw, dt, decay, cum, from_start, to_end, keep, under


def scan_forward(proj_ref, segc_ref, segr_ref, par_ref, spread_ref, wide_ref, gated_ref, y_ref, states_ref, state, tick):
    spread = spread_ref[...]
    state[...] = jnp.zeros_like(state)

    for j in range(proj_ref.shape[0] // CHUNK):
        rows, raw, dt, decay, cum, from_start, to_end, keep, under = scan_pieces(j, proj_ref, segc_ref, segr_ref, par_ref)
        place = lax.broadcasted_iota(jnp.int32, (CHUNK, CHUNK), 0)
        same = segc_ref[rows, 0:1] == segr_ref[0:1, rows]
        mask = jnp.where(same & (place >= lanes(CHUNK, CHUNK)), 0.0, FAR)
        cum_t = cum.T
        b = proj_ref[rows, B0 : B0 + 128]
        c = proj_ref[rows, C0 : C0 + 128]
        cb = dot(c, b, ((1,), (1,)))
        x = proj_ref[rows, X0 : X0 + XW].astype(F32)
        xdt = x * widen(dt, spread)
        xdt_low = xdt.astype(BF)
        old = state[...]
        states_ref[j] = old
        y_state = dot(c, old.astype(BF)) * widen(from_start, spread)
        low = lanes(CHUNK) < 64
        for pair in range(CHIP_HEADS // 2):
            cols = slice(128 * pair, 128 * (pair + 1))
            xp = xdt_low[:, cols]
            local = y_state[:, cols]
            for half in range(2):
                h = 2 * pair + half
                spread_h = jnp.exp(cum[:, h : h + 1] - cum_t[h : h + 1, :] + mask)
                mix = (cb * spread_h).astype(BF)
                xh = jnp.where(low if half == 0 else ~low, xp, jnp.zeros_like(xp))
                local = local + dot(mix, xh)
            y_ref[rows, cols] = local
            y = (local + x[:, cols] * wide_ref[0:1, cols]).astype(BF).astype(F32)
            z = proj_ref[rows, Z0 + 128 * pair : Z0 + 128 * (pair + 1)].astype(F32)
            gated_ref[rows, cols] = (y * (z / (1.0 + jnp.exp(-z)))).astype(BF)
            tick()
        weighted = (xdt * widen(to_end, spread)).astype(BF)
        keep_wide = widen(jnp.broadcast_to(keep, (8, 128)), spread)[0:1, :]
        state[...] = old * keep_wide + dot(b, weighted, ((0,), (0,)))


def gate_backward(proj_ref, wide_ref, y_ref, ggated_ref, gproj_ref, gy_ref, tick):
    for j in range(proj_ref.shape[0] // CHUNK):
        rows = pl.ds(j * CHUNK, CHUNK)
        x = proj_ref[rows, X0 : X0 + XW].astype(F32)
        z = proj_ref[rows, Z0 : Z0 + XW].astype(F32)
        gg = ggated_ref[rows, :].astype(F32)
        y = (y_ref[rows, :] + x * wide_ref[0:1, :]).astype(BF).astype(F32)
        sig = 1.0 / (1.0 + jnp.exp(-z))
        gy_ref[rows, :] = (gg * (z * sig)).astype(BF)
        gproj_ref[rows, Z0 : Z0 + XW] = (gg * y * (sig * (1.0 + z * (1.0 - sig)))).astype(BF)
        tick()


def scan_backward(proj_ref, segc_ref, segr_ref, par_ref, spread_ref, wide_ref, y_ref, states_ref, gy_ref, gproj_ref, gpar_ref, gstate, tick):
    spread = spread_ref[...]
    gstate[...] = jnp.zeros_like(gstate)
    gpar_ref[...] = jnp.zeros_like(gpar_ref)
    chunks = proj_ref.shape[0] // CHUNK

    def narrow(v):
        top = v.astype(BF)
        rest = (v - top.astype(F32)).astype(BF)
        return dot(top, spread, ((1,), (1,))) + dot(rest, spread, ((1,), (1,)))

    for j in reversed(range(chunks)):
        rows, raw, dt, decay, cum, from_start, to_end, keep, under = scan_pieces(j, proj_ref, segc_ref, segr_ref, par_ref)
        place = lax.broadcasted_iota(jnp.int32, (CHUNK, CHUNK), 0)
        same = segc_ref[rows, 0:1] == segr_ref[0:1, rows]
        mask = jnp.where(same & (place <= lanes(CHUNK, CHUNK)), 0.0, FAR)
        cum_t = cum.T
        b = proj_ref[rows, B0 : B0 + 128]
        c = proj_ref[rows, C0 : C0 + 128]
        bc = dot(b, c, ((1,), (1,)))
        x = proj_ref[rows, X0 : X0 + XW].astype(F32)
        dt_wide = widen(dt, spread)
        xdt_low = (x * dt_wide).astype(BF)
        start_wide = widen(from_start, spread)
        end_wide = widen(to_end, spread)
        old = states_ref[j]
        gnew = gstate[...]
        y_own = y_ref[rows, :]
        gy_low = gy_ref[rows, :]
        gy = gy_low.astype(F32)
        gx_state = end_wide * dot(b, gnew.astype(BF))
        gbc = jnp.zeros((CHUNK, CHUNK), F32)
        low = lanes(CHUNK) < 64
        gxdt = []
        for pair in range(CHIP_HEADS // 2):
            cols = slice(128 * pair, 128 * (pair + 1))
            xp, gp = xdt_low[:, cols], gy_low[:, cols]
            total = gx_state[:, cols]
            for half in range(2):
                h = 2 * pair + half
                mine = low if half == 0 else ~low
                spread_h = jnp.exp(cum_t[h : h + 1, :] - cum[:, h : h + 1] + mask)
                mix = (bc * spread_h).astype(BF)
                gh = jnp.where(mine, gp, jnp.zeros_like(gp))
                total = total + dot(mix, gh)
                gbc = gbc + dot(xp, gh, ((1,), (1,))) * spread_h
            gxdt.append(total)
            tick()
        gxdt = jnp.concatenate(gxdt, axis=1)
        gstart = (gy * start_wide).astype(BF)
        weighted = (xdt_low.astype(F32) * end_wide).astype(BF)
        gbc_low = gbc.astype(BF)
        gnew_low, old_low = gnew.astype(BF), old.astype(BF)
        gproj_ref[rows, C0 : C0 + 128] = (dot(gbc_low, b, ((0,), (0,))) + dot(gstart, old_low, ((1,), (1,)))).astype(BF)
        gproj_ref[rows, B0 : B0 + 128] = (dot(gbc_low, c) + dot(weighted, gnew_low, ((1,), (1,)))).astype(BF)
        keep_wide = widen(jnp.broadcast_to(keep, (8, 128)), spread)[0:1, :]
        kept = jnp.sum(old * gnew, axis=0, keepdims=True) * keep_wide
        gstate[...] = gnew * keep_wide + dot(c, gstart, ((0,), (0,)))
        xdt_f = xdt_low.astype(F32)
        gcum = narrow(gy * y_own) - narrow(xdt_f * gxdt)
        at_end = jnp.sum(xdt_f * gx_state, axis=0, keepdims=True) + kept
        at_end = narrow(jnp.broadcast_to(at_end, (8, XW)))[0:1, :]
        gdecay = dot(under, gcum, ((0,), (0,)), precision=lax.Precision.HIGHEST) + at_end
        gdt = narrow(gxdt * x) + gdecay * par_ref[1:2, :]
        graw = gdt / (1.0 + jnp.exp(-raw))
        graw = jnp.where(lanes(CHUNK) < CHIP_HEADS, graw, 0.0)
        gproj_ref[rows, T0 : T0 + 128] = graw.astype(BF)
        gproj_ref[rows, X0 : X0 + XW] = (gxdt * dt_wide + gy * wide_ref[0:1, :]).astype(BF)
        gpar_ref[0:1, :] += jnp.sum(graw, axis=0, keepdims=True)
        gpar_ref[1:2, :] += jnp.sum(gdecay * decay, axis=0, keepdims=True)
        skip = jnp.sum(gy * x, axis=0, keepdims=True)
        gpar_ref[2:3, :] += narrow(jnp.broadcast_to(skip, (8, XW)))[0:1, :]


class Ticker:
    def __init__(self, steps, ticks=1):
        self.steps, self.done = steps, 0
        self.plan(len(steps), ticks)

    def plan(self, count, ticks):
        self.first, self.last = self.done, min(self.done + count, len(self.steps))
        self.ticks, self.calls = ticks, 0

    def run(self, upto):
        while self.done < upto:
            if not isinstance(self.steps[self.done], int):
                self.steps[self.done]()
            self.done += 1

    def __call__(self):
        self.calls = min(self.calls + 1, self.ticks)
        self.run(self.first + (self.last - self.first) * self.calls // self.ticks)

    def reach(self, mark):
        if mark in self.steps[self.done :]:
            self.run(self.steps.index(mark) + 1)

    def drain(self):
        self.run(len(self.steps))


def whole(n):
    return [pl.BlockSpec(memory_space=VM)] * n


def place():
    d, s = lax.axis_index("dp"), lax.axis_index("seq")
    return d // 2, d % 2, s // 2, s % 2


def device(z, x, y, c):
    return (2 * z + x, 2 * y + c)


def greet(peers):
    barrier = pltpu.get_barrier_semaphore()
    for peer in peers:
        pl.semaphore_signal(barrier, inc=1, device_id=peer, device_id_type=MESH)
    pl.semaphore_wait(barrier, len(peers))


def send(src, dst, sems, k, target):
    copy = pltpu.make_async_remote_copy(
        src_ref=src, dst_ref=dst, send_sem=sems[0].at[k], recv_sem=sems[1].at[k], device_id=target, device_id_type=MESH
    )
    copy.start()
    return copy


def landed(dst, sems, k, target):
    pltpu.make_async_remote_copy(
        src_ref=dst, dst_ref=dst, send_sem=sems[0].at[k], recv_sem=sems[1].at[k], device_id=target, device_id_type=MESH
    ).wait_recv()


ARRAY_SENDS = 14
CORNER_X = 3
W_CUTS = 3


class Gather:
    def __init__(self, src, dst, sems, base, local_sem):
        self.src, self.dst, self.sems, self.base = src, dst, sems, base
        self.local_sem = local_sem
        self.z, self.x, self.y, self.c = place()
        half = src.shape[0] // 2
        self.mine = pl.ds(self.y * half, half)
        self.other = pl.ds((1 - self.y) * half, half)
        self.sent, self.sent_inner = [], []
        self.inner = (self.z == 1) | (self.z == 2)
        self.xpeer = device(self.z, 1 - self.x, self.y, self.c)
        self.ypeer = device(self.z, self.x, 1 - self.y, self.c)

    def push_inner(self, k, src, dst, target):
        def copy():
            return pltpu.make_async_remote_copy(
                src_ref=src,
                dst_ref=dst,
                send_sem=self.sems[0].at[self.base + k],
                recv_sem=self.sems[1].at[self.base + 2],
                device_id=target,
                device_id_type=MESH,
            )

        pl.when(self.inner)(lambda: copy().start())
        self.sent_inner.append(copy)

    def block(self, r, x, rows):
        return self.dst.at[2 * (self.z ^ r) + x, rows]

    def push(self, k, ref, target, dst=None):
        self.sent.append(send(ref, ref if dst is None else dst, self.sems, self.base + k, target))

    def start(self):
        own = 2 * self.z + self.x
        self.local = pltpu.make_async_copy(self.src, self.dst.at[own], self.local_sem)
        self.local.start()
        for r in (1, 2):
            target = device(self.z ^ r, self.x, self.y, self.c)
            self.push(r - 1, self.src.at[self.mine], target, self.dst.at[own, self.mine])
        target = device(self.z ^ 3, self.x, self.y, self.c)
        self.push_inner(2, self.src.at[self.mine], self.dst.at[own, self.mine], target)
        self.push(3, self.src, self.xpeer, self.dst.at[own])

    def cross(self):
        landed(self.block(0, 1 - self.x, slice(None)), self.sems, self.base + 3, self.xpeer)
        self.push(4, self.block(0, 1 - self.x, self.mine), device(self.z ^ 1, self.x, self.y, self.c))

    def forward(self, r):
        ref = self.block(r, self.x, self.mine)
        landed(ref, self.sems, self.base + r - 1, self.xpeer)
        if r == 2:
            self.push_inner(13, ref, ref, device(self.z ^ 1, self.x, self.y, self.c))
        self.push(6 + r, ref, self.ypeer)
        if r > 1:
            self.push(3 + r, ref, self.xpeer)

    def corner(self, r):
        if r == CORNER_X:
            ref = self.block(r, self.x, self.other)
            landed(ref, self.sems, self.base + 6 + r, self.ypeer)
            self.push(9 + r, ref, self.xpeer)
        else:
            ref = self.block(r, 1 - self.x, self.mine)
            landed(ref, self.sems, self.base + 3 + r, self.xpeer)
            self.push(9 + r, ref, self.ypeer)

    def arrive(self):
        for r in (1, 2, 3):
            if r == CORNER_X:
                landed(self.block(r, 1 - self.x, self.mine), self.sems, self.base + 3 + r, self.xpeer)
            else:
                landed(self.block(r, self.x, self.other), self.sems, self.base + 6 + r, self.ypeer)
            landed(self.block(r, 1 - self.x, self.other), self.sems, self.base + 9 + r, self.ypeer)
        self.local.wait()

    def finish(self):
        for copy in self.sent:
            copy.wait_send()
        for copy in self.sent_inner:
            pl.when(self.inner)(lambda copy=copy: copy().wait_send())


def gather_steps(gathers):
    def one(g):
        return [
            lambda: g.forward(1),
            g.cross,
            lambda: g.forward(2),
            lambda: g.forward(3),
        ]

    def corners(g):
        return [lambda r=r: g.corner(r) for r in (2, 3, 1)]

    steps = []
    count = len(gathers)
    for k in range(count + 1):
        if k + 2 < count:
            steps.append(gathers[k + 2].start)
        steps += one(gathers[k]) if k < count else []
        steps += corners(gathers[k - 1]) + [k - 1] if k else []
    return steps


def reduce_steps(sums, partner):
    def early(s):
        return [
            s.cross,
            lambda: s.relay(2),
            lambda: s.root(1),
            lambda: s.relay(3),
            lambda: s.relay(0),
        ]

    def late(s):
        return [lambda r=r: s.root(r) for r in (2, 3, 0)]

    steps = []
    count = len(sums)
    for k in range(count + 3):
        if k < count:
            steps += early(sums[k])
        if 0 <= k - 1 < count:
            steps += late(sums[k - 1])
        if 0 <= k - 2 < count:
            steps.append(lambda s=sums[k - 2]: s.total(partner))
        if 0 <= k - 3 < count:
            steps.append(lambda s=sums[k - 3]: s.spread(partner))
    return steps


def chip_peers():
    z, x, y, c = place()
    peers = [device(z ^ r, x, y, c) for r in (1, 2, 3)]
    peers += [device(z, 1 - x, y, c), device(z, x, 1 - y, c), device(z, x, y, 1 - c)]
    return peers


def start_kernel(dealt, in_proj, beside, rows, weights, w, kv, dsend, drecv, wsend, wrecv, local):
    z, x, y, c = place()
    own = 2 * z + x
    slot = 2 * y + c
    partner = device(z, x, y, 1 - c)
    others = [(r, i, j) for r in range(4) for i in range(2) for j in range(2) if r or i or j]
    targets = [device(z ^ r, x ^ i, y ^ j, c) for r, i, j in others]
    lane = lambda start, size: pl.ds(pl.multiple_of(start, 128), size)
    inner = MH * HP
    q_start = 2 * inner + 2 * NS
    kv_start = q_start + QUERY_HEADS * HEAD_WIDTH
    pieces = [
        (lane(XW * c, XW), w.at[:, Z0 : Z0 + XW]),
        (lane(inner + XW * c, XW), w.at[:, X0 : X0 + XW]),
        (lane(q_start + QW * c, QW), w.at[:, Q0 : Q0 + QW]),
        (lane(2 * inner, 2 * NS), w.at[:, B0 : B0 + 2 * NS]),
        (lane(kv_start, 256), kv),
    ]
    copies = [pltpu.make_async_copy(in_proj.at[:, cols], dst, local.at[2 + i]) for i, (cols, dst) in enumerate(pieces)]
    for copy in copies:
        copy.start()
    barrier = pltpu.get_barrier_semaphore()
    for peer in targets + [partner]:
        pl.semaphore_signal(barrier, inc=1, device_id=peer, device_id_type=MESH)
    first = c == 0
    lane_of = lanes(w.shape[0])
    near = beside[...].astype(F32).T
    far = pltpu.roll(near, 128 - CHIP_HEADS, 1)
    tail = jnp.where(lane_of < CHIP_HEADS, jnp.where(first, near, far), jnp.where(lane_of < CHIP_HEADS + 2, far, 0.0))
    w[:, T0 : T0 + 128] = tail.astype(BF)
    for copy in copies:
        copy.wait()
    keys, values = kv[:, :128].astype(F32), kv[:, 128:].astype(F32)
    keys = jnp.where(first, keys, pltpu.roll(keys, 64, 1))
    values = jnp.where(first, pltpu.roll(values, 64, 1), values)
    w[:, KV0 : KV0 + 128] = jnp.where(lane_of < 64, keys, values).astype(BF)
    pl.semaphore_wait(barrier, len(targets) + 1)
    sems = (dsend, drecv)
    cuts = [slice(i * COLS // W_CUTS, (i + 1) * COLS // W_CUTS) for i in range(W_CUTS)]
    gathers = [
        Gather(w.at[:, cols], weights.at[:, :, cols], (wsend, wrecv), ARRAY_SENDS * i, local.at[7 + i])
        for i, cols in enumerate(cuts)
    ]
    columns = lambda d: lane(d * 128, 128)
    sent = []
    for gather in gathers[:2]:
        gather.start()
    for k, (r, i, j) in enumerate(others):
        pack = 2 * (2 * (z ^ r) + (x ^ i)) + (y ^ j)
        sent.append(send(dealt.at[pack], rows.at[slot, :, columns(own)], sems, k, targets[k]))
    here = pltpu.make_async_copy(dealt.at[2 * own + y], rows.at[slot, :, columns(own)], local.at[1])
    here.start()
    for step in gather_steps(gathers):
        if not isinstance(step, int):
            step()
    here.wait()
    for same_y in (True, False):
        for k, (r, i, j) in enumerate(others):
            if (j == 0) == same_y:
                src = 2 * (z ^ r) + (x ^ i)
                landed(rows.at[2 * (y ^ j) + c, :, columns(src)], sems, k, targets[k])
        ref = rows.at[slot if same_y else 2 * (1 - y) + c]
        sent.append(send(ref, ref, sems, 15 if same_y else 16, partner))
    landed(rows.at[2 * y + 1 - c], sems, 15, partner)
    landed(rows.at[2 * (1 - y) + 1 - c], sems, 16, partner)
    for gather in gathers:
        gather.arrive()
    for copy in sent:
        copy.wait_send()
    for gather in gathers:
        gather.finish()


def start_transfers(dealt, in_proj, beside):
    packs, span, width = dealt.shape
    block = in_proj.shape[0]
    return pl.pallas_call(
        start_kernel,
        name="deal_and_gather",
        out_shape=(
            jax.ShapeDtypeStruct((4, span, 8 * width), BF),
            jax.ShapeDtypeStruct((8, block, COLS), BF),
        ),
        in_specs=whole(1) + any_specs(1) + whole(1),
        out_specs=tuple(any_specs(2)),
        scratch_shapes=[
            VM((block, COLS), BF),
            VM((block, 256), BF),
            pltpu.SemaphoreType.DMA((17,)),
            pltpu.SemaphoreType.DMA((17,)),
            pltpu.SemaphoreType.DMA((W_CUTS * ARRAY_SENDS,)),
            pltpu.SemaphoreType.DMA((W_CUTS * ARRAY_SENDS,)),
            pltpu.SemaphoreType.DMA((7 + W_CUTS,)),
        ],
        compiler_params=pltpu.CompilerParams(collective_id=0, has_side_effects=True),
    )(dealt, in_proj, beside)


def any_specs(n):
    return [pl.BlockSpec(memory_space=pl.ANY)] * n


class Cotangents:
    def __init__(self, src, dst, sems, local_sem):
        self.src, self.dst, self.sems, self.local_sem = src, dst, sems, local_sem
        self.z, self.x, self.y, self.c = place()
        self.slot = 2 * self.y + self.c
        self.partner = device(self.z, self.x, self.y, 1 - self.c)
        self.ypeer = device(self.z, self.x, 1 - self.y, self.c)

    def start(self):
        src, dst = self.src, self.dst
        self.sent = [
            send(src.at[1 - self.y], dst.at[self.slot], self.sems, 0, self.ypeer),
            send(src.at[self.y], dst.at[self.slot], self.sems, 1, self.partner),
        ]
        self.local = pltpu.make_async_copy(src.at[self.y], dst.at[self.slot], self.local_sem)
        self.local.start()

    def forward(self):
        ref = self.dst.at[2 * (1 - self.y) + self.c]
        landed(ref, self.sems, 0, self.ypeer)
        self.sent.append(send(ref, ref, self.sems, 2, self.partner))

    def arrive(self):
        landed(self.dst.at[2 * self.y + 1 - self.c], self.sems, 1, self.partner)
        landed(self.dst.at[2 * (1 - self.y) + 1 - self.c], self.sems, 2, self.partner)
        self.local.wait()

    def finish(self):
        for copy in self.sent:
            copy.wait_send()


class Halves:
    def __init__(self, gather, dst, sems, base, local_sem):
        self.gather, self.dst, self.sems, self.base, self.local_sem = gather, dst, sems, base, local_sem
        z, x, y, self.c = place()
        self.partner = device(z, x, y, 1 - self.c)

    def columns(self, k):
        half = self.gather.src.shape[1]
        return self.dst.at[:, :, pl.ds(pl.multiple_of(k * half, 128), half)]

    def start(self):
        src, c = self.gather.dst, self.c
        self.gather.arrive()
        self.local = pltpu.make_async_copy(src.at[pl.ds(4 * c, 4)], self.columns(c), self.local_sem)
        self.local.start()
        self.sent = send(src.at[pl.ds(4 * (1 - c), 4)], self.columns(c), self.sems, self.base, self.partner)

    def arrive(self):
        landed(self.columns(1 - self.c), self.sems, self.base, self.partner)
        self.local.wait()
        self.sent.wait_send()


def plain_forward_kernel(proj, cosine, sine, segc, segr, par, spread, wide, gated, attn, lse, y_own, states, state):
    tick = Ticker([])
    attention_forward(proj, cosine, sine, segc, segr, attn, lse, tick)
    scan_forward(proj, segc, segr, par, spread, wide, gated, y_own, states, state, tick)


def mixer_forward(proj, consts):
    seq_len = proj.shape[0]
    return pl.pallas_call(
        plain_forward_kernel,
        name="mixer_forward",
        out_shape=(
            jax.ShapeDtypeStruct((seq_len, XW), BF),
            jax.ShapeDtypeStruct((seq_len, QW), BF),
            jax.ShapeDtypeStruct((seq_len, 128), F32),
            jax.ShapeDtypeStruct((seq_len, XW), F32),
            jax.ShapeDtypeStruct((seq_len // CHUNK, NS, XW), F32),
        ),
        in_specs=whole(8),
        out_specs=tuple(whole(5)),
        scratch_shapes=[VM((NS, XW), F32)],
        compiler_params=pltpu.CompilerParams(vmem_limit_bytes=56 * MIB),
    )(proj, *consts)


class Reduce:
    def __init__(self, part, out, far, near_x, near_y, deep, sems, base):
        self.part, self.out, self.far, self.near_x, self.near_y, self.deep = part, out, far, near_x, near_y, deep
        self.sems, self.base = sems, base
        self.z, self.x, self.y, self.c = place()
        half = part.shape[1] // 2
        self.mine = pl.ds(self.y * half, half)
        self.other = pl.ds((1 - self.y) * half, half)
        self.xpeer = device(self.z, 1 - self.x, self.y, self.c)
        self.ypeer = device(self.z, self.x, 1 - self.y, self.c)
        self.sent = []

    def piece(self, r, x, rows):
        return self.part.at[2 * (self.z ^ r) + x, rows]

    def push(self, k, src, dst, target):
        self.sent.append(send(src, dst, self.sems, self.base + k, target))

    def start(self):
        zpeer = device(self.z ^ 1, self.x, self.y, self.c)
        self.push(5, self.piece(1, 1 - self.x, self.mine), self.near_x.at[1], zpeer)
        self.push(1, self.piece(1, 1 - self.x, self.other), self.far.at[1], zpeer)
        for r in (2, 3):
            far = self.piece(r, 1 - self.x, self.other)
            self.push(r, far, self.far.at[r], self.ypeer if r == 2 else self.xpeer)
        self.push(9, self.piece(1, self.x, self.other), self.near_y.at[1], self.ypeer)

    def add(self, ref, r, own):
        ref[r] = (own[...].astype(F32) + ref[r].astype(F32)).astype(BF)

    def cross(self):
        landed(self.far.at[1], self.sems, self.base + 1, self.xpeer)
        self.add(self.far, 1, self.piece(0, 1 - self.x, self.other))
        self.push(0, self.far.at[1], self.far.at[0], self.xpeer)
        landed(self.near_x.at[1], self.sems, self.base + 5, self.xpeer)
        self.add(self.near_x, 1, self.piece(0, 1 - self.x, self.mine))
        self.push(4, self.near_x.at[1], self.near_x.at[0], self.xpeer)

    def relay(self, r):
        landed(self.far.at[r], self.sems, self.base + r, self.xpeer)
        if r == 2:
            self.add(self.far, r, self.piece(r, 1 - self.x, self.mine))
            self.push(4 + r, self.far.at[r], self.near_x.at[r], self.xpeer)
            self.push(8 + r, self.piece(r, self.x, self.other), self.near_y.at[r], self.ypeer)
            return
        self.add(self.far, r, self.piece(r, self.x, self.other))
        self.push(8 + r, self.far.at[r], self.near_y.at[r], self.ypeer)
        if r:
            self.push(4 + r, self.piece(r, 1 - self.x, self.mine), self.near_x.at[r], self.xpeer)

    def root(self, r):
        landed(self.near_y.at[r], self.sems, self.base + 8 + r, self.ypeer)
        total = self.piece(r, self.x, self.mine)[...].astype(F32) + self.near_y[r].astype(F32)
        if r != 1:
            landed(self.near_x.at[r], self.sems, self.base + 4 + r, self.xpeer)
            total = total + self.near_x[r].astype(F32)
        self.near_y[r] = total.astype(BF)
        if r:
            target = device(self.z ^ r, self.x, self.y, self.c)
            self.push(11 + r, self.near_y.at[r], self.deep.at[r - 1], target)

    def total(self, partner):
        for r in (1, 2, 3):
            landed(self.deep.at[r - 1], self.sems, self.base + 11 + r, self.xpeer)
        total = self.near_y[0].astype(F32) + self.deep[0].astype(F32)
        total = total + (self.deep[1].astype(F32) + self.deep[2].astype(F32))
        self.out[self.c, self.mine] = total.astype(BF)
        ref = self.out.at[self.c, self.mine]
        self.push(15, ref, ref, self.ypeer)
        self.push(16, ref, ref, partner)

    def spread(self, partner):
        ref = self.out.at[self.c, self.other]
        landed(ref, self.sems, self.base + 15, self.ypeer)
        self.push(17, ref, ref, partner)

    def finish(self, partner):
        landed(self.out.at[1 - self.c, self.mine], self.sems, self.base + 16, partner)
        landed(self.out.at[1 - self.c, self.other], self.sems, self.base + 17, partner)
        for copy in self.sent:
            copy.wait_send()


REDUCE_SENDS = 18


def reduce_buffers(parts):
    scratch = []
    for p in parts:
        half = (p.shape[1] // 2, p.shape[2])
        scratch += [VM((4,) + half, BF)] * 3 + [VM((3,) + half, BF)]
    total = REDUCE_SENDS * len(parts)
    return scratch + [pltpu.SemaphoreType.DMA((total,))] * 2


def plain_backward_kernel(proj, cosine, sine, segc, segr, par, spread, wide, attn, lse, y_own, states, ggated, gattn, gproj, gpar, gkv, gstate, gy):
    tick = Ticker([])
    gate_backward(proj, wide, y_own, ggated, gproj, gy, tick)
    attention_backward(proj, cosine, sine, segc, segr, attn, lse, gattn, gproj, gkv, tick)
    scan_backward(proj, segc, segr, par, spread, wide, y_own, states, gy, gproj, gpar, gstate, tick)


def mixer_backward(proj, consts, saved, ggated, gattn):
    seq_len = proj.shape[0]
    return pl.pallas_call(
        plain_backward_kernel,
        name="mixer_backward",
        out_shape=(
            jax.ShapeDtypeStruct((seq_len, COLS), BF),
            jax.ShapeDtypeStruct((8, 128), F32),
        ),
        in_specs=whole(14),
        out_specs=tuple(whole(2)),
        scratch_shapes=[VM((seq_len, 256), F32), VM((NS, XW), F32), VM((seq_len, XW), BF)],
        compiler_params=pltpu.CompilerParams(vmem_limit_bytes=56 * MIB),
    )(proj, *consts, *saved, ggated, gattn)


class Mover:
    def __init__(self, sems):
        self.sems, self.used, self.loads, self.stores = sems, 0, {}, []

    def copy(self, src, dst):
        copy = pltpu.make_async_copy(src, dst, self.sems.at[self.used])
        self.used += 1
        copy.start()
        return copy

    def load(self, src, dst):
        self.loads.setdefault(id(dst), []).append(self.copy(src, dst))

    def need(self, *refs):
        for ref in refs:
            for copy in self.loads.pop(id(ref), []):
                copy.wait()

    def store(self, src, dst):
        copy = self.copy(src, dst)
        self.stores.append(copy)
        return copy

    def flush(self):
        for copies in self.loads.values():
            for copy in copies:
                copy.wait()
        for copy in self.stores:
            copy.wait()


def shape(dims, dtype=BF):
    return jax.ShapeDtypeStruct(tuple(dims), dtype)


def fused_call(kernel, name, inputs, outputs, scratch, spaces, collective_id):
    names = list(inputs) + list(outputs) + list(scratch)

    def wrapped(*refs):
        kernel(types.SimpleNamespace(**dict(zip(names, refs))))

    place_of = lambda n: pl.BlockSpec(memory_space=spaces.get(n, pl.ANY))
    outs = pl.pallas_call(
        wrapped,
        name=name,
        out_shape=tuple(outputs.values()),
        in_specs=[place_of(n) for n in inputs],
        out_specs=tuple(place_of(n) for n in outputs),
        scratch_shapes=list(scratch.values()),
        compiler_params=pltpu.CompilerParams(
            collective_id=collective_id, has_side_effects=True, vmem_limit_bytes=62 * MIB
        ),
    )(*inputs.values())
    return types.SimpleNamespace(**dict(zip(outputs, outs)))


def dma(n):
    return pltpu.SemaphoreType.DMA((n,))


def row_blocks(seq_len, size=256):
    return [slice(i, i + size) for i in range(0, seq_len, size)]


def mixer_constants(k, own, y, c):
    seq_len = k.segc_v.shape[0]
    pack = k.deal[2 * own + y]
    ends = [k.lengths[0, pack]]
    for i in (1, 2):
        ends.append(ends[-1] + k.lengths[i, pack])
    for ref, dims, axis in ((k.segc_v, (seq_len, 128), 0), (k.segr_v, (8, seq_len), 1)):
        place_of = lax.broadcasted_iota(jnp.int32, dims, axis)
        ref[...] = sum((place_of >= end).astype(jnp.int32) for end in ends)
    heads = k.heads[...]
    heads = jnp.where(c == 0, heads, pltpu.roll(heads, 128 - CHIP_HEADS, 1))
    heads = jnp.where(lanes(8) < CHIP_HEADS, heads, 0.0)
    k.par_v[0:1, :] = heads[0:1, :]
    k.par_v[1:2, :] = jnp.where(lanes(1) < CHIP_HEADS, -jnp.exp(heads[1:2, :]), 0.0)
    k.wide_v[...] = dot(jnp.broadcast_to(heads[2:3, :], (8, 128)), k.spread_v[...].astype(F32), precision=lax.Precision.HIGHEST)


def forward_fused(k):
    z, x, y, c = place()
    own = 2 * z + x
    partner = device(z, x, y, 1 - c)
    mover = Mover(k.local)
    lane = lambda start, size: pl.ds(pl.multiple_of(start, 128), size)
    half = k.dn.shape[0] // 2
    for side in range(2):
        for d in range(8):
            mover.load(k.gu.at[:, lane(side * FF + (2 * d + c) * half, half)], k.gu_s.at[:, side * FF // 2 + d * half : side * FF // 2 + (d + 1) * half])
    shard_loads, mover.loads = mover.loads, {}
    for src, dst in ((k.rows, k.rows_v), (k.w_in, k.w_in_v), (k.spread, k.spread_v), (k.cosine, k.cosine_v), (k.sine, k.sine_v)):
        mover.load(src, dst)
    greet(chip_peers())
    columns = lane(k.part_v.shape[1] // 2 * c, k.part_v.shape[1] // 2)
    pairs = (
        (k.ssm.at[:, columns], k.ssm_all),
        (k.att.at[:, columns], k.att_all),
        (k.gu_s, k.gu_w),
        (k.dn.at[pl.ds(half * c, half)], k.dn_w),
    )
    gathers = [Gather(a, b, (k.gsend, k.grecv), ARRAY_SENDS * i, k.own.at[i]) for i, (a, b) in enumerate(pairs)]
    cots = Cotangents(k.cot, k.cots_v, (k.csend, k.crecv), k.own.at[4])
    halves = [Halves(g, out, (k.csend, k.crecv), 3 + i, k.own.at[5 + i]) for i, (g, out) in enumerate(zip(gathers, (k.ssm_v, k.att_v)))]
    gathers[0].start()
    gathers[1].start()
    cots.start()
    for copies in shard_loads.values():
        for copy in copies:
            copy.wait()
    steps = gather_steps(gathers)
    at = steps.index(1) + 6
    steps[at:at] = [h.start for h in halves] + [9]
    steps.insert(steps.index(3) - 2, cots.forward)
    tick = Ticker(steps, 60)

    blocks = row_blocks(k.rows_v.shape[0])
    mover.need(k.rows_v, k.w_in_v)
    tile = k.w_in_v[:, T0 : T0 + 128].astype(F32).T
    k.gains_v[0:1, :] = tile[CHIP_HEADS : CHIP_HEADS + 1, :]
    k.gains_v[1:2, :] = tile[CHIP_HEADS + 1 : CHIP_HEADS + 2, :]
    mover.store(k.gains_v, k.gains)
    for rows in blocks:
        xs = k.rows_v[rows, :].astype(F32)
        unit, _ = rms_parts(xs)
        normed = (unit * k.gains_v[0:1, :]).astype(BF)
        k.normed_v[rows, :] = normed
        for n in range(0, COLS, 768):
            k.proj_v[rows, n : n + 768] = dot(normed, k.w_in_v[:, n : n + 768]).astype(BF)
            tick()
    mover.store(k.proj_v, k.proj)
    kept_normed = mover.store(k.normed_v, k.normed)
    mover.need(k.spread_v, k.cosine_v, k.sine_v)
    mixer_constants(k, own, y, c)
    for src, dst in ((k.segc_v, k.segc), (k.segr_v, k.segr), (k.par_v, k.par), (k.wide_v, k.wide)):
        mover.store(src, dst)
    attention_forward(k.proj_v, k.cosine_v, k.sine_v, k.segc_v, k.segr_v, k.attn_v, k.lse_v, tick)
    mover.store(k.attn_v, k.attn)
    mover.store(k.lse_v, k.lse)
    scan_forward(k.proj_v, k.segc_v, k.segr_v, k.par_v, k.spread_v, k.wide_v, k.gated_v, k.y_v, k.states_v, k.state, tick)
    mover.store(k.gated_v, k.gated)
    mover.store(k.y_v, k.y)
    mover.store(k.states_v, k.states)

    tick.reach(9)
    for h in halves:
        h.arrive()
    mover.store(k.ssm_v, k.w_ssm)
    mover.store(k.att_v, k.w_att)
    sent = []
    for i, rows in enumerate(blocks):
        part = dot(k.gated_v[rows, :], k.ssm_v[...].reshape(XW, -1))
        part = part + dot(k.attn_v[rows, :], k.att_v[...].reshape(QW, -1))
        k.part_v[rows, :] = part.astype(BF)
        sent.append(send(k.part_v.at[rows], k.got_v.at[rows], (k.psend, k.precv), i, partner))
        tick()
    kept_normed.wait()
    mover.stores = [v for v in mover.stores if v is not kept_normed]
    for i, rows in enumerate(blocks):
        landed(k.got_v.at[rows], (k.psend, k.precv), i, partner)
        middle = k.rows_v[rows, :].astype(F32) + (k.part_v[rows, :].astype(F32) + k.got_v[rows, :].astype(F32))
        k.middle_v[rows, :] = middle
        unit, _ = rms_parts(middle)
        k.normed_v[rows, :] = (unit * k.gains_v[1:2, :]).astype(BF)
        tick()
    mover.store(k.middle_v, k.middle)
    mover.store(k.normed_v, k.h2)

    tick.reach(2)
    gathers[2].arrive()
    mover.store(k.gu_w, k.w_gu)
    for rows in blocks:
        for n in range(0, FF // 2, 512):
            for side in (0, FF // 2):
                cols = slice(side + n, side + n + 512)
                w = k.gu_w[:, :, cols].reshape(-1, 512)
                k.w_in_v[rows, cols] = dot(k.normed_v[rows, :], w).astype(BF)
            gate = k.w_in_v[rows, n : n + 512].astype(F32)
            up = k.w_in_v[rows, FF // 2 + n : FF // 2 + n + 512].astype(F32)
            k.act_v[rows, n : n + 512] = (silu(gate) * up).astype(BF)
            tick()
    mover.store(k.w_in_v.at[:, 0:FF], k.hidden)
    mover.store(k.act_v, k.act)
    tick.drain()
    cots.arrive()
    mover.store(k.cots_v, k.cots)
    width = k.rows_v.shape[1]
    for m in range(0, FF // 2, 256):
        k.gdn_v[m : m + 256, :] = dot(k.act_v[:, m : m + 256], k.cots_v[...].reshape(-1, width), ((0,), (0,))).astype(BF)
    mover.store(k.gdn_v, k.g_dn)
    gathers[3].arrive()
    mover.store(k.dn_w, k.w_dn)
    for g in gathers:
        g.finish()
    cots.finish()
    for copy in sent:
        copy.wait_send()
    mover.flush()


def forward_stage(rows, w_in, tables, heads, deal, lengths, cot, shards):
    seq_len, width = rows.shape
    ssm, att, gu, dn = shards
    cosine, sine, spread = tables
    chunks = seq_len // CHUNK
    total = 4 * ARRAY_SENDS
    half = dn.shape[0] // 2
    inputs = dict(
        rows=rows, w_in=w_in, cosine=cosine, sine=sine, spread=spread, heads=heads, deal=deal, lengths=lengths, cot=cot, ssm=ssm, att=att, gu=gu, dn=dn
    )
    spaces = dict(heads=VM, deal=pltpu.SMEM, lengths=pltpu.SMEM)
    square = shape((seq_len, width))
    outputs = dict(
        proj=shape((seq_len, COLS)),
        normed=square,
        gains=shape((8, width), F32),
        attn=shape((seq_len, QW)),
        lse=shape((seq_len, 128), F32),
        gated=shape((seq_len, XW)),
        y=shape((seq_len, XW), F32),
        states=shape((chunks, NS, XW), F32),
        w_ssm=shape((4, ssm.shape[0], width)),
        w_att=shape((4, att.shape[0], width)),
        w_gu=shape((8, gu.shape[0], FF)),
        w_dn=shape((8, half, width)),
        middle=shape((seq_len, width), F32),
        h2=square,
        hidden=shape((seq_len, FF)),
        act=shape((seq_len, FF // 2)),
        cots=shape((4,) + cot.shape[1:]),
        g_dn=shape((FF // 2, width)),
        segc=shape((seq_len, 128), jnp.int32),
        segr=shape((8, seq_len), jnp.int32),
        par=shape((8, 128), F32),
        wide=shape((8, XW), F32),
    )
    out = types.SimpleNamespace(**outputs)
    buffer = lambda v: VM(v.shape, v.dtype)
    scratch = dict(
        rows_v=buffer(rows),
        w_in_v=buffer(w_in),
        cosine_v=buffer(cosine),
        sine_v=buffer(sine),
        spread_v=buffer(spread),
        segc_v=buffer(out.segc),
        segr_v=buffer(out.segr),
        par_v=buffer(out.par),
        wide_v=buffer(out.wide),
        proj_v=buffer(out.proj),
        normed_v=buffer(square),
        gains_v=buffer(out.gains),
        attn_v=buffer(out.attn),
        lse_v=buffer(out.lse),
        gated_v=buffer(out.gated),
        y_v=buffer(out.y),
        states_v=buffer(out.states),
        middle_v=buffer(out.middle),
        act_v=buffer(out.act),
        cots_v=buffer(out.cots),
        ssm_v=buffer(out.w_ssm),
        att_v=buffer(out.w_att),
        gu_w=buffer(out.w_gu),
        dn_w=buffer(out.w_dn),
        gu_s=VM((gu.shape[0], FF), BF),
        ssm_all=VM((8, ssm.shape[0], width // 2), BF),
        att_all=VM((8, att.shape[0], width // 2), BF),
        gdn_v=buffer(out.g_dn),
        part_v=buffer(square),
        got_v=buffer(square),
        state=VM((NS, XW), F32),
        gsend=dma(total),
        grecv=dma(total),
        csend=dma(5),
        crecv=dma(5),
        psend=dma(4),
        precv=dma(4),
        own=dma(7),
        local=dma(48),
    )
    return fused_call(forward_fused, "forward", inputs, outputs, scratch, spaces, 1)


def feed_forward_fused(k):
    z, x, y, c = place()
    partner = device(z, x, y, 1 - c)
    ypeer = device(z, x, 1 - y, c)
    mover = Mover(k.local)
    for src, dst in k.loads:
        mover.load(src, dst)
    greet(chip_peers())
    pairs = ((k.g_dn_v, k.red_dn), (k.gate_v, k.red_gate))
    sums = [Reduce(part, out, *k.bufs[4 * i : 4 * i + 4], (k.rsend, k.rrecv), REDUCE_SENDS * i) for i, (part, out) in enumerate(pairs)]
    mover.need(k.g_dn_v)
    sums[0].start()
    tick = Ticker(reduce_steps(sums, partner))
    seq_len, width = k.middle_v.shape
    span = seq_len // 4
    blocks = row_blocks(seq_len)
    half = FF // 2
    flat = lambda ref: ref[...].reshape(-1, ref.shape[-1])
    pair = (k.psend, k.precv)

    mover.need(k.cots_v, k.w_dn_v, k.hidden_v)
    for i, rows in enumerate(blocks):
        g_act = dot(k.cots_v[i], flat(k.w_dn_v), ((1,), (1,))).astype(BF).astype(F32)
        gate = k.hidden_v[rows, :half].astype(F32)
        up = k.hidden_v[rows, half:].astype(F32)
        sig = 1.0 / (1.0 + jnp.exp(-gate))
        k.hidden_v[rows, :half] = (g_act * up * (sig * (1.0 + gate * (1.0 - sig)))).astype(BF)
        k.hidden_v[rows, half:] = (g_act * (gate * sig)).astype(BF)
    mover.need(k.h2_v)
    tick.plan(2, 4)
    for d in range(0, 8, 2):
        grad = dot(k.h2_v[:, 128 * d : 128 * d + 256], k.hidden_v[:, :half], ((0,), (0,))).astype(BF)
        k.gate_v[d : d + 2] = grad.reshape(2, 128, half)
        tick()
    sums[1].start()
    tick.plan(13, 24)
    mover.need(k.w_gu_v)
    sent = []
    for i, rows in enumerate(blocks):
        part = dot(k.hidden_v[rows, :], flat(k.w_gu_v), ((1,), (1,)))
        k.part_v[rows, :] = part.astype(BF)
        sent.append(send(k.part_v.at[rows], k.got_v.at[rows], pair, i, partner))
        tick()
    mover.need(k.act_v)
    for j in range(2):
        rows = pl.ds(pl.multiple_of((2 * j + 1 - c) * span, span), span)
        k.opart_v[j] = dot(k.act_v[rows, :], flat(k.w_dn_v)).astype(BF)
        sent.append(send(k.opart_v.at[j], k.ogot_v.at[j], pair, 4 + j, partner))
        tick()
    for d in range(0, 8, 2):
        grad = dot(k.h2_v[:, 128 * d : 128 * d + 256], k.hidden_v[:, half:], ((0,), (0,))).astype(BF)
        k.up_v[d : d + 2] = grad.reshape(2, 128, half)
        tick()
    mover.store(k.up_v, k.g_up)

    mover.need(k.middle_v)
    for j in range(2):
        rows = pl.ds(pl.multiple_of((2 * j + c) * span, span), span)
        own = k.middle_v[rows, :] + dot(k.act_v[rows, :], flat(k.w_dn_v)).astype(BF).astype(F32)
        landed(k.ogot_v.at[j], pair, 4 + j, partner)
        k.out_v[j] = (own + k.ogot_v[j].astype(F32)).astype(BF)
        tick()
    sent.append(send(k.out_v.at[1 - y], k.output.at[y], pair, 14, ypeer))
    mover.store(k.out_v.at[y], k.output.at[y])

    mover.need(k.middle_v, k.gains_v, k.w_ssm_v, k.w_att_v)
    gain = k.gains_v[1:2, :]
    grad_gain = jnp.zeros((1, width), F32)
    for i, rows in enumerate(blocks):
        landed(k.got_v.at[rows], pair, i, partner)
        g_two = (k.part_v[rows, :].astype(F32) + k.got_v[rows, :].astype(F32)).astype(BF).astype(F32)
        unit, scale = rms_parts(k.middle_v[rows, :])
        grad_gain = grad_gain + jnp.sum(g_two * unit, axis=0, keepdims=True)
        g_mid = k.cots_v[i].astype(F32) + rms_back(unit, scale, gain, g_two)
        k.got_f32[rows, :] = g_mid
        branch = g_mid.astype(BF)
        k.branch_v[rows, :] = branch
        tick()
        k.ggated_v[rows, :] = dot(branch, flat(k.w_ssm_v), ((1,), (1,))).astype(BF)
        k.gattn_v[rows, :] = dot(branch, flat(k.w_att_v), ((1,), (1,))).astype(BF)
        tick()
    k.gffn_v[0:1, :] = 0.5 * grad_gain
    mover.store(k.gffn_v, k.gffn)
    mover.store(k.ggated_v, k.ggated)
    mover.store(k.gattn_v, k.gattn)
    for j in range(2):
        mover.store(k.got_f32.at[pl.ds(pl.multiple_of((2 * j + c) * span, span), span)], k.g_mid.at[j])

    mover.need(k.gated_v, k.attn_v)
    moves = []
    n = 6
    for source, rows, hold, out in ((k.gated_v, XW, k.gssm_v, k.g_ssm), (k.attn_v, QW, k.gatt_v, k.g_att)):
        for m in range(0, rows, 256):
            hold[m : m + 256, :] = dot(source[:, m : m + 256], k.branch_v[...], ((0,), (0,))).astype(BF)
            tick()
        own = rows // 4
        for d in range(4):
            columns = lambda e: hold.at[pl.ds(d * own, own), pl.ds(pl.multiple_of(e * (width // 2), 128), width // 2)]
            mover.store(columns(c), out.at[4 * c + d])
            moves.append((out.at[4 * (1 - c) + d], n))
            sent.append(send(columns(1 - c), out.at[4 * c + d], pair, n, partner))
            n += 1

    tick.drain()
    for s in sums:
        s.finish(partner)
    for ref, i in moves:
        landed(ref, pair, i, partner)
    landed(k.output.at[1 - y], pair, 14, ypeer)
    for copy in sent:
        copy.wait_send()
    mover.flush()


def reduce_scratch(shapes):
    bufs = []
    for dims in shapes:
        half = (dims[1] // 2, dims[2])
        bufs += [VM((4,) + half, BF)] * 3 + [VM((3,) + half, BF)]
    return {"b" + str(i): b for i, b in enumerate(bufs)}


def loaded(inputs, names=None):
    return {n + "_v": VM(v.shape, v.dtype) for n, v in inputs.items()}


def with_lists(kernel, inputs, bufs):
    def run(k):
        refs = vars(k)
        k.loads = [(refs[n], refs[n + "_v"]) for n in inputs if n + "_v" in refs]
        k.bufs = [refs[n] for n in bufs]
        kernel(k)

    return run


def feed_forward_stage(f):
    seq_len, width = f.middle.shape
    inputs = dict(
        g_dn=f.g_dn.reshape(8, -1, width),
        cots=f.cots,
        w_dn=f.w_dn,
        hidden=f.hidden,
        h2=f.h2,
        w_gu=f.w_gu,
        act=f.act,
        middle=f.middle,
        gains=f.gains,
        w_ssm=f.w_ssm,
        w_att=f.w_att,
        gated=f.gated,
        attn=f.attn,
    )
    span = seq_len // 4
    part = (8, width // 8, FF // 2)
    outputs = dict(
        output=shape((2, span, width)),
        red_dn=shape((2,) + inputs["g_dn"].shape[1:]),
        red_gate=shape((2,) + part[1:]),
        g_up=shape(part),
        g_ssm=shape((8, XW // 4, width // 2)),
        g_att=shape((8, QW // 4, width // 2)),
        ggated=shape((seq_len, XW)),
        gattn=shape((seq_len, QW)),
        g_mid=shape((2, span, width), F32),
        gffn=shape((8, width), F32),
    )
    bufs = reduce_scratch([inputs["g_dn"].shape, part])
    scratch = dict(
        **loaded(inputs),
        **bufs,
        gate_v=VM(part, BF),
        up_v=VM(part, BF),
        part_v=VM((seq_len, width), BF),
        got_v=VM((seq_len, width), BF),
        opart_v=VM((2, span, width), BF),
        ogot_v=VM((2, span, width), BF),
        out_v=VM((2, span, width), BF),
        got_f32=VM((seq_len, width), F32),
        branch_v=VM((seq_len, width), BF),
        ggated_v=VM((seq_len, XW), BF),
        gattn_v=VM((seq_len, QW), BF),
        gssm_v=VM((XW, width), BF),
        gatt_v=VM((QW, width), BF),
        gffn_v=VM((8, width), F32),
        rsend=dma(2 * REDUCE_SENDS),
        rrecv=dma(2 * REDUCE_SENDS),
        psend=dma(15),
        precv=dma(15),
        local=dma(32),
    )
    kernel = with_lists(feed_forward_fused, inputs, bufs)
    return fused_call(kernel, "feed_forward", inputs, outputs, scratch, dict(red_dn=VM, red_gate=VM), 2)


def backward_fused(k):
    z, x, y, c = place()
    own = 2 * z + x
    slot = 2 * own + y
    partner = device(z, x, y, 1 - c)
    others = [(r, i, j) for r in range(4) for i in range(2) for j in range(2) if r or i or j]
    targets = [device(z ^ r, x ^ i, y ^ j, c) for r, i, j in others]
    mover = Mover(k.local)
    for src, dst in k.loads:
        mover.load(src, dst)
    greet(targets + [partner])
    pairs = (
        (k.up_v, k.red_up),
        (k.ssm_v, k.red_ssm),
        (k.att_v, k.red_att),
        (k.gz_v, k.red_gz),
        (k.xbc_v, k.red_xbc),
        (k.qkv_v, k.red_qkv),
        (k.steps_v, k.red_steps),
    )
    sums = [Reduce(part, out, *k.bufs[4 * i : 4 * i + 4], (k.rsend, k.rrecv), REDUCE_SENDS * i) for i, (part, out) in enumerate(pairs)]
    mover.need(k.up_v)
    sums[0].start()
    mover.need(k.ssm_v, k.att_v)
    for step in sums[1:3]:
        step.start()
    tick = Ticker(reduce_steps(sums, partner))
    tick.plan(0, 8)
    seq_len, width = k.normed_v.shape
    span = seq_len // 4

    def grad_of(lo, hi, out, at):
        for d in range(0, 8, 2):
            grad = dot(k.normed_v[:, 128 * d : 128 * d + 256], k.gproj_v[:, lo:hi], ((0,), (0,))).astype(BF)
            out[d : d + 2, :, at : at + hi - lo] = grad.reshape(2, 128, hi - lo)
            tick()

    mover.need(k.proj_v, k.segc_v, k.segr_v, k.par_v, k.spread_v, k.wide_v, k.ggated_v, k.y_v)
    gate_backward(k.proj_v, k.wide_v, k.y_v, k.ggated_v, k.gproj_v, k.ggated_v, tick)
    mover.need(k.normed_v)
    grad_of(Z0, Z0 + XW, k.gz_v, 0)
    sums[3].start()
    mover.need(k.states_v)
    tick.plan(10, 24)
    scan_backward(k.proj_v, k.segc_v, k.segr_v, k.par_v, k.spread_v, k.wide_v, k.y_v, k.states_v, k.ggated_v, k.gproj_v, k.gpar_v, k.gstate, tick)
    grad_of(X0, X0 + XW, k.xbc_v, 0)
    grad_of(B0, T0, k.xbc_v, XW)
    sums[4].start()
    tick.plan(9, 20)
    mover.need(k.gattn_v, k.attn_v, k.lse_v, k.cosine_v, k.sine_v)
    attention_backward(k.proj_v, k.cosine_v, k.sine_v, k.segc_v, k.segr_v, k.attn_v, k.lse_v, k.gattn_v, k.gproj_v, k.gkv, tick)
    grad_of(Q0, B0, k.qkv_v, 0)
    sums[5].start()
    tick.plan(4, 4)
    pair = (k.psend, k.precv)
    mover.need(k.w_in_v, k.rows_v, k.g_mid_v, k.gains_v, k.gffn_v)
    sent = []
    for j in range(2):
        rows = pl.ds(pl.multiple_of((2 * j + 1 - c) * span, span), span)
        k.opart_v[j] = dot(k.gproj_v[rows, :], k.w_in_v[...], ((1,), (1,))).astype(BF)
        sent.append(send(k.opart_v.at[j], k.ogot_v.at[j], pair, j, partner))
        tick()
    gain = k.gains_v[0:1, :]
    grad_gain = jnp.zeros((1, width), F32)
    columns = lambda d: pl.ds(pl.multiple_of(d * 128, 128), 128)
    sems = (k.dsend, k.drecv)
    for j in range(2):
        rows = pl.ds(pl.multiple_of((2 * j + c) * span, span), span)
        part = dot(k.gproj_v[rows, :], k.w_in_v[...], ((1,), (1,))).astype(BF).astype(F32)
        landed(k.ogot_v.at[j], pair, j, partner)
        g_h1 = (part + k.ogot_v[j].astype(F32)).astype(BF).astype(F32)
        unit, scale = rms_parts(k.rows_v[rows, :].astype(F32))
        grad_gain = grad_gain + jnp.sum(g_h1 * unit, axis=0, keepdims=True)
        k.ogot_v[j] = (k.g_mid_v[j] + rms_back(unit, scale, gain, g_h1)).astype(BF)
        tick()
    mover.store(k.ogot_v.at[y, :, columns(own)], k.returned.at[slot])
    for i, (r, a, b) in enumerate(others):
        d = 2 * (z ^ r) + (x ^ a)
        sent.append(send(k.ogot_v.at[y ^ b, :, columns(d)], k.returned.at[slot], sems, i, targets[i]))
    valid = lanes(1) < CHIP_HEADS
    heads = [jnp.where(valid, k.gpar_v[p : p + 1, :], 0.0) for p in range(3)]
    lines = [grad_gain, k.gffn_v[0:1, :]] + [jnp.concatenate([h] * (width // 128), axis=1) for h in heads]
    extra = jnp.concatenate([jnp.zeros((CHIP_HEADS, width), F32)] + lines + [jnp.zeros((STEP_ROWS - CHIP_HEADS - 5, width), F32)], axis=0)
    grad = dot(k.gproj_v[:, T0:COLS], k.normed_v[...], ((0,), (0,)))[0:STEP_ROWS, :] + extra
    for d in range(8):
        k.steps_v[d] = grad[:, 128 * d : 128 * (d + 1)].astype(BF)
    sums[6].start()
    tick.drain()
    for s in sums:
        s.finish(partner)
    for i, (r, a, b) in enumerate(others):
        landed(k.returned.at[2 * (2 * (z ^ r) + (x ^ a)) + (y ^ b)], sems, i, targets[i])
    for copy in sent:
        copy.wait_send()
    mover.flush()


STEP_ROWS = 32


def backward_stage(f, m, rows, w_in, tables):
    seq_len, width = rows.shape
    span = seq_len // 4
    cosine, sine, spread = tables
    inputs = dict(
        up=m.g_up,
        ssm=m.g_ssm,
        att=m.g_att,
        proj=f.proj,
        segc=f.segc,
        segr=f.segr,
        par=f.par,
        spread=spread,
        wide=f.wide,
        ggated=m.ggated,
        y=f.y,
        normed=f.normed,
        states=f.states,
        gattn=m.gattn,
        attn=f.attn,
        lse=f.lse,
        cosine=cosine,
        sine=sine,
        w_in=w_in,
        rows=rows,
        g_mid=m.g_mid,
        gains=f.gains,
        gffn=m.gffn,
    )
    block = width // 8
    new = dict(
        gz_v=(8, block, XW), xbc_v=(8, block, XW + 256), qkv_v=(8, block, QW + 128), steps_v=(8, STEP_ROWS, block)
    )
    parts = [m.g_up.shape, m.g_ssm.shape, m.g_att.shape] + list(new.values())
    out = [shape((2,) + d[1:]) for d in parts]
    outputs = dict(
        red_up=out[0],
        red_ssm=out[1],
        red_att=out[2],
        red_gz=out[3],
        red_xbc=out[4],
        red_qkv=out[5],
        red_steps=out[6],
    )
    spaces = {n: VM for n in outputs}
    outputs.update(returned=shape((16, span, 128)))
    bufs = reduce_scratch(parts)
    scratch = dict(
        **loaded(inputs),
        **bufs,
        **{n: VM(d, BF) for n, d in new.items()},
        gproj_v=VM((seq_len, COLS), BF),
        gpar_v=VM((8, 128), F32),
        gkv=VM((seq_len, 256), F32),
        gstate=VM((NS, XW), F32),
        opart_v=VM((2, span, width), BF),
        ogot_v=VM((2, span, width), BF),
        rsend=dma(len(parts) * REDUCE_SENDS),
        rrecv=dma(len(parts) * REDUCE_SENDS),
        psend=dma(2),
        precv=dma(2),
        dsend=dma(15),
        drecv=dma(15),
        local=dma(28),
    )
    return fused_call(with_lists(backward_fused, inputs, bufs), "mixer_backward", inputs, outputs, scratch, spaces, 3)


def finish_kernel(deal, *refs):
    sources, (tokens, g_in, g_dt, g_ssm, g_att, g_gu, g_dn, small), refs = refs[:10], refs[10:18], refs[18:]
    held, (sems, load_sems) = refs[:10], refs[10:]
    up, gate, dn, ssm, att, gz, xbc, qkv, steps, returned = held
    loads = [pltpu.make_async_copy(src, dst, load_sems.at[i]) for i, (src, dst) in enumerate(zip(sources, held))]
    for copy in reversed(loads):
        copy.start()
    for copy in reversed(loads):
        copy.wait()
    copies = [pltpu.make_async_copy(returned.at[j], tokens.at[deal[j]], sems.at[j]) for j in range(16)]
    for copy in copies:
        copy.start()
    wide = lambda v: v.astype(F32)
    inner = MH * HP
    q_start = 2 * inner + 2 * NS
    kv_start = q_start + QUERY_HEADS * HEAD_WIDTH
    half = dn.shape[1]
    for c in range(2):
        g_in[:, XW * c : XW * (c + 1)] = wide(gz[c])
        g_in[:, inner + XW * c : inner + XW * (c + 1)] = wide(xbc[c, :, 0:XW])
        g_in[:, q_start + QW * c : q_start + QW * (c + 1)] = wide(qkv[c, :, 0:QW])
        g_ssm[:, ssm.shape[2] * c : ssm.shape[2] * (c + 1)] = wide(ssm[c])
        g_att[:, att.shape[2] * c : att.shape[2] * (c + 1)] = wide(att[c])
        g_dn[half * c : half * (c + 1), :] = wide(dn[c])
        for d in range(8):
            at = (2 * d + c) * half
            g_gu[:, at : at + half] = wide(gate[c, :, half * d : half * (d + 1)])
            g_gu[:, FF + at : FF + at + half] = wide(up[c, :, half * d : half * (d + 1)])
    g_in[:, 2 * inner : q_start] = wide(xbc[0, :, XW:]) + wide(xbc[1, :, XW:])
    kv = [wide(qkv[c, :, QW : QW + 128]) for c in range(2)]
    low_lanes = lanes(kv[0].shape[0]) < 64
    g_in[:, kv_start : kv_start + 128] = jnp.where(low_lanes, kv[0], pltpu.roll(kv[1], 64, 1))
    g_in[:, kv_start + 128 : kv_start + 256] = jnp.where(low_lanes, pltpu.roll(kv[0], 64, 1), kv[1])
    first, second = wide(steps[0]), wide(steps[1])
    line = lax.broadcasted_iota(jnp.int32, first.shape, 0)
    heads = jnp.where(line < CHIP_HEADS, first, pltpu.roll(second, CHIP_HEADS, 0))
    heads = jnp.concatenate([heads, jnp.zeros((128 - STEP_ROWS, 128), F32)], axis=0).T
    g_dt[...] = heads[:, 0:MH]
    small[...] = jnp.zeros_like(small)
    for i in range(2):
        row = CHIP_HEADS + i
        small[i : i + 1, :] = first[row : row + 1, :] + second[row : row + 1, :]
    for i in range(3):
        row = CHIP_HEADS + 2 + i
        moved = pltpu.roll(second[row : row + 1, :], CHIP_HEADS, 1)
        small[2 + i : 3 + i, :] = jnp.where(lanes(1) < CHIP_HEADS, first[row : row + 1, :], moved)
    for copy in copies:
        copy.wait()


def finish_stage(deal, m, b, ssm_out, attn_out, down_proj, in_proj):
    returned = b.returned
    sources = (b.red_up, m.red_gate, m.red_dn, b.red_ssm, b.red_att, b.red_gz, b.red_xbc, b.red_qkv, b.red_steps, returned)
    wide = lambda v: shape(v.shape, F32)
    block = in_proj.shape[0]
    return pl.pallas_call(
        finish_kernel,
        name="place_gradients",
        out_shape=(
            shape(returned.shape),
            wide(in_proj),
            shape((block, MH), F32),
            wide(ssm_out),
            wide(attn_out),
            shape((block, 2 * FF), F32),
            wide(down_proj),
            shape((8, 128), F32),
        ),
        in_specs=[pl.BlockSpec(memory_space=pltpu.SMEM)] + any_specs(10),
        out_specs=tuple(any_specs(1) + whole(7)),
        scratch_shapes=[VM(v.shape, v.dtype) for v in sources] + [dma(16), dma(10)],
        compiler_params=pltpu.CompilerParams(vmem_limit_bytes=62 * MIB),
    )(deal, *sources)


def mixer_tables(seq_len):
    half = HEAD_WIDTH // 2
    frequency = np.float32(THETA) ** (-np.arange(half, dtype=np.float32) * np.float32(2.0 / HEAD_WIDTH))
    angles = np.arange(seq_len, dtype=np.float32)[:, None] * frequency[None, :].astype(np.float32)
    cosine = np.tile(np.cos(angles), (1, 4)).astype(np.float32)
    sine = np.tile(np.concatenate([-np.sin(angles), np.sin(angles)], axis=1), (1, 2)).astype(np.float32)
    head_of = np.arange(XW) // HP
    spread = np.arange(128)[:, None] % 64 == head_of[None, :]
    return jnp.asarray(cosine), jnp.asarray(sine), jnp.asarray(spread, BF)


def fused_layer(dealt, cot, seq_lengths, deal_order, gains, in_proj, dt_proj, head_values, ssm_out, attn_out, gate_up, down_proj):
    block = in_proj.shape[0]
    width = cot.shape[2]
    seq_len = 4 * cot.shape[1]
    beside = jnp.concatenate([dt_proj.T] + [g[None] for g in gains] + [jnp.zeros((128 - MH - 2, block), BF)], axis=0)
    heads = jnp.pad(jnp.stack(head_values), ((0, 5), (0, 128 - MH)))
    tables = mixer_tables(seq_len)
    rows, w_in = start_transfers(dealt, in_proj, beside)
    rows, w_in = rows.reshape(seq_len, width), w_in.reshape(width, COLS)
    first = forward_stage(rows, w_in, tables, heads, deal_order, seq_lengths.T, cot, (ssm_out, attn_out, gate_up, down_proj))
    mid = feed_forward_stage(first)
    last = backward_stage(first, mid, rows, w_in, tables)
    tokens, g_in, g_dt, g_ssm, g_att, g_gu, g_dn, small = finish_stage(deal_order, mid, last, ssm_out, attn_out, down_proj, in_proj)
    heads = [small[2 + i, :MH] for i in range(3)]
    return (mid.output, tokens, small[0], g_in, g_dt, *heads, g_ssm, g_att, small[1], g_gu, g_dn)


def rms_parts(v):
    scale = lax.rsqrt(jnp.mean(v * v, axis=-1, keepdims=True) + EPS)
    return v * scale, scale


def rms_back(normed, scale, gain, grad):
    inner = grad * gain
    return scale * (inner - normed * jnp.mean(inner * normed, axis=-1, keepdims=True))


def silu(v):
    return v / (1.0 + jnp.exp(-v))


def low(v):
    return v.astype(BF)


def plain_start(dealt, cot, w, y):
    arrived = lax.all_to_all(dealt, "dp", split_axis=0, concat_axis=2, tiled=True)
    rows = lax.all_gather(arrived, "seq", axis=1, tiled=True)
    cots = lax.all_gather(cot, "seq", axis=1, tiled=True)
    pick = lambda v: lax.dynamic_index_in_dim(v, y, 0, keepdims=False)
    return pick(rows), lax.all_gather(w, "dp", axis=0, tiled=True), pick(cots)


def plain_gather(ssm, att, gu, dn, c):
    every = [lax.all_gather(v, "dp", axis=0, tiled=True) for v in (ssm, att, gu, dn)]
    out = []
    for v in every[:2]:
        rows = v.shape[0] // 2
        mine = lax.all_gather(v, "seq", axis=1, tiled=True)[:, : 2 * v.shape[1]]
        out.append(lax.dynamic_slice_in_dim(mine, c * rows, rows))
    return out + every[2:]


def plain_pair(part):
    return lax.ppermute(part, "seq", [(0, 1), (1, 0), (2, 3), (3, 2)])


def plain_reduce(parts, out_rows, gx, y, c):
    reduced = []
    for p in parts:
        total = lax.psum_scatter(p.reshape(-1, p.shape[-1]), "dp", scatter_dimension=0, tiled=True)
        every = lax.all_gather(total, "seq", axis=0).astype(F32)
        reduced.append(jnp.stack([every[0] + every[2], every[1] + every[3]]))
    peer = lax.ppermute(out_rows, "seq", [(0, 2), (1, 3), (2, 0), (3, 1)])
    output = jnp.where(jnp.arange(2)[:, None, None] == y, out_rows, jnp.flip(peer, 0))
    whole_rows = lax.all_gather(gx, "seq", axis=0)
    slot = 2 * y + c
    by_pack = lax.dynamic_index_in_dim(whole_rows, c, 0, False), lax.dynamic_index_in_dim(whole_rows, c + 2, 0, False)
    both = jnp.stack([lax.dynamic_index_in_dim(v, y, 0, False) for v in by_pack])
    returned = lax.all_to_all(both, "dp", split_axis=2, concat_axis=0, tiled=True)
    return reduced, output, returned


def plain_layer(dealt, cot, w_in, shards, consts, y, c):
    groups = lax.axis_size("dp")
    rows, w_in, cots = plain_start(dealt, cot, w_in, y)
    w_ssm, w_att, w_gu, w_dn = plain_gather(*shards, c)
    span, width = cot.shape[1:]
    block = width // groups
    cut = lambda v, start, size: lax.dynamic_slice_in_dim(v, start, size, axis=1)

    x = rows.astype(F32)
    gain_in = w_in[:, T0 + CHIP_HEADS].astype(F32)[None, :]
    gain_ffn = w_in[:, T0 + CHIP_HEADS + 1].astype(F32)[None, :]
    unit_in, scale_in = rms_parts(x)
    normed = low(unit_in * gain_in)
    proj = low(dot(normed, w_in))
    gated, *saved = mixer_forward(proj, consts)
    attn = saved[0]
    part = low(dot(gated, w_ssm) + dot(attn, w_att))
    middle = x + (part.astype(F32) + plain_pair(part).astype(F32))
    unit_ffn, scale_ffn = rms_parts(middle)
    normed_two = low(unit_ffn * gain_ffn)
    gu = low(dot(normed_two, w_gu)).astype(F32)
    gate, up = gu[:, : FF // 2], gu[:, FF // 2 :]
    act = low(silu(gate) * up)
    out_part = low(dot(act, w_dn))
    by_core = lambda v: lax.dynamic_index_in_dim(v.reshape(2, 2, span, width), c, 1, keepdims=False)
    out_rows = low(by_core(middle) + (by_core(out_part).astype(F32) + by_core(plain_pair(out_part)).astype(F32)))

    g_act = low(dot(cots, w_dn, ((1,), (1,)))).astype(F32)
    grad_dn = low(dot(act, cots, ((0,), (0,))))
    sig = 1.0 / (1.0 + jnp.exp(-gate))
    g_gu = low(jnp.concatenate([g_act * up * (sig * (1.0 + gate * (1.0 - sig))), g_act * (gate * sig)], axis=1))
    grad_gu = low(dot(normed_two, g_gu, ((0,), (0,))))
    part = low(dot(g_gu, w_gu, ((1,), (1,))))
    g_two = low(part.astype(F32) + plain_pair(part).astype(F32)).astype(F32)
    g_mid = cots.astype(F32) + rms_back(unit_ffn, scale_ffn, gain_ffn, g_two)
    grad_gain_ffn = 0.5 * jnp.sum(g_two * unit_ffn, axis=0)
    g_branch = low(g_mid)
    g_gated = low(dot(g_branch, w_ssm, ((1,), (1,))))
    g_attn = low(dot(g_branch, w_att, ((1,), (1,))))
    grad_ssm = low(dot(gated, g_branch, ((0,), (0,))))
    grad_att = low(dot(attn, g_branch, ((0,), (0,))))
    g_proj, g_par = mixer_backward(proj, consts, saved, g_gated, g_attn)
    grad_in = dot(normed, g_proj, ((0,), (0,)))
    part = low(dot(g_proj, w_in, ((1,), (1,))))
    g_h1 = low(by_core(part).astype(F32) + by_core(plain_pair(part)).astype(F32)).astype(F32)
    scale_rows = by_core(jnp.broadcast_to(scale_in, x.shape))
    g_x = low(by_core(g_mid) + rms_back(by_core(unit_in), scale_rows, gain_in, g_h1))
    grad_gain_in = jnp.sum(g_h1 * by_core(unit_in), axis=(0, 1))
    head_grads = jnp.tile(jnp.pad(g_par[:3, :CHIP_HEADS].T, ((0, block - CHIP_HEADS), (0, 0))), (groups, 1))
    extra = jnp.concatenate([grad_gain_in[:, None], grad_gain_ffn[:, None], head_grads], axis=1)
    grad_in = low(lax.dynamic_update_slice(grad_in, extra, (0, T0 + CHIP_HEADS)))

    by_block = lambda v: v.reshape(groups, -1, v.shape[-1])
    parts = [by_block(grad_in), by_block(grad_dn), by_block(grad_gu)]
    for v in (grad_ssm, grad_att):
        both = jnp.stack([v, plain_pair(v)])
        both = jnp.where(c == 0, both, both[::-1]).reshape(-1, width)
        parts.append(by_block(cut(both, width // 2 * c, width // 2)))
    reduced, output, returned = plain_reduce(parts, out_rows, g_x, y, c)
    return output, returned, reduced


def body(tokens, cot, seq_lengths, deal_order, in_gain, in_proj, dt_proj, dt_bias, a_log, d_skip, ssm_out, attn_out, ffn_gain, gate_up, down_proj):
    groups = lax.axis_size("dp")
    dealt = tokens.at[deal_order].get(mode="promise_in_bounds")
    if groups == 8:
        return fused_layer(
            dealt, cot, seq_lengths, deal_order, (in_gain, ffn_gain), in_proj, dt_proj, (dt_bias, a_log, d_skip), ssm_out, attn_out, gate_up, down_proj
        )
    dp_index, seq_index = lax.axis_index("dp"), lax.axis_index("seq")
    y, c = seq_index // 2, seq_index % 2
    packs, span, width = cot.shape
    seq_len = span * lax.axis_size("seq")
    inner = MH * HP
    block = in_proj.shape[0]

    cut = lambda v, start, size: lax.dynamic_slice_in_dim(v, start, size, axis=1)
    q_start = 2 * inner + 2 * NS
    k_start = q_start + QUERY_HEADS * HEAD_WIDTH
    v_start = k_start + KEY_VALUE_HEADS * HEAD_WIDTH
    w_in = jnp.concatenate(
        [
            cut(in_proj, XW * c, XW),
            cut(in_proj, inner + XW * c, XW),
            cut(in_proj, q_start + QW * c, QW),
            cut(in_proj, k_start + HEAD_WIDTH * c, HEAD_WIDTH),
            cut(in_proj, v_start + HEAD_WIDTH * c, HEAD_WIDTH),
            in_proj[:, 2 * inner : q_start],
            cut(dt_proj, CHIP_HEADS * c, CHIP_HEADS),
            in_gain[:, None],
            ffn_gain[:, None],
            jnp.zeros((block, 128 - CHIP_HEADS - 2), BF),
        ],
        axis=1,
    )
    half_units = down_proj.shape[0] // 2
    w_gu = gate_up.reshape(block, 2, groups, 2, half_units)
    w_gu = lax.dynamic_index_in_dim(w_gu, c, 3, keepdims=False).reshape(block, FF)
    w_dn = lax.dynamic_slice_in_dim(down_proj, half_units * c, half_units, axis=0)
    w_ssm = cut(ssm_out, width // 2 * c, width // 2)
    w_att = cut(attn_out, width // 2 * c, width // 2)

    pack = lax.dynamic_index_in_dim(deal_order, dp_index * packs + y, 0, keepdims=False)
    ends = jnp.cumsum(lax.dynamic_index_in_dim(seq_lengths, pack, 0, keepdims=False))[:-1]
    places = jnp.arange(seq_len, dtype=jnp.int32)
    seg = jnp.sum((places[:, None] >= ends[None, :]).astype(jnp.int32), axis=1)
    segc = jnp.broadcast_to(seg[:, None], (seq_len, 128))
    segr = jnp.broadcast_to(seg[None, :], (8, seq_len))
    half = HEAD_WIDTH // 2
    frequency = THETA ** (-jnp.arange(half, dtype=F32) * 2.0 / HEAD_WIDTH)
    angles = places.astype(F32)[:, None] * frequency[None, :]
    cosine = jnp.tile(jnp.cos(angles), (1, 4))
    sine = jnp.tile(jnp.concatenate([-jnp.sin(angles), jnp.sin(angles)], axis=1), (1, 2))
    own_heads = lambda v: lax.dynamic_slice_in_dim(v, CHIP_HEADS * c, CHIP_HEADS)
    par = jnp.zeros((8, 128), F32)
    par = par.at[0, :CHIP_HEADS].set(own_heads(dt_bias)).at[1, :CHIP_HEADS].set(-jnp.exp(own_heads(a_log)))
    wide = jnp.broadcast_to(jnp.repeat(own_heads(d_skip), HP)[None, :], (8, XW))
    head_of = jnp.arange(XW) // HP
    spread = (jnp.arange(128)[:, None] % 64 == head_of[None, :]).astype(BF)
    consts = (cosine, sine, segc, segr, par, spread, wide)

    shards = (w_ssm, w_att, w_gu, w_dn)
    output, returned, (r_in, r_dn, r_gu, r_ssm, r_att) = plain_layer(dealt, cot, w_in, shards, consts, y, c)

    both = lambda start, size: [r_in[0, :, start : start + size], r_in[1, :, start : start + size]]
    grad_in_proj = jnp.concatenate(
        both(Z0, XW)
        + both(X0, XW)
        + [r_in[0, :, B0:T0] + r_in[1, :, B0:T0]]
        + both(Q0, QW)
        + both(KV0, HEAD_WIDTH)
        + both(KV0 + HEAD_WIDTH, HEAD_WIDTH),
        axis=1,
    )
    grad_dt_proj = jnp.concatenate(both(T0, CHIP_HEADS), axis=1)
    tail = r_in[:, :, T0 + CHIP_HEADS : T0 + CHIP_HEADS + 5]
    gains = tail[0, :, :2] + tail[1, :, :2]
    heads = tail[:, :CHIP_HEADS, 2:5].reshape(MH, 3)
    grad_gate_up = jnp.stack(
        [r_gu[k].reshape(block, 2, groups, half_units) for k in range(2)], axis=3
    ).reshape(block, 2 * FF)
    side = lambda v: jnp.concatenate([v[0], v[1]], axis=1)
    return (
        output,
        jnp.take(returned, jnp.argsort(deal_order), axis=0),
        gains[:, 0],
        grad_in_proj,
        grad_dt_proj,
        heads[:, 0],
        heads[:, 1],
        heads[:, 2],
        side(r_ssm),
        side(r_att),
        gains[:, 1],
        grad_gate_up,
        r_dn.reshape(-1, width),
    )


def solution(mesh):
    return jax.shard_map(
        body,
        mesh=mesh,
        in_specs=(
            P(None, "seq", "dp"),
            P("dp", "seq", None),
            P(),
            P(),
            P("dp"),
            P("dp", None),
            P("dp", None),
            P(),
            P(),
            P(),
            P("dp", None),
            P("dp", None),
            P("dp"),
            P("dp", None),
            P("dp", None),
        ),
        out_specs=(
            P("dp", "seq", None),
            P(None, "seq", "dp"),
            P("dp"),
            P("dp", None),
            P("dp", None),
            P(),
            P(),
            P(),
            P("dp", None),
            P("dp", None),
            P("dp"),
            P("dp", None),
            P("dp", None),
        ),
        check_vma=False,
    )
```
